32 devices in a mesh: groups: 2 (over x), aux: 16 (over z, y, core).
Axes of the slice: x: 2, y: 2, z: 4, core: 2. Of those that a mesh axis runs over, the one named last changes fastest.
Arguments:
- integrals: bfloat16 [10240, 128, 128], P(('groups', 'aux')), parts along dimension 0, may hold values from -6 to 6
- block_index: int32 [10240, 3], P(('groups', 'aux')), parts along dimension 0, may hold values from 0 to 23, as said below
- live_count: int32 [32], P(('groups', 'aux')), parts along dimension 0, may hold values from 1 to 320, as said below
- orbitals: bfloat16 [6144, 128], P('groups'), parts along dimension 0, may hold values from -0.109375 to 0.109375
- metric: float32 [512, 256], P('groups'), parts along dimension 0, may hold values from -0.0234375 to 0.0234375
Outputs:
- exchange_applied: float32 [6144, 128], P(('groups', 'aux')), parts along dimension 0
The draws below stay inside these ranges and needn't reach their ends.
There are 2 independent parts, one for each index of `groups`. The reference program is written for one: setup_inputs(seed, part) draws one part's arguments, and reference() takes and returns one part's arrays. A program takes and returns all parts, laid end to end along the dimension named above; each array names one. Nothing has to cross between parts.
Inputs may be any that keep to these rules, and one draw needn't show every extreme that they name: `block_index`: columns 1 and 2 lie in 0 to 23, column 0 in 0 to 15. `live_count`: slots from this number on hold no data.
All inputs are finite; a program needn't handle non-finite values.
Results may differ from the reference program's by a relative error of at most 0.0049.
Values may be sent and summed in bfloat16 or wider, within the bound.
No kernel may reach another device: no remote copies, remote signals or barrier semaphores. Data moves between devices by JAX's collectives and lax.ppermute only.
A program may use at most 128 MiB of HBM per device.

```python
import jax
import jax.numpy as jnp
from jax import lax

BLOCK = 128
NBF = 3072
OCC = 128
Q_DEV = 16
BLK_DEV = 320
NAUX = 256
N_AUX = 16


def draw_block_index(key, part):
    key = jax.random.fold_in(key, 11)
    key_q, key_m, key_n = jax.random.split(key, 3)
    total = N_AUX * BLK_DEV
    nblk = NBF // BLOCK
    q_local = jax.random.randint(key_q, (total,), 0, Q_DEV, dtype=jnp.int32)
    m_block = jax.random.randint(key_m, (total,), 0, nblk, dtype=jnp.int32)
    offset = jax.random.randint(key_n, (total,), -3, 4, dtype=jnp.int32)
    n_block = (m_block + offset + 3 * nblk) % nblk
    q_local = q_local.at[1].set(0)
    m_block = m_block.at[0].set(nblk - 1)
    return jnp.stack([q_local, m_block, n_block], axis=1)


def draw_live_count(key, part):
    key = jax.random.fold_in(key, 23)
    key_r, key_f = jax.random.split(key)
    ratio = jax.random.randint(key_r, (N_AUX,), 1, 9, dtype=jnp.int32)
    counts = jnp.maximum(BLK_DEV * ratio * ratio // 64, 1)
    full_device = jax.random.randint(key_f, (), 0, N_AUX, dtype=jnp.int32)
    return counts.at[full_device].set(BLK_DEV)


def shard_levels(rng, dims, cuts, least, largest):
    loudness, own = 1.0, jax.random.fold_in(rng, 6)
    for dim, parts in cuts:
        heights = jnp.exp(jax.random.uniform(jax.random.fold_in(own, dim), (parts,), jnp.float32, least / len(cuts), largest / len(cuts)))
        loudness = loudness * jnp.repeat(heights, dims[dim] // parts).reshape([-1 if axis == dim else 1 for axis in range(len(dims))])
    return loudness


def normal_values(stream_key, shape, scale, reach, cuts=(), held_as=jnp.bfloat16):
    array = jax.random.normal(stream_key, shape, jnp.float32) * scale
    if len(cuts) > 0:
        array = shard_levels(stream_key, shape, cuts, -0.22, 0.18) * array
    return jnp.clip(array, min=-reach, max=reach).astype(held_as)


def setup_inputs(seed: int = 0, part: int = 0) -> dict:
    splits = jax.random.split(jax.random.key(seed), 6)
    part_keys = jax.random.split(jax.random.fold_in(splits[5], part), 6)
    integrals = normal_values(part_keys[0], (N_AUX * BLK_DEV, BLOCK, BLOCK), 1.0, 6.0, ((0, 16),))
    block_index = draw_block_index(jax.random.fold_in(jax.random.fold_in(splits[5], part), 71), part)
    live_count = draw_live_count(jax.random.fold_in(jax.random.fold_in(splits[5], part), 71), part)
    orbitals = normal_values(part_keys[3], (NBF, OCC), NBF ** -0.5, 0.109375)
    metric = normal_values(part_keys[4], (NAUX, NAUX), (1.0 / NAUX), 0.0234375, (), jnp.float32)
    return dict(integrals=integrals, block_index=block_index, live_count=live_count, orbitals=orbitals, metric=metric)


def half_transform(blocks, index, live, orbitals):
    nblk = NBF // BLOCK
    q_local = index[:, 0]
    m_block = index[:, 1]
    n_block = index[:, 2]
    orb_blocks = orbitals.reshape(nblk, BLOCK, OCC)
    orb_rows = orb_blocks[n_block]
    products = jnp.einsum('bmn,bni->bmi', blocks.astype(jnp.float32), orb_rows.astype(jnp.float32), precision=lax.Precision.HIGHEST)
    live_mask = (jnp.arange(BLK_DEV, dtype=jnp.int32) < live).astype(jnp.float32)
    products = products * live_mask[:, None, None]
    slot_ids = q_local * nblk + m_block
    slab = jnp.zeros((Q_DEV * nblk, BLOCK, OCC), jnp.float32).at[slot_ids].add(products)
    return slab.reshape(Q_DEV, NBF, OCC).astype(jnp.bfloat16)


def reference(integrals, block_index, live_count, orbitals, metric):
    blocks = integrals.reshape(N_AUX, BLK_DEV, BLOCK, BLOCK)
    indices = block_index.reshape(N_AUX, BLK_DEV, 3)

    def per_device(packed):
        dev_blocks, dev_index, dev_live = packed
        slab = half_transform(dev_blocks, dev_index, dev_live, orbitals)
        pairs = jnp.einsum('qni,nj->qij', slab.astype(jnp.float32), orbitals.astype(jnp.float32), precision=lax.Precision.HIGHEST)
        return slab, pairs

    slabs, pairs = lax.map(per_device, (blocks, indices, live_count))
    pairs = pairs.reshape(NAUX, OCC, OCC)
    fitted = jnp.einsum('qp,pij->qij', metric, pairs, precision=lax.Precision.HIGHEST).astype(jnp.bfloat16)
    fitted = fitted.reshape(N_AUX, Q_DEV, OCC, OCC)

    def accumulate(total, packed):
        dev_slab, dev_fitted = packed
        term = jnp.einsum('qmi,qij->mj', dev_slab.astype(jnp.float32), dev_fitted.astype(jnp.float32), precision=lax.Precision.HIGHEST)
        return total + term, None

    total, unused = lax.scan(accumulate, jnp.zeros((NBF, OCC), jnp.float32), (slabs, fitted))
    return total
```

```python
import functools

import jax
import jax.numpy as jnp
from jax import lax
from jax.experimental import pallas as pl
from jax.experimental.pallas import tpu as pltpu
from jax.sharding import PartitionSpec as P

UNROLL = 8
CHUNK = 32
F32 = jnp.float32
BF16 = jnp.bfloat16


def half_kernel(
    owners, q_dev, live_ref, code_ref, blocks_hbm, orb_ref, slab_hbm, pairs_ref,
    held, acc, slab, orb_t, in_sem, out_sem,
):
    slots, size, occupied = held.shape
    nblk = orb_ref.shape[0] // size
    chunks = slots // CHUNK
    live = live_ref[0]

    def fetch(c):
        part = pl.ds(c * CHUNK, CHUNK)
        return pltpu.make_async_copy(blocks_hbm.at[part], held.at[part], in_sem.at[c])

    for c in range(chunks):
        @pl.when(c * CHUNK < live)
        def _():
            fetch(c).start()

    @pl.loop(0, q_dev * nblk, step=2)
    def _(k):
        for u in range(2):
            acc[k + u] = jnp.zeros((size, occupied), F32)

    for b in range(nblk):
        rows = slice(b * size, (b + 1) * size)
        orb_t[:, rows] = orb_ref[rows, :].T

    @pl.loop(0, (live + CHUNK - 1) // CHUNK)
    def _(c):
        fetch(c).wait()

        @pl.loop(0, CHUNK // UNROLL)
        def _(g):
            for u in range(UNROLL):
                s = c * CHUNK + g * UNROLL + u
                code = code_ref[s]
                key = code // 256
                nb = pl.multiple_of((code % 256) * size, size)
                acc[key] += jnp.dot(held[s], orb_ref[pl.ds(nb, size), :], preferred_element_type=F32)

    def flush(t):
        return pltpu.make_async_copy(slab.at[t], slab_hbm.at[t], out_sem.at[t])

    @pl.loop(0, q_dev // 2)
    def _(t):
        total = jnp.zeros((occupied, 2 * occupied), F32)
        for b in range(0, nblk, 2):
            left = jnp.concatenate([acc[2 * t * nblk + b], acc[2 * t * nblk + b + 1]], axis=0)
            right = jnp.concatenate([acc[(2 * t + 1) * nblk + b], acc[(2 * t + 1) * nblk + b + 1]], axis=0)
            block = jnp.concatenate([left.astype(BF16), right.astype(BF16)], axis=1)
            rows = slice(b * size, (b + 2) * size)
            slab[t, rows, :] = block
            total += jnp.dot(orb_t[:, rows], block, preferred_element_type=F32)
        flush(t).start()
        for u in range(2):
            pair = total[:, u * occupied : (u + 1) * occupied]
            if owners:
                pairs_ref[:, 2 * t + u] = pair.reshape(owners, occupied // owners, occupied).astype(BF16)
            else:
                pairs_ref[2 * t + u] = pair.astype(BF16)

    @pl.loop(0, q_dev // 2)
    def _(t):
        flush(t).wait()


def half_transform(blocks, code, live, orbitals, q_dev, owners):
    slots, size, _ = blocks.shape
    basis, occupied = orbitals.shape
    nblk = basis // size
    split = (occupied // owners) % 8 == 0
    pairs_shape = (owners, q_dev, occupied // owners, occupied) if split else (q_dev, occupied, occupied)
    half = q_dev // 2
    slab, pairs = pl.pallas_call(
        functools.partial(half_kernel, owners if split else 0, q_dev),
        out_shape=(
            jax.ShapeDtypeStruct((half, basis, 2 * occupied), BF16),
            jax.ShapeDtypeStruct(pairs_shape, BF16),
        ),
        in_specs=[
            pl.BlockSpec(memory_space=pltpu.SMEM),
            pl.BlockSpec(memory_space=pltpu.SMEM),
            pl.BlockSpec(memory_space=pl.ANY),
            pl.BlockSpec(memory_space=pltpu.VMEM),
        ],
        out_specs=(pl.BlockSpec(memory_space=pl.ANY), pl.BlockSpec(memory_space=pltpu.VMEM)),
        scratch_shapes=[
            pltpu.VMEM((slots, size, size), BF16),
            pltpu.VMEM((q_dev * nblk + 1, size, occupied), F32),
            pltpu.VMEM((half, basis, 2 * occupied), BF16),
            pltpu.VMEM((occupied, basis), BF16),
            pltpu.SemaphoreType.DMA((slots // CHUNK,)),
            pltpu.SemaphoreType.DMA((half,)),
        ],
        compiler_params=pltpu.CompilerParams(vmem_limit_bytes=60 * 2**20),
        cost_estimate=pl.CostEstimate(
            flops=2 * slots * size * size * occupied + 2 * q_dev * basis * occupied * occupied,
            bytes_accessed=2 * slots * size * size + 2 * q_dev * basis * occupied,
            transcendentals=0,
        ),
        name="half_transform_pairs",
    )(live, code, blocks, orbitals)
    if not split:
        pairs = pairs.reshape(q_dev, owners, occupied // owners, occupied).transpose(1, 0, 2, 3)
    return slab, pairs


def exchange_kernel(mine, me_ref, slab_hbm, fitted_ref, out_ref, slab, fitted, sem):
    half, rows, _ = slab.shape
    parts, each, occupied = out_ref.shape
    me = me_ref[0]

    def fetch(h):
        owner = (2 * h + mine) ^ me
        there = pl.ds(pl.multiple_of(owner * each, each), each)
        here = pl.ds(h * each, each)
        return pltpu.make_async_copy(slab_hbm.at[:, there, :], slab.at[:, here, :], sem.at[h])

    for h in range(parts):
        fetch(h).start()

    for q in range(2 * half):
        if len(fitted_ref.shape) == 4:
            block = fitted_ref[:, q].astype(F32).reshape(occupied, occupied)
        else:
            block = fitted_ref[q].astype(F32)
        fitted[q * occupied : (q + 1) * occupied, :] = block.T.astype(BF16)

    for h in range(parts):
        fetch(h).wait()
        here = slice(h * each, (h + 1) * each)
        rows_all = jnp.concatenate([slab[t, here, :] for t in range(half)], axis=1)
        out_ref[h] = jnp.dot(rows_all, fitted[...], preferred_element_type=F32).astype(out_ref.dtype)


def exchange_rows(slab, fitted, me, owners, mine, dtype):
    half, basis, width = slab.shape
    occupied = width // 2
    each = basis // owners
    return pl.pallas_call(
        functools.partial(exchange_kernel, mine),
        out_shape=jax.ShapeDtypeStruct((owners // 2, each, occupied), dtype),
        in_specs=[
            pl.BlockSpec(memory_space=pltpu.SMEM),
            pl.BlockSpec(memory_space=pl.ANY),
            pl.BlockSpec(memory_space=pltpu.VMEM),
        ],
        out_specs=pl.BlockSpec(memory_space=pltpu.VMEM),
        scratch_shapes=[
            pltpu.VMEM((half, basis // 2, width), BF16),
            pltpu.VMEM((half * width, occupied), BF16),
            pltpu.SemaphoreType.DMA((owners // 2,)),
        ],
        compiler_params=pltpu.CompilerParams(vmem_limit_bytes=32 * 2**20),
        cost_estimate=pl.CostEstimate(
            flops=half * width * basis * occupied, bytes_accessed=half * width * basis, transcendentals=0
        ),
        name="exchange_rows",
    )(me, slab, fitted)


def body(owners, integrals, block_index, live_count, orbitals, metric):
    slots, size, _ = integrals.shape
    basis, occupied = orbitals.shape
    nblk = basis // size
    naux = metric.shape[1]
    q_dev = naux // owners
    each = basis // owners
    me = lax.axis_index("aux").astype(jnp.int32)

    key = block_index[:, 0] * nblk + block_index[:, 1]
    alive = jnp.arange(slots, dtype=jnp.int32) < live_count[0]
    code = jnp.where(alive, key, q_dev * nblk) * 256 + block_index[:, 2]

    slab, pairs = half_transform(integrals, code, live_count, orbitals, q_dev, owners)

    held = lax.all_to_all(pairs, "aux", split_axis=0, concat_axis=0, tiled=True)
    held = held.reshape(naux, occupied // owners, occupied).astype(F32)
    fitted = jnp.einsum("qp,pji->qji", metric, held, precision=lax.Precision.HIGHEST).astype(BF16)
    fitted = fitted.reshape(owners, q_dev, occupied // owners, occupied)
    fitted = lax.all_to_all(fitted, "aux", split_axis=0, concat_axis=0, tiled=True)
    if (occupied // owners) % 8:
        fitted = fitted.transpose(1, 0, 2, 3).reshape(q_dev, occupied, occupied)

    def swap(x, bit):
        return lax.ppermute(x, "aux", [(d, d ^ bit) for d in range(owners)])

    mine = me.reshape(1)
    away = exchange_rows(slab, fitted, mine, owners, 1, BF16)
    arrived = swap(away, 1)
    near = exchange_rows(slab, fitted, mine, owners, 0, F32)
    arrived = arrived.reshape(owners // 4, 2, each, occupied)
    near = near.reshape(owners // 4, 2, each, occupied)
    away = (near[:, 1] + arrived[:, 1].astype(F32)).astype(BF16)
    arrived_y = swap(away, 2)
    near = near[:, 0] + arrived[:, 0].astype(F32) + arrived_y.astype(F32)
    total = near[0]
    for k in range(1, owners // 4):
        total = total + swap(near[k].astype(BF16), 4 * k).astype(F32)
    return total


def solution(mesh):
    placed = (
        P(("groups", "aux"), None, None),
        P(("groups", "aux"), None),
        P(("groups", "aux")),
        P("groups", None),
        P("groups", None),
    )
    return jax.shard_map(
        functools.partial(body, mesh.shape["aux"]),
        mesh=mesh, in_specs=placed, out_specs=P(("groups", "aux"), None), check_vma=False,
    )
```

```python
import functools

import jax
import jax.numpy as jnp
from jax import lax
from jax.experimental import pallas as pl
from jax.experimental.pallas import tpu as pltpu
from jax.sharding import PartitionSpec as P

UNROLL = 8
CHUNK = 32
F32 = jnp.float32
BF16 = jnp.bfloat16


def rank_slots(live, index_ref, keys, meta, nblk, nkeys):
    slots = index_ref.shape[1]
    wide = keys.shape[1]
    keys[...] = jnp.full(keys.shape, nkeys, F32)
    key = index_ref[0:1, :] * nblk + index_ref[1:2, :]
    alive = lax.broadcasted_iota(jnp.int32, (1, slots), 1) < live
    keys[0:1, 0:slots] = jnp.where(alive, key, nkeys).astype(F32)
    row = jnp.broadcast_to(keys[0:1, :], (wide, wide))
    column = row.T
    before = lax.broadcasted_iota(jnp.int32, (wide, wide), 0) < lax.broadcasted_iota(jnp.int32, (wide, wide), 1)
    rank = jnp.sum(jnp.where((column == row) & before, 1.0, 0.0), axis=0, keepdims=True)
    pair = jnp.floor(rank * 0.5)
    odd = rank - 2.0 * pair
    opens = jnp.broadcast_to(1.0 - odd, (wide, wide)).T
    group = jnp.sum(jnp.where(column < row, opens, 0.0), axis=0, keepdims=True) + pair
    lives = keys[0:1, :] < nkeys
    place = jnp.where(lives, 2.0 * group + odd, 2.0 * slots + 2 * UNROLL)
    count = jnp.sum(jnp.where(lives, 1.0 - odd, 0.0), axis=1, keepdims=True)
    last = jnp.max(jnp.where(lives, keys[0:1, :], 0.0), axis=1, keepdims=True)
    meta[0:1, :] = place.astype(jnp.int32)
    meta[1:2, 0:slots] = lax.broadcasted_iota(jnp.int32, (1, slots), 1) * 256 + index_ref[2:3, :]
    meta[2:3, :] = (2.0 * keys[0:1, :] + jnp.where(rank < 2.0, 1.0, 0.0)).astype(jnp.int32)
    meta[3:4, :] = jnp.broadcast_to(count, (1, wide)).astype(jnp.int32)
    meta[4:5, :] = jnp.broadcast_to(last, (1, wide)).astype(jnp.int32)


def half_kernel(
    owners, q_dev, live_ref, index_hbm, blocks_hbm, orb_hbm, slab, pairs_ref,
    index_ref, held, orb_ref, orb_t, keys, meta, facts, group_slot, group_key, in_sem, meta_sem,
):
    slots, size, _ = blocks_hbm.shape
    occupied = orb_ref.shape[1]
    nblk = orb_ref.shape[0] // size
    nkeys = q_dev * nblk
    chunks = slots // CHUNK

    def fetch(c):
        part = pl.ds(c * CHUNK, CHUNK)
        return pltpu.make_async_copy(blocks_hbm.at[part], held.at[part], in_sem.at[c])

    small = [
        pltpu.make_async_copy(source, target, meta_sem.at[1 + k])
        for k, (source, target) in enumerate([(index_hbm, index_ref), (orb_hbm, orb_ref)])
    ]
    for copy in small:
        copy.start()
    for c in range(chunks):
        fetch(c).start()

    small[0].wait()
    rank_slots(live_ref[0], index_ref, keys, meta, nblk, nkeys)
    copy = pltpu.make_async_copy(meta, facts, meta_sem.at[0])
    copy.start()

    nothing = slots * 256
    held[slots] = jnp.zeros((size, size), BF16)

    @pl.loop(0, nkeys, step=4)
    def _(k):
        for u in range(4):
            slab[k + u] = jnp.zeros((size, occupied), BF16)

    @pl.loop(0, 2 * slots, step=16)
    def _(k):
        for u in range(16):
            group_slot[k + u] = nothing

    for u in range(2 * UNROLL):
        group_slot[2 * slots + u] = nothing

    small[1].wait()
    for b in range(nblk):
        rows = slice(b * size, (b + 1) * size)
        orb_t[:, rows] = orb_ref[rows, :].T

    copy.wait()
    groups = facts[3, 0]

    @pl.loop(0, slots, step=8)
    def _(k):
        for u in range(8):
            place = facts[0, k + u]
            group_slot[place] = facts[1, k + u]
            group_key[place // 2] = facts[2, k + u]

    for u in range(UNROLL):
        group_key[groups + u] = 2 * facts[4, 0]

    for c in range(chunks):
        fetch(c).wait()

    def step(g, total):
        for u in range(UNROLL):
            first, second = group_slot[2 * (g * UNROLL + u)], group_slot[2 * (g * UNROLL + u) + 1]
            code = group_key[g * UNROLL + u]
            blocks = jnp.concatenate([held[first // 256], held[second // 256]], axis=1)
            orbs = jnp.concatenate(
                [orb_ref[pl.ds(pl.multiple_of((s % 256) * size, size), size), :] for s in (first, second)], axis=0
            )
            product = jnp.dot(blocks, orbs, preferred_element_type=F32)
            total = jnp.where(code % 2 == 1, product, total + product)
            slab[code // 2] = total.astype(BF16)
        return total

    lax.fori_loop(0, (groups + UNROLL - 1) // UNROLL, step, jnp.zeros((size, occupied), F32))

    @pl.loop(0, q_dev // 2)
    def _(t):
        total = jnp.zeros((occupied, 2 * occupied), F32)
        for b in range(0, nblk, 2):
            block = jnp.concatenate(
                [
                    jnp.concatenate([slab[(2 * t + u) * nblk + b], slab[(2 * t + u) * nblk + b + 1]], axis=0)
                    for u in range(2)
                ],
                axis=1,
            )
            total += jnp.dot(orb_t[:, b * size : (b + 2) * size], block, preferred_element_type=F32)
        for u in range(2):
            pair = total[:, u * occupied : (u + 1) * occupied].T
            if owners:
                pairs_ref[:, 2 * t + u] = pair.reshape(owners, occupied // owners, occupied).astype(BF16)
            else:
                pairs_ref[2 * t + u] = pair.astype(BF16)


def half_transform(blocks, index, live, orbitals, q_dev, owners):
    slots, size, _ = blocks.shape
    basis, occupied = orbitals.shape
    nblk = basis // size
    split = (occupied // owners) % 8 == 0
    pairs_shape = (owners, q_dev, occupied // owners, occupied) if split else (q_dev, occupied, occupied)
    wide = -(-slots // 128) * 128
    slab, pairs = pl.pallas_call(
        functools.partial(half_kernel, owners if split else 0, q_dev),
        out_shape=(
            pltpu.VMEM((q_dev * nblk, size, occupied), BF16),
            jax.ShapeDtypeStruct(pairs_shape, BF16),
        ),
        in_specs=[pl.BlockSpec(memory_space=pltpu.SMEM)] + [pl.BlockSpec(memory_space=pl.ANY)] * 3,
        out_specs=(pl.BlockSpec(memory_space=pltpu.VMEM), pl.BlockSpec(memory_space=pltpu.VMEM)),
        scratch_shapes=[
            pltpu.VMEM(index.shape, jnp.int32),
            pltpu.VMEM((slots + 1, size, size), BF16),
            pltpu.VMEM((basis, occupied), BF16),
            pltpu.VMEM((occupied, basis), BF16),
            pltpu.VMEM((8, wide), F32),
            pltpu.VMEM((8, wide), jnp.int32),
            pltpu.SMEM((8, wide), jnp.int32),
            pltpu.SMEM((2 * slots + 2 * UNROLL + 2,), jnp.int32),
            pltpu.SMEM((slots + UNROLL + 1,), jnp.int32),
            pltpu.SemaphoreType.DMA((slots // CHUNK,)),
            pltpu.SemaphoreType.DMA((3,)),
        ],
        compiler_params=pltpu.CompilerParams(vmem_limit_bytes=36 * 2**20),
        cost_estimate=pl.CostEstimate(
            flops=2 * slots * size * size * occupied + 2 * q_dev * basis * occupied * occupied,
            bytes_accessed=2 * slots * size * size + 2 * q_dev * basis * occupied,
            transcendentals=0,
        ),
        name="half_transform_pairs",
    )(live, *(pltpu.with_memory_space_constraint(x, pltpu.HBM) for x in (index, blocks, orbitals)))
    if not split:
        pairs = pairs.reshape(q_dev, owners, occupied // owners, occupied).transpose(1, 0, 2, 3)
    return slab.reshape(q_dev, basis, occupied), pairs


def exchange_kernel(mine, me_ref, slab, fitted_ref, out_ref, fitted):
    q_dev = slab.shape[0]
    parts, each, occupied = out_ref.shape
    me = me_ref[0]

    for q in range(q_dev):
        if len(fitted_ref.shape) == 4:
            block = fitted_ref[:, q].astype(F32).reshape(occupied, occupied).astype(BF16)
        else:
            block = fitted_ref[q]
        fitted[q * occupied : (q + 1) * occupied, :] = block

    @pl.loop(0, parts)
    def _(h):
        owner = (2 * h + mine) ^ me
        rows = pl.ds(pl.multiple_of(owner * each, each), each)
        every = jnp.concatenate([slab[q, rows, :] for q in range(q_dev)], axis=1)
        out_ref[h] = jnp.dot(every, fitted[...], preferred_element_type=F32).astype(out_ref.dtype)


def exchange_rows(slab, fitted, me, owners, mine, dtype):
    q_dev, basis, occupied = slab.shape
    each = basis // owners
    return pl.pallas_call(
        functools.partial(exchange_kernel, mine),
        out_shape=jax.ShapeDtypeStruct((owners // 2, each, occupied), dtype),
        in_specs=[
            pl.BlockSpec(memory_space=pltpu.SMEM),
            pl.BlockSpec(memory_space=pltpu.VMEM),
            pl.BlockSpec(memory_space=pltpu.VMEM),
        ],
        out_specs=pl.BlockSpec(memory_space=pltpu.VMEM),
        scratch_shapes=[pltpu.VMEM((q_dev * occupied, occupied), BF16)],
        compiler_params=pltpu.CompilerParams(vmem_limit_bytes=24 * 2**20),
        cost_estimate=pl.CostEstimate(
            flops=q_dev * occupied * basis * occupied, bytes_accessed=q_dev * occupied * basis, transcendentals=0
        ),
        name="exchange_rows",
    )(me, pltpu.with_memory_space_constraint(slab, pltpu.VMEM), fitted)


def body(owners, integrals, block_index, live_count, orbitals, metric):
    basis, occupied = orbitals.shape
    naux = metric.shape[1]
    q_dev = naux // owners
    me = lax.axis_index("aux").astype(jnp.int32)

    slab, pairs = half_transform(integrals, block_index.T, live_count, orbitals, q_dev, owners)

    held = lax.all_to_all(pairs, "aux", split_axis=0, concat_axis=0, tiled=True)
    held = held.reshape(naux, occupied // owners, occupied).astype(F32)
    fitted = jnp.einsum("qp,pij->qij", metric, held, precision=lax.Precision.HIGHEST).astype(BF16)
    fitted = fitted.reshape(owners, q_dev, occupied // owners, occupied)
    fitted = lax.all_to_all(fitted, "aux", split_axis=0, concat_axis=0, tiled=True)
    if (occupied // owners) % 8:
        fitted = fitted.transpose(1, 0, 2, 3).reshape(q_dev, occupied, occupied)

    def swap(x, bit):
        return lax.ppermute(x, "aux", [(d, d ^ bit) for d in range(owners)])

    mine = me.reshape(1)
    away = exchange_rows(slab, fitted, mine, owners, 1, BF16)
    arrived = swap(away, 1)
    near = exchange_rows(slab, fitted, mine, owners, 0, F32) + arrived.astype(F32)
    total = near[0]
    for k in range(1, owners // 2):
        total = total + swap(near[k].astype(BF16), 2 * k).astype(F32)
    return total


def solution(mesh):
    placed = (
        P(("groups", "aux"), None, None),
        P(("groups", "aux"), None),
        P(("groups", "aux")),
        P("groups", None),
        P("groups", None),
    )
    return jax.shard_map(
        functools.partial(body, mesh.shape["aux"]),
        mesh=mesh, in_specs=placed, out_specs=P(("groups", "aux"), None), check_vma=False,
    )
```

```python
import functools

import jax
import jax.numpy as jnp
from jax import lax
from jax.experimental import pallas as pl
from jax.experimental.pallas import tpu as pltpu
from jax.sharding import PartitionSpec as P

UNROLL = 8
CHUNK = 32
F32 = jnp.float32
BF16 = jnp.bfloat16


def rank_slots(live, index_ref, keys, meta, nblk, nkeys):
    slots = index_ref.shape[1]
    wide = keys.shape[1]
    keys[...] = jnp.full(keys.shape, nkeys, F32)
    key = index_ref[0:1, :] * nblk + index_ref[1:2, :]
    alive = lax.broadcasted_iota(jnp.int32, (1, slots), 1) < live
    keys[0:1, 0:slots] = jnp.where(alive, key, nkeys).astype(F32)
    row = keys[0:1, :]
    column = keys[...].T[:, 0:1]
    before = lax.broadcasted_iota(jnp.int32, (wide, wide), 0) < lax.broadcasted_iota(jnp.int32, (wide, wide), 1)
    rank = jnp.sum(jnp.where((column == row) & before, 1.0, 0.0), axis=0, keepdims=True)
    pair = jnp.floor(rank * 0.5)
    odd = rank - 2.0 * pair
    opens = jnp.broadcast_to(1.0 - odd, (8, wide)).T[:, 0:1]
    group = jnp.sum(jnp.where(column < row, opens, 0.0), axis=0, keepdims=True) + pair
    lives = keys[0:1, :] < nkeys
    place = jnp.where(lives, 2.0 * group + odd, 2.0 * slots + 2 * UNROLL)
    count = jnp.sum(jnp.where(lives, 1.0 - odd, 0.0), axis=1, keepdims=True)
    last = jnp.max(jnp.where(lives, keys[0:1, :], 0.0), axis=1, keepdims=True)
    meta[0:1, :] = place.astype(jnp.int32)
    meta[1:2, 0:slots] = lax.broadcasted_iota(jnp.int32, (1, slots), 1) * 256 + index_ref[2:3, :]
    meta[2:3, :] = (2.0 * keys[0:1, :] + jnp.where(rank < 2.0, 1.0, 0.0)).astype(jnp.int32)
    meta[3:4, :] = jnp.broadcast_to(count, (1, wide)).astype(jnp.int32)
    meta[4:5, :] = jnp.broadcast_to(last, (1, wide)).astype(jnp.int32)


def half_kernel(
    owners, q_dev, live_ref, index_hbm, blocks_hbm, orb_hbm, slab, pairs_ref,
    index_ref, held, orb_ref, orb_t, keys, meta, facts, group_slot, group_key, in_sem, meta_sem,
):
    slots, size, _ = blocks_hbm.shape
    occupied = orb_ref.shape[1]
    nblk = orb_ref.shape[0] // size
    nkeys = q_dev * nblk
    chunks = slots // CHUNK

    def fetch(c):
        part = pl.ds(c * CHUNK, CHUNK)
        return pltpu.make_async_copy(blocks_hbm.at[part], held.at[part], in_sem.at[c])

    small = [
        pltpu.make_async_copy(source, target, meta_sem.at[1 + k])
        for k, (source, target) in enumerate([(index_hbm, index_ref), (orb_hbm, orb_ref)])
    ]
    for copy in small:
        copy.start()
    for c in range(chunks):
        fetch(c).start()

    nothing = slots * 256
    held[slots] = jnp.zeros((size, size), BF16)

    @pl.loop(0, nkeys, step=8)
    def _(k):
        for u in range(8):
            slab[k + u] = jnp.zeros((size, occupied), BF16)

    @pl.loop(0, 2 * slots, step=16)
    def _(k):
        for u in range(16):
            group_slot[k + u] = nothing

    for u in range(2 * UNROLL):
        group_slot[2 * slots + u] = nothing

    small[0].wait()
    rank_slots(live_ref[0], index_ref, keys, meta, nblk, nkeys)
    copy = pltpu.make_async_copy(meta, facts, meta_sem.at[0])
    copy.start()

    small[1].wait()
    for b in range(nblk):
        rows = slice(b * size, (b + 1) * size)
        orb_t[:, rows] = orb_ref[rows, :].T

    copy.wait()
    groups = facts[3, 0]

    @pl.loop(0, slots, step=8)
    def _(k):
        for u in range(8):
            place = facts[0, k + u]
            group_slot[place] = facts[1, k + u]
            group_key[place >> 1] = facts[2, k + u]

    for u in range(UNROLL):
        group_key[groups + u] = 2 * facts[4, 0]

    for c in range(chunks):
        fetch(c).wait()

    def step(g, total):
        for u in range(UNROLL):
            first, second = group_slot[2 * (g * UNROLL + u)], group_slot[2 * (g * UNROLL + u) + 1]
            code = group_key[g * UNROLL + u]
            blocks = jnp.concatenate([held[first >> 8], held[second >> 8]], axis=1)
            orbs = jnp.concatenate(
                [orb_ref[pl.ds(pl.multiple_of((s & 255) * size, size), size), :] for s in (first, second)], axis=0
            )
            product = jnp.dot(blocks, orbs, preferred_element_type=F32)
            total = jnp.where((code & 1) == 1, product, total + product)
            slab[code >> 1] = total.astype(BF16)
        return total

    lax.fori_loop(0, (groups + UNROLL - 1) // UNROLL, step, jnp.zeros((size, occupied), F32))

    @pl.loop(0, q_dev // 2)
    def _(t):
        block = jnp.concatenate(
            [slab[pl.ds((2 * t + u) * nblk, nblk)].reshape(nblk * size, occupied) for u in range(2)], axis=1
        )
        total = jnp.dot(orb_t[...], block, preferred_element_type=F32)
        for u in range(2):
            pair = total[:, u * occupied : (u + 1) * occupied].T
            if owners:
                pairs_ref[:, 2 * t + u] = pair.reshape(owners, occupied // owners, occupied).astype(BF16)
            else:
                pairs_ref[2 * t + u] = pair.astype(BF16)


def half_transform(blocks, index, live, orbitals, q_dev, owners):
    slots, size, _ = blocks.shape
    basis, occupied = orbitals.shape
    nblk = basis // size
    split = (occupied // owners) % 8 == 0
    pairs_shape = (owners, q_dev, occupied // owners, occupied) if split else (q_dev, occupied, occupied)
    wide = -(-slots // 128) * 128
    slab, pairs = pl.pallas_call(
        functools.partial(half_kernel, owners if split else 0, q_dev),
        out_shape=(
            pltpu.VMEM((q_dev * nblk, size, occupied), BF16),
            jax.ShapeDtypeStruct(pairs_shape, BF16),
        ),
        in_specs=[pl.BlockSpec(memory_space=pltpu.SMEM)] + [pl.BlockSpec(memory_space=pl.ANY)] * 3,
        out_specs=(pl.BlockSpec(memory_space=pltpu.VMEM), pl.BlockSpec(memory_space=pltpu.VMEM)),
        scratch_shapes=[
            pltpu.VMEM(index.shape, jnp.int32),
            pltpu.VMEM((slots + 1, size, size), BF16),
            pltpu.VMEM((basis, occupied), BF16),
            pltpu.VMEM((occupied, basis), BF16),
            pltpu.VMEM((8, wide), F32),
            pltpu.VMEM((8, wide), jnp.int32),
            pltpu.SMEM((8, wide), jnp.int32),
            pltpu.SMEM((2 * slots + 2 * UNROLL + 2,), jnp.int32),
            pltpu.SMEM((slots + UNROLL + 1,), jnp.int32),
            pltpu.SemaphoreType.DMA((slots // CHUNK,)),
            pltpu.SemaphoreType.DMA((3,)),
        ],
        compiler_params=pltpu.CompilerParams(vmem_limit_bytes=36 * 2**20),
        cost_estimate=pl.CostEstimate(
            flops=2 * slots * size * size * occupied + 2 * q_dev * basis * occupied * occupied,
            bytes_accessed=2 * slots * size * size + 2 * q_dev * basis * occupied,
            transcendentals=0,
        ),
        name="half_transform_pairs",
    )(live, *(pltpu.with_memory_space_constraint(x, pltpu.HBM) for x in (index, blocks, orbitals)))
    if not split:
        pairs = pairs.reshape(q_dev, owners, occupied // owners, occupied).transpose(1, 0, 2, 3)
    return slab.reshape(q_dev, basis, occupied), pairs


def metric_kernel(metric_ref, held_ref, out_ref, spread, mixed):
    naux, each, occupied = held_ref.shape
    metric = metric_ref[...]
    high = metric.astype(BF16)
    low = (metric - high.astype(F32)).astype(BF16)
    spread[...] = held_ref[...].astype(F32).reshape(naux * each, occupied)
    for r in range(each):
        pairs = spread[pl.ds(r, naux, stride=each), :].astype(BF16)
        fitted = jnp.dot(high, pairs, preferred_element_type=F32) + jnp.dot(low, pairs, preferred_element_type=F32)
        mixed[pl.ds(r, naux, stride=each), :] = fitted
    out_ref[...] = mixed[...].reshape(naux, each, occupied).astype(BF16)


def apply_metric(metric, held):
    naux, each, occupied = held.shape
    if each % 8:
        fitted = jnp.einsum("qp,pij->qij", metric, held.astype(F32), precision=lax.Precision.HIGHEST)
        return fitted.astype(BF16)
    return pl.pallas_call(
        metric_kernel,
        out_shape=jax.ShapeDtypeStruct(held.shape, BF16),
        in_specs=[pl.BlockSpec(memory_space=pltpu.VMEM)] * 2,
        out_specs=pl.BlockSpec(memory_space=pltpu.VMEM),
        scratch_shapes=[pltpu.VMEM((naux * each, occupied), F32)] * 2,
        compiler_params=pltpu.CompilerParams(vmem_limit_bytes=12 * 2**20),
        cost_estimate=pl.CostEstimate(
            flops=4 * naux * naux * each * occupied, bytes_accessed=4 * naux * each * occupied, transcendentals=0
        ),
        name="apply_metric",
    )(metric, held)


def gather_fitted(fitted_ref, fitted):
    q_dev = fitted.shape[0] // fitted.shape[1]
    occupied = fitted.shape[1]
    for q in range(q_dev):
        if len(fitted_ref.shape) == 4:
            block = fitted_ref[:, q].astype(F32).reshape(occupied, occupied).astype(BF16)
        else:
            block = fitted_ref[q]
        fitted[q * occupied : (q + 1) * occupied, :] = block


def exchange_kernel(start, together, more, slab, fitted_ref, *refs):
    refs = list(refs)
    more_ref = refs.pop(0) if more else None
    out_ref = refs.pop(0)
    if start == 3:
        fitted = refs.pop(0)
        gather_fitted(fitted_ref, fitted)
    else:
        fitted = fitted_ref
    q_dev = slab.shape[0]
    parts, each, occupied = out_ref.shape
    me = lax.axis_index("aux").astype(jnp.int32)

    @pl.loop(0, parts // together)
    def _(g):
        rows = []
        for u in range(together):
            owner = (4 * (g * together + u) + start) ^ me
            rows.append(pl.ds(pl.multiple_of(owner * each, each), each))
        every = jnp.concatenate(
            [jnp.concatenate([slab[q, r, :] for r in rows], axis=0) for q in range(q_dev)], axis=1
        )
        sums = jnp.dot(every, fitted[...], preferred_element_type=F32)
        for u in range(together):
            part = sums[u * each : (u + 1) * each]
            if more:
                part = part + more_ref[g * together + u].astype(F32)
            out_ref[g * together + u] = part.astype(out_ref.dtype)


def exchange_rows(slab, fitted, owners, start, dtype, more=None):
    q_dev, basis, occupied = slab.shape
    each = basis // owners
    parts = owners // 4
    out = [jax.ShapeDtypeStruct((parts, each, occupied), dtype)]
    if start == 3:
        out.append(jax.ShapeDtypeStruct((q_dev * occupied, occupied), BF16))
    operands = [pltpu.with_memory_space_constraint(slab, pltpu.VMEM), fitted] + ([] if more is None else [more])
    return pl.pallas_call(
        functools.partial(exchange_kernel, start, 2 if parts % 2 == 0 else 1, more is not None),
        out_shape=out,
        in_specs=[pl.BlockSpec(memory_space=pltpu.VMEM)] * len(operands),
        out_specs=[pl.BlockSpec(memory_space=pltpu.VMEM)] * len(out),
        compiler_params=pltpu.CompilerParams(vmem_limit_bytes=24 * 2**20),
        cost_estimate=pl.CostEstimate(
            flops=2 * q_dev * occupied * basis * occupied // 4,
            bytes_accessed=q_dev * occupied * basis // 2,
            transcendentals=0,
        ),
        name="exchange_rows",
    )(*operands)


def body(owners, integrals, block_index, live_count, orbitals, metric):
    basis, occupied = orbitals.shape
    naux = metric.shape[1]
    q_dev = naux // owners

    slab, pairs = half_transform(integrals, block_index.T, live_count, orbitals, q_dev, owners)

    held = lax.all_to_all(pairs, "aux", split_axis=0, concat_axis=0, tiled=True)
    fitted = apply_metric(metric, held.reshape(naux, occupied // owners, occupied))
    fitted = fitted.reshape(owners, q_dev, occupied // owners, occupied)
    fitted = lax.all_to_all(fitted, "aux", split_axis=0, concat_axis=0, tiled=True)
    if (occupied // owners) % 8:
        fitted = fitted.transpose(1, 0, 2, 3).reshape(q_dev, occupied, occupied)

    def swap(x, bit):
        return lax.ppermute(x, "aux", [(d, d ^ bit) for d in range(owners)])

    away, fitted = exchange_rows(slab, fitted, owners, 3, BF16)
    far = swap(away, 1)
    (away,) = exchange_rows(slab, fitted, owners, 1, BF16)
    near = swap(away, 1)
    (away,) = exchange_rows(slab, fitted, owners, 2, BF16, far)
    far = swap(away, 2)
    (near,) = exchange_rows(slab, fitted, owners, 0, F32, near)
    near = near + far.astype(F32)
    total = near[0]
    for k in range(1, owners // 4):
        total = total + swap(near[k].astype(BF16), 4 * k).astype(F32)
    return total


def solution(mesh):
    placed = (
        P(("groups", "aux"), None, None),
        P(("groups", "aux"), None),
        P(("groups", "aux")),
        P("groups", None),
        P("groups", None),
    )
    return jax.shard_map(
        functools.partial(body, mesh.shape["aux"]),
        mesh=mesh, in_specs=placed, out_specs=P(("groups", "aux"), None), check_vma=False,
    )
```

```python
import functools

import jax
import jax.numpy as jnp
from jax import lax
from jax.experimental import pallas as pl
from jax.experimental.pallas import tpu as pltpu
from jax.sharding import PartitionSpec as P

UNROLL = 8
CHUNK = 32
F32 = jnp.float32
BF16 = jnp.bfloat16


def rank_slots(live, index_ref, rows, meta, nblk, nkeys):
    slots = index_ref.shape[1]
    wide = rows.shape[1]
    many = meta.shape[1]
    nothing = float(slots * 256)
    rows[...] = jnp.full(rows.shape, nkeys, F32)
    key = index_ref[0:1, :] * nblk + index_ref[1:2, :]
    slot = lax.broadcasted_iota(jnp.int32, (1, slots), 1)
    rows[0:1, 0:slots] = jnp.where(slot < live, key, nkeys).astype(F32)
    rows[1:2, 0:slots] = (slot * 256 + index_ref[2:3, :]).astype(F32)
    row = rows[0:1, :]
    column = rows[...].T[:, 0:1]
    before = lax.broadcasted_iota(jnp.int32, (wide, wide), 0) < lax.broadcasted_iota(jnp.int32, (wide, wide), 1)
    rank = jnp.sum(jnp.where((column == row) & before, 1.0, 0.0), axis=0, keepdims=True)
    pair = jnp.floor(rank * 0.5)
    odd = rank - 2.0 * pair
    opens = jnp.broadcast_to(1.0 - odd, (8, wide)).T[:, 0:1]
    group = jnp.sum(jnp.where(column < row, opens, 0.0), axis=0, keepdims=True) + pair
    lives = row < nkeys
    count = jnp.sum(jnp.where(lives, 1.0 - odd, 0.0), axis=1, keepdims=True)
    last = 2.0 * jnp.max(jnp.where(lives, row, 0.0), axis=1, keepdims=True)
    rows[1:2, :] = rows[1:2, :] - nothing
    rows[2:3, :] = jnp.where(lives, 2.0 * group + odd, -1.0)
    rows[3:4, :] = jnp.where(lives & (odd == 0.0), group, -1.0)
    rows[4:5, :] = 2.0 * row + jnp.where(rank < 2.0, 1.0, 0.0) - last
    columns = rows[...].T
    place = lax.broadcasted_iota(jnp.int32, (1, many), 1).astype(F32)
    members = jnp.sum(jnp.where(columns[:, 2:3] == place, columns[:, 1:2], 0.0), axis=0, keepdims=True)
    keys = jnp.sum(jnp.where(columns[:, 3:4] == place[:, :wide], columns[:, 4:5], 0.0), axis=0, keepdims=True)
    meta[0:1, :] = (members + nothing).astype(jnp.int32)
    meta[1:2, 0:wide] = (keys + last).astype(jnp.int32)
    meta[2:3, :] = jnp.broadcast_to(count, (1, many)).astype(jnp.int32)


def half_kernel(
    owners, q_dev, live_ref, index_hbm, blocks_hbm, orb_hbm, metric_hbm, slab, pairs_ref, split_ref,
    index_ref, held, orb_ref, metric_ref, orb_t, rows, meta, facts, in_sem, small_sem,
):
    slots, size, _ = blocks_hbm.shape
    occupied = orb_ref.shape[1]
    nblk = orb_ref.shape[0] // size
    nkeys = q_dev * nblk
    chunks = slots // CHUNK

    def fetch(c):
        part = pl.ds(c * CHUNK, CHUNK)
        return pltpu.make_async_copy(blocks_hbm.at[part], held.at[part], in_sem.at[c])

    def clear(first, last):
        @pl.loop(first, last, step=8)
        def _(k):
            for u in range(8):
                slab[k + u] = jnp.zeros((size, occupied), BF16)

    small = [
        pltpu.make_async_copy(source, target, small_sem.at[1 + k])
        for k, (source, target) in enumerate(
            [(index_hbm, index_ref), (orb_hbm, orb_ref), (metric_hbm, metric_ref)]
        )
    ]
    for copy in small:
        copy.start()
    for c in range(chunks):
        fetch(c).start()

    held[slots] = jnp.zeros((size, size), BF16)
    clear(0, nkeys // 2)

    small[0].wait()
    rank_slots(live_ref[0], index_ref, rows, meta, nblk, nkeys)
    copy = pltpu.make_async_copy(meta, facts, small_sem.at[0])
    copy.start()

    clear(nkeys // 2, nkeys)
    small[1].wait()
    for b in range(nblk):
        part = slice(b * size, (b + 1) * size)
        orb_t[:, part] = orb_ref[part, :].T
    small[2].wait()
    metric = metric_ref[...]
    high = metric.astype(BF16)
    split_ref[0] = high
    split_ref[1] = (metric - high.astype(F32)).astype(BF16)

    copy.wait()
    groups = facts[2, 0]
    for c in range(chunks):
        fetch(c).wait()

    def step(g, total):
        for u in range(UNROLL):
            first, second = facts[0, 2 * (g * UNROLL + u)], facts[0, 2 * (g * UNROLL + u) + 1]
            code = facts[1, g * UNROLL + u]
            blocks = jnp.concatenate([held[first >> 8], held[second >> 8]], axis=1)
            orbs = jnp.concatenate(
                [orb_ref[pl.ds(pl.multiple_of((s & 255) * size, size), size), :] for s in (first, second)], axis=0
            )
            product = jnp.dot(blocks, orbs, preferred_element_type=F32)
            total = jnp.where((code & 1) == 1, product, total + product)
            slab[code >> 1] = total.astype(BF16)
        return total

    lax.fori_loop(0, (groups + UNROLL - 1) // UNROLL, step, jnp.zeros((size, occupied), F32))

    @pl.loop(0, q_dev // 2)
    def _(t):
        block = jnp.concatenate(
            [slab[pl.ds((2 * t + u) * nblk, nblk)].reshape(nblk * size, occupied) for u in range(2)], axis=1
        )
        total = jnp.dot(orb_t[...], block, preferred_element_type=F32)
        for u in range(2):
            pair = total[:, u * occupied : (u + 1) * occupied].T
            if owners:
                pairs_ref[:, 2 * t + u] = pair.reshape(owners, occupied // owners, occupied).astype(BF16)
            else:
                pairs_ref[2 * t + u] = pair.astype(BF16)


def half_transform(blocks, index, live, orbitals, metric, q_dev, owners):
    slots, size, _ = blocks.shape
    basis, occupied = orbitals.shape
    nblk = basis // size
    split = (occupied // owners) % 8 == 0
    pairs_shape = (owners, q_dev, occupied // owners, occupied) if split else (q_dev, occupied, occupied)
    wide = -(-(slots + UNROLL) // 128) * 128
    many = -(-2 * (slots + UNROLL) // 128) * 128
    slab, pairs, metric_split = pl.pallas_call(
        functools.partial(half_kernel, owners if split else 0, q_dev),
        out_shape=(
            pltpu.VMEM((q_dev * nblk, size, occupied), BF16),
            jax.ShapeDtypeStruct(pairs_shape, BF16),
            pltpu.VMEM((2,) + metric.shape, BF16),
        ),
        in_specs=[pl.BlockSpec(memory_space=pltpu.SMEM)] + [pl.BlockSpec(memory_space=pl.ANY)] * 4,
        out_specs=(pl.BlockSpec(memory_space=pltpu.VMEM),) * 3,
        scratch_shapes=[
            pltpu.VMEM(index.shape, jnp.int32),
            pltpu.VMEM((slots + 1, size, size), BF16),
            pltpu.VMEM((basis, occupied), BF16),
            pltpu.VMEM(metric.shape, F32),
            pltpu.VMEM((occupied, basis), BF16),
            pltpu.VMEM((8, wide), F32),
            pltpu.VMEM((8, many), jnp.int32),
            pltpu.SMEM((8, many), jnp.int32),
            pltpu.SemaphoreType.DMA((slots // CHUNK,)),
            pltpu.SemaphoreType.DMA((4,)),
        ],
        compiler_params=pltpu.CompilerParams(vmem_limit_bytes=36 * 2**20),
        cost_estimate=pl.CostEstimate(
            flops=2 * slots * size * size * occupied + 2 * q_dev * basis * occupied * occupied,
            bytes_accessed=2 * slots * size * size + 2 * q_dev * basis * occupied,
            transcendentals=0,
        ),
        name="half_transform_pairs",
    )(live, *(pltpu.with_memory_space_constraint(x, pltpu.HBM) for x in (index, blocks, orbitals, metric)))
    if not split:
        pairs = pairs.reshape(q_dev, owners, occupied // owners, occupied).transpose(1, 0, 2, 3)
    return slab.reshape(q_dev, basis, occupied), pairs, metric_split


def metric_kernel(order, split_ref, held_ref, out_ref, spread, mixed):
    naux, each, occupied = held_ref.shape
    q_dev = naux // len(order)
    for k, d in enumerate(order):
        block = held_ref[k * q_dev : (k + 1) * q_dev].astype(F32)
        spread[d * q_dev * each : (d + 1) * q_dev * each, :] = block.reshape(q_dev * each, occupied)
    for r in range(each):
        pairs = spread[pl.ds(r, naux, stride=each), :].astype(BF16)
        fitted = jnp.dot(split_ref[0], pairs, preferred_element_type=F32)
        fitted = fitted + jnp.dot(split_ref[1], pairs, preferred_element_type=F32)
        mixed[pl.ds(r, naux, stride=each), :] = fitted
    for k, d in enumerate(order):
        block = mixed[d * q_dev * each : (d + 1) * q_dev * each, :]
        out_ref[k * q_dev : (k + 1) * q_dev] = block.reshape(q_dev, each, occupied).astype(BF16)


def apply_metric(metric, metric_split, held, order):
    naux, each, occupied = held.shape
    if each % 8:
        q_dev = naux // len(order)
        back = [order.index(d) for d in range(len(order))]
        held = held.reshape(len(order), q_dev, each, occupied)[jnp.array(back)].reshape(held.shape)
        fitted = jnp.einsum("qp,pij->qij", metric, held.astype(F32), precision=lax.Precision.HIGHEST).astype(BF16)
        return fitted.reshape(len(order), q_dev, each, occupied)[jnp.array(order)].reshape(held.shape)
    return pl.pallas_call(
        functools.partial(metric_kernel, order),
        out_shape=jax.ShapeDtypeStruct(held.shape, BF16),
        in_specs=[pl.BlockSpec(memory_space=pltpu.VMEM)] * 2,
        out_specs=pl.BlockSpec(memory_space=pltpu.VMEM),
        scratch_shapes=[pltpu.VMEM((naux * each, occupied), F32)] * 2,
        compiler_params=pltpu.CompilerParams(vmem_limit_bytes=12 * 2**20),
        cost_estimate=pl.CostEstimate(
            flops=4 * naux * naux * each * occupied, bytes_accessed=4 * naux * each * occupied, transcendentals=0
        ),
        name="apply_metric",
    )(pltpu.with_memory_space_constraint(metric_split, pltpu.VMEM), held)


def gather_fitted(fitted_ref, fitted):
    q_dev = fitted.shape[0] // fitted.shape[1]
    occupied = fitted.shape[1]
    for q in range(q_dev):
        if len(fitted_ref.shape) == 4:
            block = fitted_ref[:, q].astype(F32).reshape(occupied, occupied).astype(BF16)
        else:
            block = fitted_ref[q]
        fitted[q * occupied : (q + 1) * occupied, :] = block


def exchange_kernel(start, together, more, slab, fitted_ref, *refs):
    refs = list(refs)
    more_ref = refs.pop(0) if more else None
    out_ref = refs.pop(0)
    if start == 3:
        fitted = refs.pop(0)
        gather_fitted(fitted_ref, fitted)
    else:
        fitted = fitted_ref
    q_dev = slab.shape[0]
    parts, each, occupied = out_ref.shape
    me = lax.axis_index("aux").astype(jnp.int32)

    @pl.loop(0, parts // together)
    def _(g):
        rows = []
        for u in range(together):
            owner = (4 * (g * together + u) + start) ^ me
            rows.append(pl.ds(pl.multiple_of(owner * each, each), each))
        every = jnp.concatenate(
            [jnp.concatenate([slab[q, r, :] for r in rows], axis=0) for q in range(q_dev)], axis=1
        )
        sums = jnp.dot(every, fitted[...], preferred_element_type=F32)
        for u in range(together):
            part = sums[u * each : (u + 1) * each]
            if more:
                part = part + more_ref[g * together + u].astype(F32)
            out_ref[g * together + u] = part.astype(out_ref.dtype)


def exchange_rows(slab, fitted, owners, start, dtype, more=None):
    q_dev, basis, occupied = slab.shape
    each = basis // owners
    parts = owners // 4
    out = [jax.ShapeDtypeStruct((parts, each, occupied), dtype)]
    if start == 3:
        out.append(jax.ShapeDtypeStruct((q_dev * occupied, occupied), BF16))
    operands = [pltpu.with_memory_space_constraint(slab, pltpu.VMEM), fitted] + ([] if more is None else [more])
    return pl.pallas_call(
        functools.partial(exchange_kernel, start, 4 if parts % 4 == 0 else 1, more is not None),
        out_shape=out,
        in_specs=[pl.BlockSpec(memory_space=pltpu.VMEM)] * len(operands),
        out_specs=[pl.BlockSpec(memory_space=pltpu.VMEM)] * len(out),
        compiler_params=pltpu.CompilerParams(vmem_limit_bytes=24 * 2**20),
        cost_estimate=pl.CostEstimate(
            flops=2 * q_dev * occupied * basis * occupied // 4,
            bytes_accessed=q_dev * occupied * basis // 2,
            transcendentals=0,
        ),
        name="exchange_rows",
    )(*operands)


def body(owners, integrals, block_index, live_count, orbitals, metric):
    basis, occupied = orbitals.shape
    naux = metric.shape[1]
    q_dev = naux // owners

    slab, pairs, metric_split = half_transform(integrals, block_index.T, live_count, orbitals, metric, q_dev, owners)

    order = [4 * a + b for b in range(4) for a in range(owners // 4)]
    trade = functools.partial(
        lax.all_to_all, axis_name="aux", split_axis=0, concat_axis=0, tiled=True, axis_index_groups=[order]
    )
    held = trade(pairs).reshape(naux, occupied // owners, occupied)
    fitted = apply_metric(metric, metric_split, held, order)
    fitted = trade(fitted.reshape(owners, q_dev, occupied // owners, occupied))
    if (occupied // owners) % 8:
        fitted = fitted.transpose(1, 0, 2, 3).reshape(q_dev, occupied, occupied)

    def swap(x, bit):
        return lax.ppermute(x, "aux", [(d, d ^ bit) for d in range(owners)])

    away, fitted = exchange_rows(slab, fitted, owners, 3, BF16)
    far = swap(away, 1)
    (away,) = exchange_rows(slab, fitted, owners, 1, BF16)
    near = swap(away, 1)
    (away,) = exchange_rows(slab, fitted, owners, 2, BF16, far)
    far = swap(away, 2)
    (near,) = exchange_rows(slab, fitted, owners, 0, F32, near)
    near = near + far.astype(F32)
    total = near[0]
    for k in range(1, owners // 4):
        total = total + swap(near[k].astype(BF16), 4 * k).astype(F32)
    return total


def solution(mesh):
    placed = (
        P(("groups", "aux"), None, None),
        P(("groups", "aux"), None),
        P(("groups", "aux")),
        P("groups", None),
        P("groups", None),
    )
    return jax.shard_map(
        functools.partial(body, mesh.shape["aux"]),
        mesh=mesh, in_specs=placed, out_specs=P(("groups", "aux"), None), check_vma=False,
    )
```

```python
import functools

import jax
import jax.numpy as jnp
from jax import lax
from jax.experimental import pallas as pl
from jax.experimental.pallas import tpu as pltpu
from jax.sharding import PartitionSpec as P

UNROLL = 8
CHUNK = 32
F32 = jnp.float32
BF16 = jnp.bfloat16


def rank_slots(live, index_ref, rows, meta, nblk, nkeys):
    slots = index_ref.shape[1]
    wide = rows.shape[1]
    nothing = float(slots * 256)
    rows[...] = jnp.full(rows.shape, nkeys, F32)
    key = index_ref[0:1, :] * nblk + index_ref[1:2, :]
    slot = lax.broadcasted_iota(jnp.int32, (1, slots), 1)
    rows[0:1, 0:slots] = jnp.where(slot < live, key, nkeys).astype(F32)
    rows[1:2, 0:slots] = (slot * 256 + index_ref[2:3, :]).astype(F32)
    row = rows[0:1, :]
    column = rows[...].T[:, 0:1]
    before = lax.broadcasted_iota(jnp.int32, (wide, wide), 0) < lax.broadcasted_iota(jnp.int32, (wide, wide), 1)
    same = (column == row) & before
    rank = jnp.sum(jnp.where(same, 1.0, 0.0), axis=0, keepdims=True)
    place = jnp.sum(jnp.where(same | (column < row), 1.0, 0.0), axis=0, keepdims=True)
    lives = row < nkeys
    last = 2.0 * jnp.max(jnp.where(lives, row, 0.0), axis=1, keepdims=True)
    rows[1:2, :] = rows[1:2, :] - nothing
    rows[2:3, :] = jnp.where(lives, place, -1.0)
    rows[3:4, :] = 2.0 * row + jnp.where(rank == 0.0, 1.0, 0.0) - last
    columns = rows[...].T
    found = columns[:, 2:3] == lax.broadcasted_iota(jnp.int32, (1, wide), 1).astype(F32)
    members = jnp.sum(jnp.where(found, columns[:, 1:2], 0.0), axis=0, keepdims=True)
    keys = jnp.sum(jnp.where(found, columns[:, 3:4], 0.0), axis=0, keepdims=True)
    meta[0:1, :] = (members + nothing).astype(jnp.int32)
    meta[1:2, :] = (keys + last).astype(jnp.int32)


def half_kernel(
    owners, q_dev, live_ref, index_hbm, blocks_hbm, orb_hbm, metric_hbm, slab, pairs_ref, split_ref,
    index_ref, held, orb_ref, metric_ref, orb_t, rows, meta, facts, in_sem, small_sem,
):
    slots, size, _ = blocks_hbm.shape
    occupied = orb_ref.shape[1]
    nblk = orb_ref.shape[0] // size
    nkeys = q_dev * nblk
    chunks = slots // CHUNK

    def fetch(c):
        part = pl.ds(c * CHUNK, CHUNK)
        return pltpu.make_async_copy(blocks_hbm.at[part], held.at[part], in_sem.at[c])

    def clear(first, last):
        @pl.loop(first, last, step=8)
        def _(k):
            for u in range(8):
                slab[k + u] = jnp.zeros((size, occupied), BF16)

    small = [
        pltpu.make_async_copy(source, target, small_sem.at[1 + k])
        for k, (source, target) in enumerate(
            [(index_hbm, index_ref), (orb_hbm, orb_ref), (metric_hbm, metric_ref)]
        )
    ]
    for copy in small:
        copy.start()
    for c in range(chunks):
        fetch(c).start()

    held[slots] = jnp.zeros((size, size), BF16)
    clear(0, nkeys // 2)

    small[0].wait()
    rank_slots(live_ref[0], index_ref, rows, meta, nblk, nkeys)
    copy = pltpu.make_async_copy(meta, facts, small_sem.at[0])
    copy.start()

    clear(nkeys // 2, nkeys)
    small[1].wait()
    for b in range(nblk):
        part = slice(b * size, (b + 1) * size)
        orb_t[:, part] = orb_ref[part, :].T
    small[2].wait()
    metric = metric_ref[...]
    high = metric.astype(BF16)
    naux = metric.shape[0]
    split_ref[0:naux, :] = high
    split_ref[naux : 2 * naux, :] = (metric - high.astype(F32)).astype(BF16)

    copy.wait()
    for c in range(chunks):
        fetch(c).wait()

    def step(g, total):
        for u in range(UNROLL):
            slot, code = facts[0, g * UNROLL + u], facts[1, g * UNROLL + u]
            orbs = orb_ref[pl.ds(pl.multiple_of((slot & 255) * size, size), size), :]
            product = jnp.dot(held[slot >> 8], orbs, preferred_element_type=F32)
            total = jnp.where((code & 1) == 1, product, total + product)
            slab[code >> 1] = total.astype(BF16)
        return total

    lax.fori_loop(0, (live_ref[0] + UNROLL - 1) // UNROLL, step, jnp.zeros((size, occupied), F32))

    @pl.loop(0, q_dev // 2, unroll=2)
    def _(t):
        block = jnp.concatenate(
            [slab[pl.ds((2 * t + u) * nblk, nblk)].reshape(nblk * size, occupied) for u in range(2)], axis=1
        )
        total = jnp.dot(orb_t[...], block, preferred_element_type=F32)
        for u in range(2):
            pair = total[:, u * occupied : (u + 1) * occupied].T
            if owners:
                pairs_ref[:, 2 * t + u] = pair.reshape(owners, occupied // owners, occupied).astype(BF16)
            else:
                pairs_ref[2 * t + u] = pair.astype(BF16)


def half_transform(blocks, index, live, orbitals, metric, q_dev, owners):
    slots, size, _ = blocks.shape
    basis, occupied = orbitals.shape
    nblk = basis // size
    split = (occupied // owners) % 8 == 0
    pairs_shape = (owners, q_dev, occupied // owners, occupied) if split else (q_dev, occupied, occupied)
    wide = -(-(slots + UNROLL) // 128) * 128
    slab, pairs, metric_split = pl.pallas_call(
        functools.partial(half_kernel, owners if split else 0, q_dev),
        out_shape=(
            pltpu.VMEM((q_dev * nblk, size, occupied), BF16),
            jax.ShapeDtypeStruct(pairs_shape, BF16),
            pltpu.VMEM((2 * metric.shape[0], metric.shape[1]), BF16),
        ),
        in_specs=[pl.BlockSpec(memory_space=pltpu.SMEM)] + [pl.BlockSpec(memory_space=pl.ANY)] * 4,
        out_specs=(pl.BlockSpec(memory_space=pltpu.VMEM),) * 3,
        scratch_shapes=[
            pltpu.VMEM(index.shape, jnp.int32),
            pltpu.VMEM((slots + 1, size, size), BF16),
            pltpu.VMEM((basis, occupied), BF16),
            pltpu.VMEM(metric.shape, F32),
            pltpu.VMEM((occupied, basis), BF16),
            pltpu.VMEM((8, wide), F32),
            pltpu.VMEM((8, wide), jnp.int32),
            pltpu.SMEM((8, wide), jnp.int32),
            pltpu.SemaphoreType.DMA((slots // CHUNK,)),
            pltpu.SemaphoreType.DMA((4,)),
        ],
        compiler_params=pltpu.CompilerParams(vmem_limit_bytes=36 * 2**20),
        cost_estimate=pl.CostEstimate(
            flops=2 * slots * size * size * occupied + 2 * q_dev * basis * occupied * occupied,
            bytes_accessed=2 * slots * size * size + 2 * q_dev * basis * occupied,
            transcendentals=0,
        ),
        name="half_transform_pairs",
    )(live, *(pltpu.with_memory_space_constraint(x, pltpu.HBM) for x in (index, blocks, orbitals, metric)))
    if not split:
        pairs = pairs.reshape(q_dev, owners, occupied // owners, occupied).transpose(1, 0, 2, 3)
    return slab.reshape(q_dev, basis, occupied), pairs, metric_split


def metric_kernel(split_ref, held_ref, out_ref, spread, mixed):
    naux, each, occupied = held_ref.shape
    spread[...] = held_ref[...].astype(F32).reshape(naux * each, occupied)
    for r in range(0, each, 2):
        both = [spread[pl.ds(r + u, naux, stride=each), :].astype(BF16) for u in range(2)]
        parts = jnp.dot(split_ref[...], jnp.concatenate(both, axis=1), preferred_element_type=F32)
        fitted = parts[:naux] + parts[naux:]
        for u in range(2):
            mixed[pl.ds(r + u, naux, stride=each), :] = fitted[:, u * occupied : (u + 1) * occupied]
    out_ref[...] = mixed[...].reshape(naux, each, occupied).astype(BF16)


def apply_metric(metric, metric_split, held):
    naux, each, occupied = held.shape
    if each % 8:
        fitted = jnp.einsum("qp,pij->qij", metric, held.astype(F32), precision=lax.Precision.HIGHEST)
        return fitted.astype(BF16)
    return pl.pallas_call(
        metric_kernel,
        out_shape=jax.ShapeDtypeStruct(held.shape, BF16),
        in_specs=[pl.BlockSpec(memory_space=pltpu.VMEM)] * 2,
        out_specs=pl.BlockSpec(memory_space=pltpu.VMEM),
        scratch_shapes=[pltpu.VMEM((naux * each, occupied), F32)] * 2,
        compiler_params=pltpu.CompilerParams(vmem_limit_bytes=12 * 2**20),
        cost_estimate=pl.CostEstimate(
            flops=4 * naux * naux * each * occupied, bytes_accessed=4 * naux * each * occupied, transcendentals=0
        ),
        name="apply_metric",
    )(pltpu.with_memory_space_constraint(metric_split, pltpu.VMEM), held)


def gather_fitted(fitted_ref, fitted):
    q_dev = fitted.shape[0] // fitted.shape[1]
    occupied = fitted.shape[1]
    for q in range(q_dev):
        if len(fitted_ref.shape) == 4:
            block = fitted_ref[:, q].astype(F32).reshape(occupied, occupied).astype(BF16)
        else:
            block = fitted_ref[q]
        fitted[q * occupied : (q + 1) * occupied, :] = block


def exchange_kernel(start, together, more, slab, fitted_ref, *refs):
    refs = list(refs)
    more_ref = refs.pop(0) if more else None
    out_ref = refs.pop(0)
    if start == 3:
        fitted = refs.pop(0)
        gather_fitted(fitted_ref, fitted)
    else:
        fitted = fitted_ref
    q_dev = slab.shape[0]
    parts, each, occupied = out_ref.shape
    me = lax.axis_index("aux").astype(jnp.int32)

    @pl.loop(0, parts // together)
    def _(g):
        rows = []
        for u in range(together):
            owner = (4 * (g * together + u) + start) ^ me
            rows.append(pl.ds(pl.multiple_of(owner * each, each), each))
        every = jnp.concatenate(
            [jnp.concatenate([slab[q, r, :] for r in rows], axis=0) for q in range(q_dev)], axis=1
        )
        sums = jnp.dot(every, fitted[...], preferred_element_type=F32)
        for u in range(together):
            part = sums[u * each : (u + 1) * each]
            if more:
                part = part + more_ref[g * together + u].astype(F32)
            out_ref[g * together + u] = part.astype(out_ref.dtype)


def exchange_rows(slab, fitted, owners, start, dtype, more=None):
    q_dev, basis, occupied = slab.shape
    each = basis // owners
    parts = owners // 4
    out = [jax.ShapeDtypeStruct((parts, each, occupied), dtype)]
    if start == 3:
        out.append(jax.ShapeDtypeStruct((q_dev * occupied, occupied), BF16))
    operands = [pltpu.with_memory_space_constraint(slab, pltpu.VMEM), fitted] + ([] if more is None else [more])
    return pl.pallas_call(
        functools.partial(exchange_kernel, start, 4 if parts % 4 == 0 else 1, more is not None),
        out_shape=out,
        in_specs=[pl.BlockSpec(memory_space=pltpu.VMEM)] * len(operands),
        out_specs=[pl.BlockSpec(memory_space=pltpu.VMEM)] * len(out),
        compiler_params=pltpu.CompilerParams(vmem_limit_bytes=24 * 2**20),
        cost_estimate=pl.CostEstimate(
            flops=2 * q_dev * occupied * basis * occupied // 4,
            bytes_accessed=q_dev * occupied * basis // 2,
            transcendentals=0,
        ),
        name="exchange_rows",
    )(*operands)


def body(owners, integrals, block_index, live_count, orbitals, metric):
    basis, occupied = orbitals.shape
    naux = metric.shape[1]
    q_dev = naux // owners

    slab, pairs, metric_split = half_transform(integrals, block_index.T, live_count, orbitals, metric, q_dev, owners)

    trade = functools.partial(lax.all_to_all, axis_name="aux", split_axis=0, concat_axis=0, tiled=True)
    held = trade(pairs).reshape(naux, occupied // owners, occupied)
    fitted = apply_metric(metric, metric_split, held)
    fitted = trade(fitted.reshape(owners, q_dev, occupied // owners, occupied))
    if (occupied // owners) % 8:
        fitted = fitted.transpose(1, 0, 2, 3).reshape(q_dev, occupied, occupied)

    def swap(x, bit):
        return lax.ppermute(x, "aux", [(d, d ^ bit) for d in range(owners)])

    away, fitted = exchange_rows(slab, fitted, owners, 3, BF16)
    far = swap(away, 1)
    (away,) = exchange_rows(slab, fitted, owners, 1, BF16)
    near = swap(away, 1)
    (away,) = exchange_rows(slab, fitted, owners, 2, BF16, far)
    far = swap(away, 2)
    (near,) = exchange_rows(slab, fitted, owners, 0, F32, near)
    near = near + far.astype(F32)
    total = near[0]
    for k in range(1, owners // 4):
        total = total + swap(near[k].astype(BF16), 4 * k).astype(F32)
    return total


def solution(mesh):
    placed = (
        P(("groups", "aux"), None, None),
        P(("groups", "aux"), None),
        P(("groups", "aux")),
        P("groups", None),
        P("groups", None),
    )
    return jax.shard_map(
        functools.partial(body, mesh.shape["aux"]),
        mesh=mesh, in_specs=placed, out_specs=P(("groups", "aux"), None), check_vma=False,
    )
```

```python
import functools

import jax
import jax.numpy as jnp
from jax import lax
from jax.experimental import pallas as pl
from jax.experimental.pallas import tpu as pltpu
from jax.sharding import PartitionSpec as P

UNROLL = 32
CHUNK = 32
F32 = jnp.float32
BF16 = jnp.bfloat16


def rank_slots(live, index_ref, rows, meta, nblk, nkeys):
    slots = index_ref.shape[1]
    wide = rows.shape[1]
    nothing = float(slots * 256)
    rows[...] = jnp.full(rows.shape, nkeys, F32)
    key = index_ref[0:1, :] * nblk + index_ref[1:2, :]
    slot = lax.broadcasted_iota(jnp.int32, (1, slots), 1)
    rows[0:1, 0:slots] = jnp.where(slot < live, key, nkeys).astype(F32)
    rows[1:2, 0:slots] = (slot * 256 + index_ref[2:3, :]).astype(F32)
    row = rows[0:1, :]
    column = rows[...].T[:, 0:1]
    before = lax.broadcasted_iota(jnp.int32, (wide, wide), 0) < lax.broadcasted_iota(jnp.int32, (wide, wide), 1)
    same = (column == row) & before
    rank = jnp.sum(jnp.where(same, 1.0, 0.0), axis=0, keepdims=True)
    place = jnp.sum(jnp.where(same | (column < row), 1.0, 0.0), axis=0, keepdims=True)
    lives = row < nkeys
    last = 2.0 * jnp.max(jnp.where(lives, row, 0.0), axis=1, keepdims=True)
    rows[1:2, :] = rows[1:2, :] - nothing
    rows[2:3, :] = jnp.where(lives, place, -1.0)
    rows[3:4, :] = 2.0 * row + jnp.where(rank == 0.0, 1.0, 0.0) - last
    columns = rows[...].T
    found = columns[:, 2:3] == lax.broadcasted_iota(jnp.int32, (1, wide), 1).astype(F32)
    members = jnp.sum(jnp.where(found, columns[:, 1:2], 0.0), axis=0, keepdims=True)
    keys = jnp.sum(jnp.where(found, columns[:, 3:4], 0.0), axis=0, keepdims=True)
    meta[0:1, :] = (members + nothing).astype(jnp.int32)
    meta[1:2, :] = (keys + last).astype(jnp.int32)


def half_kernel(
    owners, q_dev, live_ref, index_hbm, blocks_hbm, orb_hbm, metric_hbm, slab, pairs_ref, split_ref,
    index_ref, held, orb_ref, metric_ref, orb_t, rows, meta, facts, in_sem, small_sem,
):
    slots, size, _ = blocks_hbm.shape
    occupied = orb_ref.shape[1]
    nblk = orb_ref.shape[0] // size
    nkeys = q_dev * nblk
    chunks = slots // CHUNK

    def fetch(c):
        part = pl.ds(c * CHUNK, CHUNK)
        return pltpu.make_async_copy(blocks_hbm.at[part], held.at[part], in_sem.at[c])

    def clear(first, last):
        @pl.loop(first, last, step=8)
        def _(k):
            for u in range(8):
                slab[k + u] = jnp.zeros((size, occupied), BF16)

    small = [
        pltpu.make_async_copy(source, target, small_sem.at[1 + k])
        for k, (source, target) in enumerate(
            [(index_hbm, index_ref), (orb_hbm, orb_ref), (metric_hbm, metric_ref)]
        )
    ]
    for copy in small:
        copy.start()
    for c in range(chunks):
        fetch(c).start()

    held[slots] = jnp.zeros((size, size), BF16)
    clear(0, nkeys // 2)

    small[0].wait()
    rank_slots(live_ref[0], index_ref, rows, meta, nblk, nkeys)
    copy = pltpu.make_async_copy(meta, facts, small_sem.at[0])
    copy.start()

    clear(nkeys // 2, nkeys)
    small[1].wait()
    for b in range(nblk):
        part = slice(b * size, (b + 1) * size)
        orb_t[:, part] = orb_ref[part, :].T
    small[2].wait()
    metric = metric_ref[...]
    high = metric.astype(BF16)
    naux = metric.shape[0]
    split_ref[0:naux, :] = high
    split_ref[naux : 2 * naux, :] = (metric - high.astype(F32)).astype(BF16)

    copy.wait()
    for c in range(chunks):
        fetch(c).wait()

    def step(g, total):
        for u in range(UNROLL):
            slot, code = facts[0, g * UNROLL + u], facts[1, g * UNROLL + u]
            orbs = orb_ref[pl.ds(pl.multiple_of((slot & 255) * size, size), size), :]
            product = jnp.dot(held[slot >> 8], orbs, preferred_element_type=F32)
            total = jnp.where((code & 1) == 1, product, total + product)
            slab[code >> 1] = total.astype(BF16)
        return total

    lax.fori_loop(0, (live_ref[0] + UNROLL - 1) // UNROLL, step, jnp.zeros((size, occupied), F32))

    @pl.loop(0, q_dev // 2, unroll=4)
    def _(t):
        block = jnp.concatenate(
            [slab[pl.ds((2 * t + u) * nblk, nblk)].reshape(nblk * size, occupied) for u in range(2)], axis=1
        )
        total = jnp.dot(orb_t[...], block, preferred_element_type=F32)
        for u in range(2):
            pair = total[:, u * occupied : (u + 1) * occupied].T
            if owners:
                pairs_ref[:, 2 * t + u] = pair.reshape(owners, occupied // owners, occupied).astype(BF16)
            else:
                pairs_ref[2 * t + u] = pair.astype(BF16)


def half_transform(blocks, index, live, orbitals, metric, q_dev, owners):
    slots, size, _ = blocks.shape
    basis, occupied = orbitals.shape
    nblk = basis // size
    split = (occupied // owners) % 8 == 0
    pairs_shape = (owners, q_dev, occupied // owners, occupied) if split else (q_dev, occupied, occupied)
    wide = -(-(slots + UNROLL) // 128) * 128
    slab, pairs, metric_split = pl.pallas_call(
        functools.partial(half_kernel, owners if split else 0, q_dev),
        out_shape=(
            pltpu.VMEM((q_dev * nblk, size, occupied), BF16),
            jax.ShapeDtypeStruct(pairs_shape, BF16),
            pltpu.VMEM((2 * metric.shape[0], metric.shape[1]), BF16),
        ),
        in_specs=[pl.BlockSpec(memory_space=pltpu.SMEM)] + [pl.BlockSpec(memory_space=pl.ANY)] * 4,
        out_specs=(pl.BlockSpec(memory_space=pltpu.VMEM),) * 3,
        scratch_shapes=[
            pltpu.VMEM(index.shape, jnp.int32),
            pltpu.VMEM((slots + 1, size, size), BF16),
            pltpu.VMEM((basis, occupied), BF16),
            pltpu.VMEM(metric.shape, F32),
            pltpu.VMEM((occupied, basis), BF16),
            pltpu.VMEM((8, wide), F32),
            pltpu.VMEM((8, wide), jnp.int32),
            pltpu.SMEM((8, wide), jnp.int32),
            pltpu.SemaphoreType.DMA((slots // CHUNK,)),
            pltpu.SemaphoreType.DMA((4,)),
        ],
        compiler_params=pltpu.CompilerParams(vmem_limit_bytes=36 * 2**20),
        cost_estimate=pl.CostEstimate(
            flops=2 * slots * size * size * occupied + 2 * q_dev * basis * occupied * occupied,
            bytes_accessed=2 * slots * size * size + 2 * q_dev * basis * occupied,
            transcendentals=0,
        ),
        name="half_transform_pairs",
    )(live, *(pltpu.with_memory_space_constraint(x, pltpu.HBM) for x in (index, blocks, orbitals, metric)))
    if not split:
        pairs = pairs.reshape(q_dev, owners, occupied // owners, occupied).transpose(1, 0, 2, 3)
    return slab.reshape(q_dev, basis, occupied), pairs, metric_split


def metric_kernel(split_ref, held_ref, out_ref, spread, mixed):
    naux, each, occupied = held_ref.shape
    spread[...] = held_ref[...].astype(F32).reshape(naux * each, occupied)
    for r in range(0, each, 2):
        both = [spread[pl.ds(r + u, naux, stride=each), :].astype(BF16) for u in range(2)]
        parts = jnp.dot(split_ref[...], jnp.concatenate(both, axis=1), preferred_element_type=F32)
        fitted = parts[:naux] + parts[naux:]
        for u in range(2):
            mixed[pl.ds(r + u, naux, stride=each), :] = fitted[:, u * occupied : (u + 1) * occupied]
    out_ref[...] = mixed[...].reshape(naux, each, occupied).astype(BF16)


def apply_metric(metric, metric_split, held):
    naux, each, occupied = held.shape
    if each % 8:
        fitted = jnp.einsum("qp,pij->qij", metric, held.astype(F32), precision=lax.Precision.HIGHEST)
        return fitted.astype(BF16)
    return pl.pallas_call(
        metric_kernel,
        out_shape=jax.ShapeDtypeStruct(held.shape, BF16),
        in_specs=[pl.BlockSpec(memory_space=pltpu.VMEM)] * 2,
        out_specs=pl.BlockSpec(memory_space=pltpu.VMEM),
        scratch_shapes=[pltpu.VMEM((naux * each, occupied), F32)] * 2,
        compiler_params=pltpu.CompilerParams(vmem_limit_bytes=12 * 2**20),
        cost_estimate=pl.CostEstimate(
            flops=4 * naux * naux * each * occupied, bytes_accessed=4 * naux * each * occupied, transcendentals=0
        ),
        name="apply_metric",
    )(pltpu.with_memory_space_constraint(metric_split, pltpu.VMEM), held)


def gather_fitted(fitted_ref, fitted):
    q_dev = fitted.shape[0] // fitted.shape[1]
    occupied = fitted.shape[1]
    for q in range(q_dev):
        if len(fitted_ref.shape) == 4:
            block = fitted_ref[:, q].astype(F32).reshape(occupied, occupied).astype(BF16)
        else:
            block = fitted_ref[q]
        fitted[q * occupied : (q + 1) * occupied, :] = block


def exchange_kernel(start, together, more, slab, fitted_ref, *refs):
    refs = list(refs)
    more_ref = refs.pop(0) if more else None
    out_ref = refs.pop(0)
    if start == 3:
        fitted = refs.pop(0)
        gather_fitted(fitted_ref, fitted)
    else:
        fitted = fitted_ref
    q_dev = slab.shape[0]
    parts, each, occupied = out_ref.shape
    me = lax.axis_index("aux").astype(jnp.int32)

    @pl.loop(0, parts // together)
    def _(g):
        rows = []
        for u in range(together):
            owner = (4 * (g * together + u) + start) ^ me
            rows.append(pl.ds(pl.multiple_of(owner * each, each), each))
        every = jnp.concatenate(
            [jnp.concatenate([slab[q, r, :] for r in rows], axis=0) for q in range(q_dev)], axis=1
        )
        sums = jnp.dot(every, fitted[...], preferred_element_type=F32)
        for u in range(together):
            part = sums[u * each : (u + 1) * each]
            if more:
                part = part + more_ref[g * together + u].astype(F32)
            out_ref[g * together + u] = part.astype(out_ref.dtype)


def exchange_rows(slab, fitted, owners, start, dtype, more=None):
    q_dev, basis, occupied = slab.shape
    each = basis // owners
    parts = owners // 4
    out = [jax.ShapeDtypeStruct((parts, each, occupied), dtype)]
    if start == 3:
        out.append(jax.ShapeDtypeStruct((q_dev * occupied, occupied), BF16))
    operands = [pltpu.with_memory_space_constraint(slab, pltpu.VMEM), fitted] + ([] if more is None else [more])
    return pl.pallas_call(
        functools.partial(exchange_kernel, start, 4 if parts % 4 == 0 else 1, more is not None),
        out_shape=out,
        in_specs=[pl.BlockSpec(memory_space=pltpu.VMEM)] * len(operands),
        out_specs=[pl.BlockSpec(memory_space=pltpu.VMEM)] * len(out),
        compiler_params=pltpu.CompilerParams(vmem_limit_bytes=24 * 2**20),
        cost_estimate=pl.CostEstimate(
            flops=2 * q_dev * occupied * basis * occupied // 4,
            bytes_accessed=q_dev * occupied * basis // 2,
            transcendentals=0,
        ),
        name="exchange_rows",
    )(*operands)


def body(owners, integrals, block_index, live_count, orbitals, metric):
    basis, occupied = orbitals.shape
    naux = metric.shape[1]
    q_dev = naux // owners

    slab, pairs, metric_split = half_transform(integrals, block_index.T, live_count, orbitals, metric, q_dev, owners)

    trade = functools.partial(lax.all_to_all, axis_name="aux", split_axis=0, concat_axis=0, tiled=True)
    held = trade(pairs).reshape(naux, occupied // owners, occupied)
    fitted = apply_metric(metric, metric_split, held)
    fitted = trade(fitted.reshape(owners, q_dev, occupied // owners, occupied))
    if (occupied // owners) % 8:
        fitted = fitted.transpose(1, 0, 2, 3).reshape(q_dev, occupied, occupied)

    def swap(x, bit):
        return lax.ppermute(x, "aux", [(d, d ^ bit) for d in range(owners)])

    away, fitted = exchange_rows(slab, fitted, owners, 3, BF16)
    far = swap(away, 1)
    (away,) = exchange_rows(slab, fitted, owners, 1, BF16)
    near = swap(away, 1)
    (away,) = exchange_rows(slab, fitted, owners, 2, BF16, far)
    far = swap(away, 2)
    (near,) = exchange_rows(slab, fitted, owners, 0, F32, near)
    near = near + far.astype(F32)
    total = near[0]
    for k in range(1, owners // 4):
        total = total + swap(near[k].astype(BF16), 4 * k).astype(F32)
    return total


def solution(mesh):
    placed = (
        P(("groups", "aux"), None, None),
        P(("groups", "aux"), None),
        P(("groups", "aux")),
        P("groups", None),
        P("groups", None),
    )
    return jax.shard_map(
        functools.partial(body, mesh.shape["aux"]),
        mesh=mesh, in_specs=placed, out_specs=P(("groups", "aux"), None), check_vma=False,
    )
```

```python
import functools

import jax
import jax.numpy as jnp
from jax import lax
from jax.experimental import pallas as pl
from jax.experimental.pallas import tpu as pltpu
from jax.sharding import PartitionSpec as P

UNROLL = 32
CHUNK = 32
F32 = jnp.float32
BF16 = jnp.bfloat16


def rank_slots(live, index_ref, rows, meta, nblk, nkeys):
    slots = index_ref.shape[1]
    wide = rows.shape[1]
    nothing = float(slots * 256)
    rows[...] = jnp.full(rows.shape, nkeys, F32)
    key = index_ref[0:1, :] * nblk + index_ref[1:2, :]
    slot = lax.broadcasted_iota(jnp.int32, (1, slots), 1)
    rows[0:1, 0:slots] = jnp.where(slot < live, key, nkeys).astype(F32)
    rows[1:2, 0:slots] = (slot * 256 + index_ref[2:3, :]).astype(F32)
    row = rows[0:1, :]
    column = rows[...].T[:, 0:1]
    before = lax.broadcasted_iota(jnp.int32, (wide, wide), 0) < lax.broadcasted_iota(jnp.int32, (wide, wide), 1)
    same = (column == row) & before
    rank = jnp.sum(jnp.where(same, 1.0, 0.0), axis=0, keepdims=True)
    place = jnp.sum(jnp.where(same | (column < row), 1.0, 0.0), axis=0, keepdims=True)
    lives = row < nkeys
    last = 2.0 * jnp.max(jnp.where(lives, row, 0.0), axis=1, keepdims=True)
    rows[1:2, :] = rows[1:2, :] - nothing
    rows[2:3, :] = jnp.where(lives, place, -1.0)
    rows[3:4, :] = 2.0 * row + jnp.where(rank == 0.0, 1.0, 0.0) - last
    columns = rows[...].T
    found = columns[:, 2:3] == lax.broadcasted_iota(jnp.int32, (1, wide), 1).astype(F32)
    members = jnp.sum(jnp.where(found, columns[:, 1:2], 0.0), axis=0, keepdims=True)
    keys = jnp.sum(jnp.where(found, columns[:, 3:4], 0.0), axis=0, keepdims=True)
    meta[0:1, :] = (members + nothing).astype(jnp.int32)
    meta[1:2, :] = (keys + last).astype(jnp.int32)


def half_kernel(
    owners, q_dev, live_ref, index_hbm, blocks_hbm, orb_hbm, metric_hbm, slab, pairs_ref, split_ref,
    index_ref, held, orb_ref, metric_ref, orb_t, rows, meta, facts, in_sem, small_sem,
):
    slots, size, _ = blocks_hbm.shape
    occupied = orb_ref.shape[1]
    nblk = orb_ref.shape[0] // size
    nkeys = q_dev * nblk
    chunks = slots // CHUNK

    def fetch(c):
        part = pl.ds(c * CHUNK, CHUNK)
        return pltpu.make_async_copy(blocks_hbm.at[part], held.at[part], in_sem.at[c])

    def clear(first, last):
        @pl.loop(first, last, step=8)
        def _(k):
            for u in range(8):
                slab[k + u] = jnp.zeros((size, occupied), BF16)

    small = [
        pltpu.make_async_copy(source, target, small_sem.at[1 + k])
        for k, (source, target) in enumerate(
            [(index_hbm, index_ref), (orb_hbm, orb_ref), (metric_hbm, metric_ref)]
        )
    ]
    for copy in small:
        copy.start()
    for c in range(chunks):
        fetch(c).start()

    held[slots] = jnp.zeros((size, size), BF16)
    clear(0, nkeys // 2)

    small[0].wait()
    rank_slots(live_ref[0], index_ref, rows, meta, nblk, nkeys)
    copy = pltpu.make_async_copy(meta, facts, small_sem.at[0])
    copy.start()

    clear(nkeys // 2, nkeys)
    small[1].wait()
    for b in range(nblk):
        part = slice(b * size, (b + 1) * size)
        orb_t[:, part] = orb_ref[part, :].T
    small[2].wait()
    metric = metric_ref[...]
    high = metric.astype(BF16)
    naux = metric.shape[0]
    split_ref[0:naux, :] = high
    split_ref[naux : 2 * naux, :] = (metric - high.astype(F32)).astype(BF16)

    copy.wait()
    for c in range(chunks):
        fetch(c).wait()

    def step(g, total):
        for u in range(UNROLL):
            slot, code = facts[0, g * UNROLL + u], facts[1, g * UNROLL + u]
            orbs = orb_ref[pl.ds(pl.multiple_of((slot & 255) * size, size), size), :]
            product = jnp.dot(held[slot >> 8], orbs, preferred_element_type=F32)
            total = jnp.where((code & 1) == 1, product, total + product)
            slab[code >> 1] = total.astype(BF16)
        return total

    lax.fori_loop(0, (live_ref[0] + UNROLL - 1) // UNROLL, step, jnp.zeros((size, occupied), F32))

    @pl.loop(0, q_dev // 2, unroll=4)
    def _(t):
        block = jnp.concatenate(
            [slab[pl.ds((2 * t + u) * nblk, nblk)].reshape(nblk * size, occupied) for u in range(2)], axis=1
        )
        total = jnp.dot(orb_t[...], block, preferred_element_type=F32)
        for u in range(2):
            pair = total[:, u * occupied : (u + 1) * occupied].T
            if owners:
                pairs_ref[:, 2 * t + u] = pair.reshape(owners, occupied // owners, occupied).astype(BF16)
            else:
                pairs_ref[2 * t + u] = pair.astype(BF16)


def half_transform(blocks, index, live, orbitals, metric, q_dev, owners):
    slots, size, _ = blocks.shape
    basis, occupied = orbitals.shape
    nblk = basis // size
    split = (occupied // owners) % 8 == 0
    pairs_shape = (owners, q_dev, occupied // owners, occupied) if split else (q_dev, occupied, occupied)
    wide = -(-(slots + UNROLL) // 128) * 128
    slab, pairs, metric_split = pl.pallas_call(
        functools.partial(half_kernel, owners if split else 0, q_dev),
        out_shape=(
            pltpu.VMEM((q_dev * nblk, size, occupied), BF16),
            jax.ShapeDtypeStruct(pairs_shape, BF16),
            pltpu.VMEM((2 * metric.shape[0], metric.shape[1]), BF16),
        ),
        in_specs=[pl.BlockSpec(memory_space=pltpu.SMEM)] + [pl.BlockSpec(memory_space=pl.ANY)] * 4,
        out_specs=(pl.BlockSpec(memory_space=pltpu.VMEM),) * 3,
        scratch_shapes=[
            pltpu.VMEM(index.shape, jnp.int32),
            pltpu.VMEM((slots + 1, size, size), BF16),
            pltpu.VMEM((basis, occupied), BF16),
            pltpu.VMEM(metric.shape, F32),
            pltpu.VMEM((occupied, basis), BF16),
            pltpu.VMEM((8, wide), F32),
            pltpu.VMEM((8, wide), jnp.int32),
            pltpu.SMEM((8, wide), jnp.int32),
            pltpu.SemaphoreType.DMA((slots // CHUNK,)),
            pltpu.SemaphoreType.DMA((4,)),
        ],
        compiler_params=pltpu.CompilerParams(vmem_limit_bytes=36 * 2**20),
        cost_estimate=pl.CostEstimate(
            flops=2 * slots * size * size * occupied + 2 * q_dev * basis * occupied * occupied,
            bytes_accessed=2 * slots * size * size + 2 * q_dev * basis * occupied,
            transcendentals=0,
        ),
        name="half_transform_pairs",
    )(live, *(pltpu.with_memory_space_constraint(x, pltpu.HBM) for x in (index, blocks, orbitals, metric)))
    if not split:
        pairs = pairs.reshape(q_dev, owners, occupied // owners, occupied).transpose(1, 0, 2, 3)
    return slab.reshape(q_dev, basis, occupied), pairs, metric_split


def metric_kernel(split_ref, held_ref, out_ref, spread, mixed):
    naux, each, occupied = held_ref.shape
    spread[...] = held_ref[...].astype(F32).reshape(naux * each, occupied)
    for r in range(0, each, 2):
        both = [spread[pl.ds(r + u, naux, stride=each), :].astype(BF16) for u in range(2)]
        parts = jnp.dot(split_ref[...], jnp.concatenate(both, axis=1), preferred_element_type=F32)
        fitted = parts[:naux] + parts[naux:]
        for u in range(2):
            mixed[pl.ds(r + u, naux, stride=each), :] = fitted[:, u * occupied : (u + 1) * occupied]
    out_ref[...] = mixed[...].reshape(naux, each, occupied).astype(BF16)


def apply_metric(metric, metric_split, held):
    naux, each, occupied = held.shape
    if each % 8:
        fitted = jnp.einsum("qp,pij->qij", metric, held.astype(F32), precision=lax.Precision.HIGHEST)
        return fitted.astype(BF16)
    return pl.pallas_call(
        metric_kernel,
        out_shape=jax.ShapeDtypeStruct(held.shape, BF16),
        in_specs=[pl.BlockSpec(memory_space=pltpu.VMEM)] * 2,
        out_specs=pl.BlockSpec(memory_space=pltpu.VMEM),
        scratch_shapes=[pltpu.VMEM((naux * each, occupied), F32)] * 2,
        compiler_params=pltpu.CompilerParams(vmem_limit_bytes=12 * 2**20),
        cost_estimate=pl.CostEstimate(
            flops=4 * naux * naux * each * occupied, bytes_accessed=4 * naux * each * occupied, transcendentals=0
        ),
        name="apply_metric",
    )(pltpu.with_memory_space_constraint(metric_split, pltpu.VMEM), held)


def gather_fitted(fitted_ref, fitted):
    q_dev = fitted.shape[0] // fitted.shape[1]
    occupied = fitted.shape[1]
    for q in range(q_dev):
        if len(fitted_ref.shape) == 4:
            block = fitted_ref[:, q].astype(F32).reshape(occupied, occupied).astype(BF16)
        else:
            block = fitted_ref[q]
        fitted[q * occupied : (q + 1) * occupied, :] = block


def exchange_kernel(start, more, slab, fitted_ref, *refs):
    refs = list(refs)
    more_ref = refs.pop(0) if more else None
    out_ref = refs.pop(0)
    if start == 3:
        fitted = refs.pop(0)
        gather_fitted(fitted_ref, fitted)
    else:
        fitted = fitted_ref
    q_dev = slab.shape[0]
    parts, each, occupied = out_ref.shape
    me = lax.axis_index("aux").astype(jnp.int32)
    core = (me & 1) ^ (start & 1)
    first, second = 2 + 2 * core, 4 - 2 * core
    fixed = me ^ (start & 1) ^ (first if start & 2 else 0)
    together = 4 if parts % 4 == 0 else 1

    for g in range(parts // together):
        rows = []
        for h in range(g * together, (g + 1) * together):
            owner = fixed ^ (8 * (h % (parts // 2)))
            if h >= parts // 2:
                owner = owner ^ second
            rows.append(pl.ds(pl.multiple_of(owner * each, each), each))
        every = jnp.concatenate(
            [jnp.concatenate([slab[q, r, :] for r in rows], axis=0) for q in range(q_dev)], axis=1
        )
        sums = jnp.dot(every, fitted[...], preferred_element_type=F32)
        for u in range(together):
            part = sums[u * each : (u + 1) * each]
            if more:
                part = part + more_ref[g * together + u].astype(F32)
            out_ref[g * together + u] = part.astype(out_ref.dtype)


def exchange_rows(slab, fitted, owners, start, dtype, more=None):
    q_dev, basis, occupied = slab.shape
    each = basis // owners
    parts = owners // 4
    out = [jax.ShapeDtypeStruct((parts, each, occupied), dtype)]
    if start == 3:
        out.append(jax.ShapeDtypeStruct((q_dev * occupied, occupied), BF16))
    operands = [pltpu.with_memory_space_constraint(slab, pltpu.VMEM), fitted] + ([] if more is None else [more])
    return pl.pallas_call(
        functools.partial(exchange_kernel, start, more is not None),
        out_shape=out,
        in_specs=[pl.BlockSpec(memory_space=pltpu.VMEM)] * len(operands),
        out_specs=[pl.BlockSpec(memory_space=pltpu.VMEM)] * len(out),
        compiler_params=pltpu.CompilerParams(vmem_limit_bytes=24 * 2**20),
        cost_estimate=pl.CostEstimate(
            flops=2 * q_dev * occupied * basis * occupied // 4,
            bytes_accessed=q_dev * occupied * basis // 2,
            transcendentals=0,
        ),
        name="exchange_rows",
    )(*operands)


def body(owners, integrals, block_index, live_count, orbitals, metric):
    basis, occupied = orbitals.shape
    naux = metric.shape[1]
    q_dev = naux // owners

    slab, pairs, metric_split = half_transform(integrals, block_index.T, live_count, orbitals, metric, q_dev, owners)

    trade = functools.partial(lax.all_to_all, axis_name="aux", split_axis=0, concat_axis=0, tiled=True)
    held = trade(pairs).reshape(naux, occupied // owners, occupied)
    fitted = apply_metric(metric, metric_split, held)
    fitted = trade(fitted.reshape(owners, q_dev, occupied // owners, occupied))
    if (occupied // owners) % 8:
        fitted = fitted.transpose(1, 0, 2, 3).reshape(q_dev, occupied, occupied)

    def swap(x, even, odd):
        return lax.ppermute(x, "aux", [(d, d ^ (odd if d % 2 else even)) for d in range(owners)])

    away, fitted = exchange_rows(slab, fitted, owners, 3, BF16)
    far = swap(away, 1, 1)
    (away,) = exchange_rows(slab, fitted, owners, 1, BF16)
    near = swap(away, 1, 1)
    (away,) = exchange_rows(slab, fitted, owners, 2, BF16, far)
    far = swap(away, 2, 4)
    (near,) = exchange_rows(slab, fitted, owners, 0, F32, near)
    half = owners // 8
    away = (near[half:] + far[half:].astype(F32)).astype(BF16)
    near = near[:half] + far[:half].astype(F32)
    near = near + swap(away, 4, 2).astype(F32)
    total = near[0]
    for k in range(1, half):
        total = total + swap(near[k].astype(BF16), 8 * k, 8 * k).astype(F32)
    return total


def solution(mesh):
    placed = (
        P(("groups", "aux"), None, None),
        P(("groups", "aux"), None),
        P(("groups", "aux")),
        P("groups", None),
        P("groups", None),
    )
    return jax.shard_map(
        functools.partial(body, mesh.shape["aux"]),
        mesh=mesh, in_specs=placed, out_specs=P(("groups", "aux"), None), check_vma=False,
    )
```

```python
import functools

import jax
import jax.numpy as jnp
from jax import lax
from jax.experimental import pallas as pl
from jax.experimental.pallas import tpu as pltpu
from jax.sharding import PartitionSpec as P

UNROLL = 32
CHUNK = 32
F32 = jnp.float32
BF16 = jnp.bfloat16


def rank_slots(live, index_ref, rows, meta, nblk, nkeys):
    slots = index_ref.shape[1]
    wide = rows.shape[1]
    nothing = float(slots * 256)
    rows[...] = jnp.full(rows.shape, nkeys, F32)
    key = index_ref[0:1, :] * nblk + index_ref[1:2, :]
    slot = lax.broadcasted_iota(jnp.int32, (1, slots), 1)
    rows[0:1, 0:slots] = jnp.where(slot < live, key, nkeys).astype(F32)
    rows[1:2, 0:slots] = (slot * 256 + index_ref[2:3, :]).astype(F32)
    row = rows[0:1, :]
    column = rows[...].T[:, 0:1]
    before = lax.broadcasted_iota(jnp.int32, (wide, wide), 0) < lax.broadcasted_iota(jnp.int32, (wide, wide), 1)
    same = (column == row) & before
    rank = jnp.sum(jnp.where(same, 1.0, 0.0), axis=0, keepdims=True)
    place = jnp.sum(jnp.where(same | (column < row), 1.0, 0.0), axis=0, keepdims=True)
    lives = row < nkeys
    last = 2.0 * jnp.max(jnp.where(lives, row, 0.0), axis=1, keepdims=True)
    rows[1:2, :] = rows[1:2, :] - nothing
    rows[2:3, :] = jnp.where(lives, place, -1.0)
    rows[3:4, :] = 2.0 * row + jnp.where(rank == 0.0, 1.0, 0.0) - last
    columns = rows[...].T
    found = columns[:, 2:3] == lax.broadcasted_iota(jnp.int32, (1, wide), 1).astype(F32)
    members = jnp.sum(jnp.where(found, columns[:, 1:2], 0.0), axis=0, keepdims=True)
    keys = jnp.sum(jnp.where(found, columns[:, 3:4], 0.0), axis=0, keepdims=True)
    meta[0:1, :] = (members + nothing).astype(jnp.int32)
    meta[1:2, :] = (keys + last).astype(jnp.int32)


def half_kernel(
    owners, q_dev, live_ref, index_hbm, blocks_hbm, orb_hbm, metric_hbm, slab, pairs_ref, split_ref,
    index_ref, held, orb_ref, metric_ref, orb_t, rows, meta, facts, in_sem, small_sem,
):
    slots, size, _ = blocks_hbm.shape
    occupied = orb_ref.shape[1]
    nblk = orb_ref.shape[0] // size
    nkeys = q_dev * nblk
    chunks = slots // CHUNK

    def fetch(c):
        part = pl.ds(c * CHUNK, CHUNK)
        return pltpu.make_async_copy(blocks_hbm.at[part], held.at[part], in_sem.at[c])

    def clear(first, last):
        @pl.loop(first, last, step=8)
        def _(k):
            for u in range(8):
                slab[k + u] = jnp.zeros((size, occupied), BF16)

    small = [
        pltpu.make_async_copy(source, target, small_sem.at[1 + k])
        for k, (source, target) in enumerate(
            [(index_hbm, index_ref), (orb_hbm, orb_ref), (metric_hbm, metric_ref)]
        )
    ]
    for copy in small:
        copy.start()
    for c in range(chunks):
        fetch(c).start()

    held[slots] = jnp.zeros((size, size), BF16)
    clear(0, nkeys // 2)

    small[0].wait()
    rank_slots(live_ref[0], index_ref, rows, meta, nblk, nkeys)
    copy = pltpu.make_async_copy(meta, facts, small_sem.at[0])
    copy.start()

    clear(nkeys // 2, nkeys)
    small[1].wait()
    for b in range(nblk):
        part = slice(b * size, (b + 1) * size)
        orb_t[:, part] = orb_ref[part, :].T
    small[2].wait()
    metric = metric_ref[...]
    high = metric.astype(BF16)
    naux = metric.shape[0]
    split_ref[0:naux, :] = high
    split_ref[naux : 2 * naux, :] = (metric - high.astype(F32)).astype(BF16)

    copy.wait()
    for c in range(chunks):
        fetch(c).wait()

    def step(g, total):
        for u in range(UNROLL):
            slot, code = facts[0, g * UNROLL + u], facts[1, g * UNROLL + u]
            orbs = orb_ref[pl.ds(pl.multiple_of((slot & 255) * size, size), size), :]
            product = jnp.dot(held[slot >> 8], orbs, preferred_element_type=F32)
            total = jnp.where((code & 1) == 1, product, total + product)
            slab[code >> 1] = total.astype(BF16)
        return total

    lax.fori_loop(0, (live_ref[0] + UNROLL - 1) // UNROLL, step, jnp.zeros((size, occupied), F32))

    @pl.loop(0, q_dev // 2, unroll=4)
    def _(t):
        block = jnp.concatenate(
            [slab[pl.ds((2 * t + u) * nblk, nblk)].reshape(nblk * size, occupied) for u in range(2)], axis=1
        )
        total = jnp.dot(orb_t[...], block, preferred_element_type=F32)
        for u in range(2):
            pair = total[:, u * occupied : (u + 1) * occupied].T
            if owners:
                pairs_ref[:, 2 * t + u] = pair.reshape(owners, occupied // owners, occupied).astype(BF16)
            else:
                pairs_ref[2 * t + u] = pair.astype(BF16)


def half_transform(blocks, index, live, orbitals, metric, q_dev, owners):
    slots, size, _ = blocks.shape
    basis, occupied = orbitals.shape
    nblk = basis // size
    split = (occupied // owners) % 8 == 0
    pairs_shape = (owners, q_dev, occupied // owners, occupied) if split else (q_dev, occupied, occupied)
    wide = -(-(slots + UNROLL) // 128) * 128
    slab, pairs, metric_split = pl.pallas_call(
        functools.partial(half_kernel, owners if split else 0, q_dev),
        out_shape=(
            pltpu.VMEM((q_dev * nblk, size, occupied), BF16),
            jax.ShapeDtypeStruct(pairs_shape, BF16),
            pltpu.VMEM((2 * metric.shape[0], metric.shape[1]), BF16),
        ),
        in_specs=[pl.BlockSpec(memory_space=pltpu.SMEM)] + [pl.BlockSpec(memory_space=pl.ANY)] * 4,
        out_specs=(pl.BlockSpec(memory_space=pltpu.VMEM),) * 3,
        scratch_shapes=[
            pltpu.VMEM(index.shape, jnp.int32),
            pltpu.VMEM((slots + 1, size, size), BF16),
            pltpu.VMEM((basis, occupied), BF16),
            pltpu.VMEM(metric.shape, F32),
            pltpu.VMEM((occupied, basis), BF16),
            pltpu.VMEM((8, wide), F32),
            pltpu.VMEM((8, wide), jnp.int32),
            pltpu.SMEM((8, wide), jnp.int32),
            pltpu.SemaphoreType.DMA((slots // CHUNK,)),
            pltpu.SemaphoreType.DMA((4,)),
        ],
        compiler_params=pltpu.CompilerParams(vmem_limit_bytes=36 * 2**20),
        cost_estimate=pl.CostEstimate(
            flops=2 * slots * size * size * occupied + 2 * q_dev * basis * occupied * occupied,
            bytes_accessed=2 * slots * size * size + 2 * q_dev * basis * occupied,
            transcendentals=0,
        ),
        name="half_transform_pairs",
    )(live, *(pltpu.with_memory_space_constraint(x, pltpu.HBM) for x in (index, blocks, orbitals, metric)))
    if not split:
        pairs = pairs.reshape(q_dev, owners, occupied // owners, occupied).transpose(1, 0, 2, 3)
    return slab.reshape(q_dev, basis, occupied), pairs, metric_split


def metric_kernel(split_ref, held_ref, out_ref, spread, mixed):
    naux, each, occupied = held_ref.shape
    spread[...] = held_ref[...].astype(F32).reshape(naux * each, occupied)
    for r in range(0, each, 2):
        both = [spread[pl.ds(r + u, naux, stride=each), :].astype(BF16) for u in range(2)]
        parts = jnp.dot(split_ref[...], jnp.concatenate(both, axis=1), preferred_element_type=F32)
        fitted = parts[:naux] + parts[naux:]
        for u in range(2):
            mixed[pl.ds(r + u, naux, stride=each), :] = fitted[:, u * occupied : (u + 1) * occupied]
    out_ref[...] = mixed[...].reshape(naux, each, occupied).astype(BF16)


def apply_metric(metric, metric_split, held):
    naux, each, occupied = held.shape
    if each % 8:
        fitted = jnp.einsum("qp,pij->qij", metric, held.astype(F32), precision=lax.Precision.HIGHEST)
        return fitted.astype(BF16)
    return pl.pallas_call(
        metric_kernel,
        out_shape=jax.ShapeDtypeStruct(held.shape, BF16),
        in_specs=[pl.BlockSpec(memory_space=pltpu.VMEM)] * 2,
        out_specs=pl.BlockSpec(memory_space=pltpu.VMEM),
        scratch_shapes=[pltpu.VMEM((naux * each, occupied), F32)] * 2,
        compiler_params=pltpu.CompilerParams(vmem_limit_bytes=12 * 2**20),
        cost_estimate=pl.CostEstimate(
            flops=4 * naux * naux * each * occupied, bytes_accessed=4 * naux * each * occupied, transcendentals=0
        ),
        name="apply_metric",
    )(pltpu.with_memory_space_constraint(metric_split, pltpu.VMEM), held)


def gather_fitted(fitted_ref, fitted):
    q_dev = fitted.shape[0] // fitted.shape[1]
    occupied = fitted.shape[1]
    for q in range(q_dev):
        if len(fitted_ref.shape) == 4:
            block = fitted_ref[:, q].astype(F32).reshape(occupied, occupied).astype(BF16)
        else:
            block = fitted_ref[q]
        fitted[q * occupied : (q + 1) * occupied, :] = block


def exchange_kernel(blocks, gather, more, slab, fitted_ref, *refs):
    refs = list(refs)
    more_ref = refs.pop(0) if more else None
    out_refs = [refs.pop(0) for _ in blocks]
    if gather:
        fitted = refs.pop(0)
        gather_fitted(fitted_ref, fitted)
    else:
        fitted = fitted_ref
    q_dev = slab.shape[0]
    each = out_refs[0].shape[1]
    me = lax.axis_index("aux").astype(jnp.int32)
    todo = [(k, c, h) for c, part in enumerate(blocks) for h, k in enumerate(part)]
    together = next(n for n in (4, 3, 2, 1) if len(todo) % n == 0)
    for g in range(0, len(todo), together):
        rows = [pl.ds(pl.multiple_of((me ^ k) * each, each), each) for k, _, _ in todo[g : g + together]]
        every = jnp.concatenate(
            [jnp.concatenate([slab[q, r, :] for r in rows], axis=0) for q in range(q_dev)], axis=1
        )
        sums = jnp.dot(every, fitted[...], preferred_element_type=F32)
        for u, (_, c, h) in enumerate(todo[g : g + together]):
            part = sums[u * each : (u + 1) * each]
            if more:
                part = part + more_ref[g + u].astype(F32)
            out_refs[c][h] = part.astype(out_refs[c].dtype)


def exchange_rows(slab, fitted, owners, blocks, dtype, gather=False, more=None):
    q_dev, basis, occupied = slab.shape
    each = basis // owners
    count = sum(len(part) for part in blocks)
    out = [jax.ShapeDtypeStruct((len(part), each, occupied), dtype) for part in blocks]
    if gather:
        out.append(jax.ShapeDtypeStruct((q_dev * occupied, occupied), BF16))
    operands = [pltpu.with_memory_space_constraint(slab, pltpu.VMEM), fitted] + ([] if more is None else [more])
    return pl.pallas_call(
        functools.partial(exchange_kernel, blocks, gather, more is not None),
        out_shape=out,
        in_specs=[pl.BlockSpec(memory_space=pltpu.VMEM)] * len(operands),
        out_specs=[pl.BlockSpec(memory_space=pltpu.VMEM)] * len(out),
        compiler_params=pltpu.CompilerParams(vmem_limit_bytes=24 * 2**20),
        cost_estimate=pl.CostEstimate(
            flops=2 * q_dev * occupied * count * each * occupied,
            bytes_accessed=2 * q_dev * occupied * count * each,
            transcendentals=0,
        ),
        name="exchange_rows",
    )(*operands)


def body(owners, integrals, block_index, live_count, orbitals, metric):
    basis, occupied = orbitals.shape
    naux = metric.shape[1]
    q_dev = naux // owners

    slab, pairs, metric_split = half_transform(integrals, block_index.T, live_count, orbitals, metric, q_dev, owners)

    trade = functools.partial(lax.all_to_all, axis_name="aux", split_axis=0, concat_axis=0, tiled=True)
    held = trade(pairs).reshape(naux, occupied // owners, occupied)
    fitted = apply_metric(metric, metric_split, held)
    fitted = trade(fitted.reshape(owners, q_dev, occupied // owners, occupied))
    if (occupied // owners) % 8:
        fitted = fitted.transpose(1, 0, 2, 3).reshape(q_dev, occupied, occupied)

    def swap(x, bits):
        return lax.ppermute(x, "aux", [(d, d ^ bits) for d in range(owners)])

    far = range(0, owners, 8)
    leave = [tuple(x + k for k in far) for x in (2, 4, 6)]
    stay = [tuple(far)]
    flip = lambda parts: [tuple(k ^ 1 for k in part) for part in parts]
    *away, fitted = exchange_rows(slab, fitted, owners, flip([sum(leave, ())]), BF16, gather=True)
    from_core = swap(away[0], 1)
    away = exchange_rows(slab, fitted, owners, flip(stay), BF16)
    to_stay = swap(away[0], 1)
    away = exchange_rows(slab, fitted, owners, leave, BF16, more=from_core)
    arrived = [swap(x, bits) for x, bits in zip(away, (2, 4, 6))]
    (near,) = exchange_rows(slab, fitted, owners, stay, F32, more=to_stay)
    for x in arrived:
        near = near + x.astype(F32)
    total = near[0]
    for c, k in enumerate(far):
        if k:
            total = total + swap(near[c].astype(BF16), k).astype(F32)
    return total


def solution(mesh):
    placed = (
        P(("groups", "aux"), None, None),
        P(("groups", "aux"), None),
        P(("groups", "aux")),
        P("groups", None),
        P("groups", None),
    )
    return jax.shard_map(
        functools.partial(body, mesh.shape["aux"]),
        mesh=mesh, in_specs=placed, out_specs=P(("groups", "aux"), None), check_vma=False,
    )
```

```python
import functools

import jax
import jax.numpy as jnp
from jax import lax
from jax.experimental import pallas as pl
from jax.experimental.pallas import tpu as pltpu
from jax.sharding import PartitionSpec as P

UNROLL = 32
CHUNK = 32
F32 = jnp.float32
BF16 = jnp.bfloat16


def rank_slots(live, index_ref, rows, meta, nblk, nkeys, chunks):
    slots = index_ref.shape[1]
    wide = rows.shape[1]
    nothing = float(slots * 256)
    never = float(chunks * nkeys)
    rows[...] = jnp.full(rows.shape, nkeys, F32)
    key = index_ref[0:1, :] * nblk + index_ref[1:2, :]
    slot = lax.broadcasted_iota(jnp.int32, (1, slots), 1)
    rows[0:1, 0:slots] = jnp.where(slot < live, key, nkeys).astype(F32)
    rows[1:2, 0:slots] = (slot * 256 + index_ref[2:3, :]).astype(F32)
    rows[2:3, 0:slots] = (slot // CHUNK).astype(F32)
    row = rows[0:1, :]
    lives = row < nkeys
    columns = rows[...].T
    late = jnp.max(jnp.where(columns[:, 0:1] == row, columns[:, 2:3], 0.0), axis=0, keepdims=True)
    order = jnp.where(lives, late * nkeys + row, never)
    column = jnp.broadcast_to(order, (8, wide)).T[:, 0:1]
    before = lax.broadcasted_iota(jnp.int32, (wide, wide), 0) < lax.broadcasted_iota(jnp.int32, (wide, wide), 1)
    same = (column == order) & before
    rank = jnp.sum(jnp.where(same, 1.0, 0.0), axis=0, keepdims=True)
    place = jnp.sum(jnp.where(same | (column < order), 1.0, 0.0), axis=0, keepdims=True)
    opens = jnp.where(rank == 0.0, 1.0, 0.0)
    end = jnp.max(jnp.where(lives, order, 0.0), axis=1, keepdims=True)
    last = 2.0 * jnp.max(jnp.where(lives & (order == end), row, 0.0), axis=1, keepdims=True)
    rows[1:2, :] = rows[1:2, :] - nothing
    rows[2:3, :] = jnp.where(lives, place, -1.0)
    rows[3:4, :] = 2.0 * row + opens - last
    rows[4:5, :] = late - (chunks - 1)
    columns = rows[...].T
    found = columns[:, 2:3] == lax.broadcasted_iota(jnp.int32, (1, wide), 1).astype(F32)
    for r, (c, rest) in enumerate([(1, nothing), (3, last), (4, float(chunks - 1))]):
        facts = jnp.sum(jnp.where(found, columns[:, c : c + 1], 0.0), axis=0, keepdims=True) + rest
        meta[r : r + 1, :] = facts.astype(jnp.int32)


def half_kernel(
    owners, q_dev, live_ref, index_hbm, blocks_hbm, orb_hbm, metric_hbm, slab, pairs_ref, split_ref,
    index_ref, held, orb_ref, metric_ref, orb_t, rows, meta, facts, in_sem, small_sem,
):
    slots, size, _ = blocks_hbm.shape
    occupied = orb_ref.shape[1]
    nblk = orb_ref.shape[0] // size
    nkeys = q_dev * nblk
    chunks = slots // CHUNK

    def fetch(c):
        part = pl.ds(c * CHUNK, CHUNK)
        return pltpu.make_async_copy(blocks_hbm.at[part], held.at[part], in_sem.at[c])

    def clear(first, last):
        @pl.loop(first, last, step=8)
        def _(k):
            for u in range(8):
                slab[k + u] = jnp.zeros((size, occupied), BF16)

    small = [
        pltpu.make_async_copy(source, target, small_sem.at[1 + k])
        for k, (source, target) in enumerate(
            [(index_hbm, index_ref), (orb_hbm, orb_ref), (metric_hbm, metric_ref)]
        )
    ]
    small[0].start()
    small[1].start()
    for c in range(chunks):
        fetch(c).start()
    small[2].start()

    held[slots] = jnp.zeros((size, size), BF16)
    clear(0, nkeys // 2)

    small[0].wait()
    rank_slots(live_ref[0], index_ref, rows, meta, nblk, nkeys, chunks)
    copy = pltpu.make_async_copy(meta, facts, small_sem.at[0])
    copy.start()

    clear(nkeys // 2, nkeys)
    small[1].wait()
    for b in range(nblk):
        part = slice(b * size, (b + 1) * size)
        orb_t[:, part] = orb_ref[part, :].T
    copy.wait()

    def arrive(c, nothing):
        fetch(c).wait()
        return nothing

    def step(g, carry):
        arrived, total = carry
        needed = jnp.maximum(arrived, facts[2, g * UNROLL + UNROLL - 1] + 1)
        lax.fori_loop(arrived, needed, arrive, 0)
        for u in range(UNROLL):
            slot, code = facts[0, g * UNROLL + u], facts[1, g * UNROLL + u]
            orbs = orb_ref[pl.ds(pl.multiple_of((slot & 255) * size, size), size), :]
            product = jnp.dot(held[slot >> 8], orbs, preferred_element_type=F32)
            total = jnp.where((code & 1) == 1, product, total + product)
            slab[code >> 1] = total.astype(BF16)
        return needed, total

    bodies = (live_ref[0] + UNROLL - 1) // UNROLL
    arrived, _ = lax.fori_loop(0, bodies, step, (jnp.int32(0), jnp.zeros((size, occupied), F32)))
    lax.fori_loop(arrived, chunks, arrive, 0)

    small[2].wait()
    metric = metric_ref[...]
    high = metric.astype(BF16)
    naux = metric.shape[0]
    split_ref[0:naux, :] = high
    split_ref[naux : 2 * naux, :] = (metric - high.astype(F32)).astype(BF16)

    @pl.loop(0, q_dev // 2, unroll=8)
    def _(t):
        block = jnp.concatenate(
            [slab[pl.ds((2 * t + u) * nblk, nblk)].reshape(nblk * size, occupied) for u in range(2)], axis=1
        )
        total = jnp.dot(orb_t[...], block, preferred_element_type=F32)
        for u in range(2):
            pair = total[:, u * occupied : (u + 1) * occupied].T
            if owners:
                pairs_ref[:, 2 * t + u] = pair.reshape(owners, occupied // owners, occupied).astype(BF16)
            else:
                pairs_ref[2 * t + u] = pair.astype(BF16)


def half_transform(blocks, index, live, orbitals, metric, q_dev, owners):
    slots, size, _ = blocks.shape
    basis, occupied = orbitals.shape
    nblk = basis // size
    split = (occupied // owners) % 8 == 0
    pairs_shape = (owners, q_dev, occupied // owners, occupied) if split else (q_dev, occupied, occupied)
    wide = -(-(slots + UNROLL) // 128) * 128
    slab, pairs, metric_split = pl.pallas_call(
        functools.partial(half_kernel, owners if split else 0, q_dev),
        out_shape=(
            pltpu.VMEM((q_dev * nblk, size, occupied), BF16),
            jax.ShapeDtypeStruct(pairs_shape, BF16),
            pltpu.VMEM((2 * metric.shape[0], metric.shape[1]), BF16),
        ),
        in_specs=[pl.BlockSpec(memory_space=pltpu.SMEM)] + [pl.BlockSpec(memory_space=pl.ANY)] * 4,
        out_specs=(pl.BlockSpec(memory_space=pltpu.VMEM),) * 3,
        scratch_shapes=[
            pltpu.VMEM(index.shape, jnp.int32),
            pltpu.VMEM((slots + 1, size, size), BF16),
            pltpu.VMEM((basis, occupied), BF16),
            pltpu.VMEM(metric.shape, F32),
            pltpu.VMEM((occupied, basis), BF16),
            pltpu.VMEM((8, wide), F32),
            pltpu.VMEM((8, wide), jnp.int32),
            pltpu.SMEM((8, wide), jnp.int32),
            pltpu.SemaphoreType.DMA((slots // CHUNK,)),
            pltpu.SemaphoreType.DMA((4,)),
        ],
        compiler_params=pltpu.CompilerParams(vmem_limit_bytes=36 * 2**20),
        cost_estimate=pl.CostEstimate(
            flops=2 * slots * size * size * occupied + 2 * q_dev * basis * occupied * occupied,
            bytes_accessed=2 * slots * size * size + 2 * q_dev * basis * occupied,
            transcendentals=0,
        ),
        name="half_transform_pairs",
    )(live, *(pltpu.with_memory_space_constraint(x, pltpu.HBM) for x in (index, blocks, orbitals, metric)))
    if not split:
        pairs = pairs.reshape(q_dev, owners, occupied // owners, occupied).transpose(1, 0, 2, 3)
    return slab.reshape(q_dev, basis, occupied), pairs, metric_split


def metric_kernel(split_ref, held_ref, out_ref, spread, mixed):
    naux, each, occupied = held_ref.shape
    spread[...] = held_ref[...].astype(F32).reshape(naux * each, occupied)
    for r in range(0, each, 2):
        both = [spread[pl.ds(r + u, naux, stride=each), :].astype(BF16) for u in range(2)]
        parts = jnp.dot(split_ref[...], jnp.concatenate(both, axis=1), preferred_element_type=F32)
        fitted = parts[:naux] + parts[naux:]
        for u in range(2):
            mixed[pl.ds(r + u, naux, stride=each), :] = fitted[:, u * occupied : (u + 1) * occupied]
    out_ref[...] = mixed[...].reshape(naux, each, occupied).astype(BF16)


def apply_metric(metric, metric_split, held):
    naux, each, occupied = held.shape
    if each % 8:
        fitted = jnp.einsum("qp,pij->qij", metric, held.astype(F32), precision=lax.Precision.HIGHEST)
        return fitted.astype(BF16)
    return pl.pallas_call(
        metric_kernel,
        out_shape=jax.ShapeDtypeStruct(held.shape, BF16),
        in_specs=[pl.BlockSpec(memory_space=pltpu.VMEM)] * 2,
        out_specs=pl.BlockSpec(memory_space=pltpu.VMEM),
        scratch_shapes=[pltpu.VMEM((naux * each, occupied), F32)] * 2,
        compiler_params=pltpu.CompilerParams(vmem_limit_bytes=12 * 2**20),
        cost_estimate=pl.CostEstimate(
            flops=4 * naux * naux * each * occupied, bytes_accessed=4 * naux * each * occupied, transcendentals=0
        ),
        name="apply_metric",
    )(pltpu.with_memory_space_constraint(metric_split, pltpu.VMEM), held)


def gather_fitted(fitted_ref, fitted):
    q_dev = fitted.shape[0] // fitted.shape[1]
    occupied = fitted.shape[1]
    for q in range(q_dev):
        if len(fitted_ref.shape) == 4:
            block = fitted_ref[:, q].astype(F32).reshape(occupied, occupied).astype(BF16)
        else:
            block = fitted_ref[q]
        fitted[q * occupied : (q + 1) * occupied, :] = block


def exchange_kernel(blocks, gather, more, slab, fitted_ref, *refs):
    refs = list(refs)
    more_ref = refs.pop(0) if more else None
    out_refs = [refs.pop(0) for _ in blocks]
    if gather:
        fitted = refs.pop(0)
        gather_fitted(fitted_ref, fitted)
    else:
        fitted = fitted_ref
    q_dev = slab.shape[0]
    each = out_refs[0].shape[1]
    me = lax.axis_index("aux").astype(jnp.int32)
    todo = [(k, c, h) for c, part in enumerate(blocks) for h, k in enumerate(part)]
    together = next(n for n in (4, 3, 2, 1) if len(todo) % n == 0)
    for g in range(0, len(todo), together):
        rows = [pl.ds(pl.multiple_of((me ^ k) * each, each), each) for k, _, _ in todo[g : g + together]]
        every = jnp.concatenate(
            [jnp.concatenate([slab[q, r, :] for r in rows], axis=0) for q in range(q_dev)], axis=1
        )
        sums = jnp.dot(every, fitted[...], preferred_element_type=F32)
        for u, (_, c, h) in enumerate(todo[g : g + together]):
            part = sums[u * each : (u + 1) * each]
            if more:
                part = part + more_ref[g + u].astype(F32)
            out_refs[c][h] = part.astype(out_refs[c].dtype)


def exchange_rows(slab, fitted, owners, blocks, dtype, gather=False, more=None):
    q_dev, basis, occupied = slab.shape
    each = basis // owners
    count = sum(len(part) for part in blocks)
    out = [jax.ShapeDtypeStruct((len(part), each, occupied), dtype) for part in blocks]
    if gather:
        out.append(jax.ShapeDtypeStruct((q_dev * occupied, occupied), BF16))
    operands = [pltpu.with_memory_space_constraint(slab, pltpu.VMEM), fitted] + ([] if more is None else [more])
    return pl.pallas_call(
        functools.partial(exchange_kernel, blocks, gather, more is not None),
        out_shape=out,
        in_specs=[pl.BlockSpec(memory_space=pltpu.VMEM)] * len(operands),
        out_specs=[pl.BlockSpec(memory_space=pltpu.VMEM)] * len(out),
        compiler_params=pltpu.CompilerParams(vmem_limit_bytes=24 * 2**20),
        cost_estimate=pl.CostEstimate(
            flops=2 * q_dev * occupied * count * each * occupied,
            bytes_accessed=2 * q_dev * occupied * count * each,
            transcendentals=0,
        ),
        name="exchange_rows",
    )(*operands)


def body(owners, integrals, block_index, live_count, orbitals, metric):
    basis, occupied = orbitals.shape
    naux = metric.shape[1]
    q_dev = naux // owners

    slab, pairs, metric_split = half_transform(integrals, block_index.T, live_count, orbitals, metric, q_dev, owners)

    trade = functools.partial(lax.all_to_all, axis_name="aux", split_axis=0, concat_axis=0, tiled=True)
    held = trade(pairs).reshape(naux, occupied // owners, occupied)
    fitted = apply_metric(metric, metric_split, held)
    fitted = trade(fitted.reshape(owners, q_dev, occupied // owners, occupied))
    if (occupied // owners) % 8:
        fitted = fitted.transpose(1, 0, 2, 3).reshape(q_dev, occupied, occupied)

    def swap(x, bits):
        return lax.ppermute(x, "aux", [(d, d ^ bits) for d in range(owners)])

    far = range(0, owners, 8)
    leave = [tuple(x + k for k in far) for x in (2, 4, 6)]
    stay = [tuple(far)]
    flip = lambda parts: [tuple(k ^ 1 for k in part) for part in parts]
    *away, fitted = exchange_rows(slab, fitted, owners, flip([sum(leave, ())]), BF16, gather=True)
    from_core = swap(away[0], 1)
    away = exchange_rows(slab, fitted, owners, flip(stay), BF16)
    to_stay = swap(away[0], 1)
    away = exchange_rows(slab, fitted, owners, leave, BF16, more=from_core)
    arrived = [swap(x, bits) for x, bits in zip(away, (2, 4, 6))]
    (near,) = exchange_rows(slab, fitted, owners, stay, F32, more=to_stay)
    for x in arrived:
        near = near + x.astype(F32)
    total = near[0]
    for c, k in enumerate(far):
        if k:
            total = total + swap(near[c].astype(BF16), k).astype(F32)
    return total


def solution(mesh):
    placed = (
        P(("groups", "aux"), None, None),
        P(("groups", "aux"), None),
        P(("groups", "aux")),
        P("groups", None),
        P("groups", None),
    )
    return jax.shard_map(
        functools.partial(body, mesh.shape["aux"]),
        mesh=mesh, in_specs=placed, out_specs=P(("groups", "aux"), None), check_vma=False,
    )
```

```python
import functools

import jax
import jax.numpy as jnp
from jax import lax
from jax.experimental import pallas as pl
from jax.experimental.pallas import tpu as pltpu
from jax.sharding import PartitionSpec as P

UNROLL = 32
CHUNK = 32
TURNS = 3
F32 = jnp.float32
BF16 = jnp.bfloat16


def rank_slots(live, index_ref, rows, meta, nblk, nkeys, chunks):
    slots = index_ref.shape[1]
    wide = rows.shape[1]
    nothing = float(slots * 256)
    never = float(chunks * nkeys)
    rows[...] = jnp.full(rows.shape, nkeys, F32)
    key = index_ref[0:1, :] * nblk + index_ref[1:2, :]
    slot = lax.broadcasted_iota(jnp.int32, (1, slots), 1)
    rows[0:1, 0:slots] = jnp.where(slot < live, key, nkeys).astype(F32)
    rows[1:2, 0:slots] = (slot * 256 + index_ref[2:3, :]).astype(F32)
    rows[2:3, 0:slots] = (slot // CHUNK).astype(F32)
    row = rows[0:1, :]
    lives = row < nkeys
    columns = rows[...].T
    late = jnp.max(jnp.where(columns[:, 0:1] == row, columns[:, 2:3], 0.0), axis=0, keepdims=True)
    order = jnp.where(lives, late * nkeys + row, never)
    column = jnp.broadcast_to(order, (8, wide)).T[:, 0:1]
    before = lax.broadcasted_iota(jnp.int32, (wide, wide), 0) < lax.broadcasted_iota(jnp.int32, (wide, wide), 1)
    same = (column == order) & before
    rank = jnp.sum(jnp.where(same, 1.0, 0.0), axis=0, keepdims=True)
    place = jnp.sum(jnp.where(same | (column < order), 1.0, 0.0), axis=0, keepdims=True)
    opens = jnp.where(rank == 0.0, 1.0, 0.0)
    end = jnp.max(jnp.where(lives, order, 0.0), axis=1, keepdims=True)
    last = 2.0 * jnp.max(jnp.where(lives & (order == end), row, 0.0), axis=1, keepdims=True)
    rows[1:2, :] = rows[1:2, :] - nothing
    rows[2:3, :] = jnp.where(lives, place, -1.0)
    rows[3:4, :] = 2.0 * row + opens - last
    rows[4:5, :] = late - (chunks - 1)
    columns = rows[...].T
    found = columns[:, 2:3] == lax.broadcasted_iota(jnp.int32, (1, wide), 1).astype(F32)
    for r, (c, rest) in enumerate([(1, nothing), (3, last), (4, float(chunks - 1))]):
        facts = jnp.sum(jnp.where(found, columns[:, c : c + 1], 0.0), axis=0, keepdims=True) + rest
        meta[r : r + 1, :] = facts.astype(jnp.int32)


def half_kernel(
    owners, q_dev, live_ref, index_hbm, blocks_hbm, orb_hbm, metric_hbm, slab, pairs_ref, split_ref,
    index_ref, held, orb_ref, metric_ref, orb_t, rows, meta, facts, in_sem, small_sem,
):
    slots, size, _ = blocks_hbm.shape
    occupied = orb_ref.shape[1]
    nblk = orb_ref.shape[0] // size
    nkeys = q_dev * nblk
    chunks = slots // CHUNK

    def fetch(c):
        part = pl.ds(c * CHUNK, CHUNK)
        return pltpu.make_async_copy(blocks_hbm.at[part], held.at[part], in_sem.at[c])

    def clear(first, last):
        @pl.loop(first, last, step=8)
        def _(k):
            for u in range(8):
                slab[k + u] = jnp.zeros((size, occupied), BF16)

    small = [
        pltpu.make_async_copy(source, target, small_sem.at[1 + k])
        for k, (source, target) in enumerate(
            [(index_hbm, index_ref), (orb_hbm, orb_ref), (metric_hbm, metric_ref)]
        )
    ]
    small[0].start()
    small[1].start()
    for c in range(chunks):
        fetch(c).start()
    small[2].start()

    held[slots] = jnp.zeros((size, size), BF16)
    clear(0, nkeys // 2)

    small[0].wait()
    rank_slots(live_ref[0], index_ref, rows, meta, nblk, nkeys, chunks)
    copy = pltpu.make_async_copy(meta, facts, small_sem.at[0])
    copy.start()

    clear(nkeys // 2, nkeys)
    small[1].wait()
    copy.wait()

    def arrive(c, nothing):
        fetch(c).wait()
        return nothing

    def turn(b):
        part = pl.ds(pl.multiple_of(b * size, size), size)
        orb_t[:, part] = orb_ref[part, :].T

    def step(g, carry):
        arrived, total = carry
        needed = jnp.maximum(arrived, facts[2, g * UNROLL + UNROLL - 1] + 1)
        lax.fori_loop(arrived, needed, arrive, 0)
        for u in range(TURNS):
            turn(jnp.minimum(g * TURNS + u, nblk - 1))
        for u in range(UNROLL):
            slot, code = facts[0, g * UNROLL + u], facts[1, g * UNROLL + u]
            orbs = orb_ref[pl.ds(pl.multiple_of((slot & 255) * size, size), size), :]
            product = jnp.dot(held[slot >> 8], orbs, preferred_element_type=F32)
            total = jnp.where((code & 1) == 1, product, total + product)
            slab[code >> 1] = total.astype(BF16)
        return needed, total

    bodies = (live_ref[0] + UNROLL - 1) // UNROLL
    arrived, _ = lax.fori_loop(0, bodies, step, (jnp.int32(0), jnp.zeros((size, occupied), F32)))
    lax.fori_loop(arrived, chunks, arrive, 0)

    @pl.loop(jnp.minimum(bodies * TURNS, nblk), nblk)
    def _(b):
        turn(b)

    small[2].wait()
    metric = metric_ref[...]
    high = metric.astype(BF16)
    naux = metric.shape[0]
    split_ref[0:naux, :] = high
    split_ref[naux : 2 * naux, :] = (metric - high.astype(F32)).astype(BF16)

    @pl.loop(0, q_dev // 2, unroll=8)
    def _(t):
        block = jnp.concatenate(
            [slab[pl.ds((2 * t + u) * nblk, nblk)].reshape(nblk * size, occupied) for u in range(2)], axis=1
        )
        total = jnp.dot(orb_t[...], block, preferred_element_type=F32)
        for u in range(2):
            pair = total[:, u * occupied : (u + 1) * occupied].T
            if owners:
                pairs_ref[:, 2 * t + u] = pair.reshape(owners, occupied // owners, occupied).astype(BF16)
            else:
                pairs_ref[2 * t + u] = pair.astype(BF16)


def half_transform(blocks, index, live, orbitals, metric, q_dev, owners):
    slots, size, _ = blocks.shape
    basis, occupied = orbitals.shape
    nblk = basis // size
    split = (occupied // owners) % 8 == 0
    pairs_shape = (owners, q_dev, occupied // owners, occupied) if split else (q_dev, occupied, occupied)
    wide = -(-(slots + UNROLL) // 128) * 128
    slab, pairs, metric_split = pl.pallas_call(
        functools.partial(half_kernel, owners if split else 0, q_dev),
        out_shape=(
            pltpu.VMEM((q_dev * nblk, size, occupied), BF16),
            jax.ShapeDtypeStruct(pairs_shape, BF16),
            pltpu.VMEM((2 * metric.shape[0], metric.shape[1]), BF16),
        ),
        in_specs=[pl.BlockSpec(memory_space=pltpu.SMEM)] + [pl.BlockSpec(memory_space=pl.ANY)] * 4,
        out_specs=(pl.BlockSpec(memory_space=pltpu.VMEM),) * 3,
        scratch_shapes=[
            pltpu.VMEM(index.shape, jnp.int32),
            pltpu.VMEM((slots + 1, size, size), BF16),
            pltpu.VMEM((basis, occupied), BF16),
            pltpu.VMEM(metric.shape, F32),
            pltpu.VMEM((occupied, basis), BF16),
            pltpu.VMEM((8, wide), F32),
            pltpu.VMEM((8, wide), jnp.int32),
            pltpu.SMEM((8, wide), jnp.int32),
            pltpu.SemaphoreType.DMA((slots // CHUNK,)),
            pltpu.SemaphoreType.DMA((4,)),
        ],
        compiler_params=pltpu.CompilerParams(vmem_limit_bytes=36 * 2**20),
        cost_estimate=pl.CostEstimate(
            flops=2 * slots * size * size * occupied + 2 * q_dev * basis * occupied * occupied,
            bytes_accessed=2 * slots * size * size + 2 * q_dev * basis * occupied,
            transcendentals=0,
        ),
        name="half_transform_pairs",
    )(live, *(pltpu.with_memory_space_constraint(x, pltpu.HBM) for x in (index, blocks, orbitals, metric)))
    if not split:
        pairs = pairs.reshape(q_dev, owners, occupied // owners, occupied).transpose(1, 0, 2, 3)
    return slab.reshape(q_dev, basis, occupied), pairs, metric_split


def metric_kernel(split_ref, held_ref, out_ref, spread, mixed):
    naux, each, occupied = held_ref.shape
    spread[...] = held_ref[...].astype(F32).reshape(naux * each, occupied)
    for r in range(0, each, 2):
        both = [spread[pl.ds(r + u, naux, stride=each), :].astype(BF16) for u in range(2)]
        parts = jnp.dot(split_ref[...], jnp.concatenate(both, axis=1), preferred_element_type=F32)
        fitted = parts[:naux] + parts[naux:]
        for u in range(2):
            mixed[pl.ds(r + u, naux, stride=each), :] = fitted[:, u * occupied : (u + 1) * occupied]
    out_ref[...] = mixed[...].reshape(naux, each, occupied).astype(BF16)


def apply_metric(metric, metric_split, held):
    naux, each, occupied = held.shape
    if each % 8:
        fitted = jnp.einsum("qp,pij->qij", metric, held.astype(F32), precision=lax.Precision.HIGHEST)
        return fitted.astype(BF16)
    return pl.pallas_call(
        metric_kernel,
        out_shape=jax.ShapeDtypeStruct(held.shape, BF16),
        in_specs=[pl.BlockSpec(memory_space=pltpu.VMEM)] * 2,
        out_specs=pl.BlockSpec(memory_space=pltpu.VMEM),
        scratch_shapes=[pltpu.VMEM((naux * each, occupied), F32)] * 2,
        compiler_params=pltpu.CompilerParams(vmem_limit_bytes=12 * 2**20),
        cost_estimate=pl.CostEstimate(
            flops=4 * naux * naux * each * occupied, bytes_accessed=4 * naux * each * occupied, transcendentals=0
        ),
        name="apply_metric",
    )(pltpu.with_memory_space_constraint(metric_split, pltpu.VMEM), held)


def gather_fitted(fitted_ref, fitted):
    q_dev = fitted.shape[0] // fitted.shape[1]
    occupied = fitted.shape[1]
    for q in range(q_dev):
        if len(fitted_ref.shape) == 4:
            block = fitted_ref[:, q].astype(F32).reshape(occupied, occupied).astype(BF16)
        else:
            block = fitted_ref[q]
        fitted[q * occupied : (q + 1) * occupied, :] = block


def exchange_kernel(blocks, gather, more, slab, fitted_ref, *refs):
    refs = list(refs)
    more_ref = refs.pop(0) if more else None
    out_refs = [refs.pop(0) for _ in blocks]
    if gather:
        fitted = refs.pop(0)
        gather_fitted(fitted_ref, fitted)
    else:
        fitted = fitted_ref
    q_dev = slab.shape[0]
    each = out_refs[0].shape[1]
    me = lax.axis_index("aux").astype(jnp.int32)
    todo = [(k, c, h) for c, part in enumerate(blocks) for h, k in enumerate(part)]
    together = next(n for n in (4, 3, 2, 1) if len(todo) % n == 0)
    for g in range(0, len(todo), together):
        rows = [pl.ds(pl.multiple_of((me ^ k) * each, each), each) for k, _, _ in todo[g : g + together]]
        every = jnp.concatenate(
            [jnp.concatenate([slab[q, r, :] for r in rows], axis=0) for q in range(q_dev)], axis=1
        )
        sums = jnp.dot(every, fitted[...], preferred_element_type=F32)
        for u, (_, c, h) in enumerate(todo[g : g + together]):
            part = sums[u * each : (u + 1) * each]
            if more:
                part = part + more_ref[g + u].astype(F32)
            out_refs[c][h] = part.astype(out_refs[c].dtype)


def exchange_rows(slab, fitted, owners, blocks, dtype, gather=False, more=None):
    q_dev, basis, occupied = slab.shape
    each = basis // owners
    count = sum(len(part) for part in blocks)
    out = [jax.ShapeDtypeStruct((len(part), each, occupied), dtype) for part in blocks]
    if gather:
        out.append(jax.ShapeDtypeStruct((q_dev * occupied, occupied), BF16))
    operands = [pltpu.with_memory_space_constraint(slab, pltpu.VMEM), fitted] + ([] if more is None else [more])
    return pl.pallas_call(
        functools.partial(exchange_kernel, blocks, gather, more is not None),
        out_shape=out,
        in_specs=[pl.BlockSpec(memory_space=pltpu.VMEM)] * len(operands),
        out_specs=[pl.BlockSpec(memory_space=pltpu.VMEM)] * len(out),
        compiler_params=pltpu.CompilerParams(vmem_limit_bytes=24 * 2**20),
        cost_estimate=pl.CostEstimate(
            flops=2 * q_dev * occupied * count * each * occupied,
            bytes_accessed=2 * q_dev * occupied * count * each,
            transcendentals=0,
        ),
        name="exchange_rows",
    )(*operands)


def body(owners, integrals, block_index, live_count, orbitals, metric):
    basis, occupied = orbitals.shape
    naux = metric.shape[1]
    q_dev = naux // owners

    slab, pairs, metric_split = half_transform(integrals, block_index.T, live_count, orbitals, metric, q_dev, owners)

    trade = functools.partial(lax.all_to_all, axis_name="aux", split_axis=0, concat_axis=0, tiled=True)
    held = trade(pairs).reshape(naux, occupied // owners, occupied)
    fitted = apply_metric(metric, metric_split, held)
    fitted = trade(fitted.reshape(owners, q_dev, occupied // owners, occupied))
    if (occupied // owners) % 8:
        fitted = fitted.transpose(1, 0, 2, 3).reshape(q_dev, occupied, occupied)

    def swap(x, bits):
        return lax.ppermute(x, "aux", [(d, d ^ bits) for d in range(owners)])

    far = range(0, owners, 8)
    leave = [tuple(x + k for k in far) for x in (2, 4, 6)]
    stay = [tuple(far)]
    flip = lambda parts: [tuple(k ^ 1 for k in part) for part in parts]
    *away, fitted = exchange_rows(slab, fitted, owners, flip([sum(leave, ())]), BF16, gather=True)
    from_core = swap(away[0], 1)
    away = exchange_rows(slab, fitted, owners, flip(stay), BF16)
    to_stay = swap(away[0], 1)
    away = exchange_rows(slab, fitted, owners, leave, BF16, more=from_core)
    arrived = [swap(x, bits) for x, bits in zip(away, (2, 4, 6))]
    (near,) = exchange_rows(slab, fitted, owners, stay, F32, more=to_stay)
    for x in arrived:
        near = near + x.astype(F32)
    total = near[0]
    for c, k in enumerate(far):
        if k:
            total = total + swap(near[c].astype(BF16), k).astype(F32)
    return total


def solution(mesh):
    placed = (
        P(("groups", "aux"), None, None),
        P(("groups", "aux"), None),
        P(("groups", "aux")),
        P("groups", None),
        P("groups", None),
    )
    return jax.shard_map(
        functools.partial(body, mesh.shape["aux"]),
        mesh=mesh, in_specs=placed, out_specs=P(("groups", "aux"), None), check_vma=False,
    )
```

```python
import functools

import jax
import jax.numpy as jnp
from jax import lax
from jax.experimental import pallas as pl
from jax.experimental.pallas import tpu as pltpu
from jax.sharding import PartitionSpec as P

UNROLL = 32
CHUNK = 32
TURNS = 3
F32 = jnp.float32
BF16 = jnp.bfloat16


def rank_slots(live, index_ref, rows, meta, nblk, nkeys, chunks):
    slots = index_ref.shape[1]
    wide = rows.shape[1]
    never = float(chunks * nkeys)
    assert slots < 512 and nblk <= 32 and nkeys <= 512 and CHUNK % 8 == 0
    rows[...] = jnp.full(rows.shape, nkeys, F32)
    key = index_ref[0:1, :] * nblk + index_ref[1:2, :]
    slot = lax.broadcasted_iota(jnp.int32, (1, slots), 1)
    rows[0:1, 0:slots] = jnp.where(slot < live, key, nkeys).astype(F32)
    rows[1:2, 0:slots] = (slot * 32768 + index_ref[2:3, :] * 1024).astype(F32)
    row = rows[0:1, :]
    lives = row < nkeys
    tile = (8, wide)
    zero = jnp.zeros(tile, F32)
    lane = lax.broadcasted_iota(jnp.int32, tile, 1)
    ahead = lane - lax.broadcasted_iota(jnp.int32, tile, 0)

    every = jnp.broadcast_to(row, tile)
    columns = rows[...].T
    late = zero
    for s in range(0, slots, 8):
        late = jnp.where(columns[s : s + 8, 0:1] == every, float(s // CHUNK), late)
    late = jnp.max(late, axis=0, keepdims=True)
    order = jnp.where(lives, late * nkeys + row, never)

    every = jnp.broadcast_to(order, tile)
    columns = every.T
    rank, place = zero, zero
    for s in range(0, slots, 8):
        column = columns[s : s + 8, 0:1]
        same = (column == every) & (ahead > s)
        rank = rank + jnp.where(same, 1.0, 0.0)
        place = place + jnp.where(same | (column < every), 1.0, 0.0)
    rank = jnp.sum(rank, axis=0, keepdims=True)
    place = jnp.sum(place, axis=0, keepdims=True)
    end = jnp.max(jnp.where(lives, order, 0.0), axis=1, keepdims=True)
    last = jnp.max(jnp.where(lives & (order == end), row, 0.0), axis=1, keepdims=True)
    nothing = 2.0 * last + slots * 32768.0
    rows[1:2, :] = rows[1:2, :] + 2.0 * row + jnp.where(rank == 0.0, 1.0, 0.0) - nothing
    rows[2:3, :] = jnp.where(lives, place, -1.0)
    rows[3:4, :] = late - (chunks - 1)

    columns = rows[...].T
    spot = lane.astype(F32)
    number, need = zero, zero
    for s in range(0, slots, 8):
        found = columns[s : s + 8, 2:3] == spot
        number = number + jnp.where(found, columns[s : s + 8, 1:2], 0.0)
        need = need + jnp.where(found, columns[s : s + 8, 3:4], 0.0)
    meta[0:1, :] = (jnp.sum(number, axis=0, keepdims=True) + nothing).astype(jnp.int32)
    meta[1:2, :] = (jnp.sum(need, axis=0, keepdims=True) + (chunks - 1)).astype(jnp.int32)


def half_kernel(
    owners, q_dev, live_ref, index_hbm, blocks_hbm, orb_hbm, metric_hbm, slab, pairs_ref, split_ref,
    index_ref, held, orb_ref, metric_ref, orb_t, rows, meta, facts, in_sem, small_sem,
):
    slots, size, _ = blocks_hbm.shape
    occupied = orb_ref.shape[1]
    nblk = orb_ref.shape[0] // size
    nkeys = q_dev * nblk
    chunks = slots // CHUNK

    def fetch(c):
        part = pl.ds(c * CHUNK, CHUNK)
        return pltpu.make_async_copy(blocks_hbm.at[part], held.at[part], in_sem.at[c])

    def clear(first, last):
        @pl.loop(first, last, step=8)
        def _(k):
            for u in range(8):
                slab[k + u] = jnp.zeros((size, occupied), BF16)

    small = [
        pltpu.make_async_copy(source, target, small_sem.at[1 + k])
        for k, (source, target) in enumerate(
            [(index_hbm, index_ref), (orb_hbm, orb_ref), (metric_hbm, metric_ref)]
        )
    ]
    small[0].start()
    small[1].start()
    for c in range(chunks):
        fetch(c).start()
    small[2].start()

    held[slots] = jnp.zeros((size, size), BF16)
    clear(0, nkeys // 2)

    small[0].wait()
    rank_slots(live_ref[0], index_ref, rows, meta, nblk, nkeys, chunks)
    copy = pltpu.make_async_copy(meta, facts, small_sem.at[0])
    copy.start()

    clear(nkeys // 2, nkeys)
    small[1].wait()
    copy.wait()

    def arrive(c, nothing):
        fetch(c).wait()
        return nothing

    def turn(b):
        part = pl.ds(pl.multiple_of(b * size, size), size)
        orb_t[:, part] = orb_ref[part, :].T

    def step(g, carry):
        arrived, total = carry
        needed = jnp.maximum(arrived, facts[1, g * UNROLL + UNROLL - 1] + 1)
        lax.fori_loop(arrived, needed, arrive, 0)
        for u in range(TURNS):
            turn(jnp.minimum(g * TURNS + u, nblk - 1))
        empty = jnp.zeros((size, occupied), BF16)
        for u in range(0, UNROLL, 2):
            pair = [facts[0, g * UNROLL + u + w] for w in range(2)]
            orbs = [orb_ref[pl.ds(pl.multiple_of(((v >> 10) & 31) * size, size), size), :] for v in pair]
            diagonal = jnp.concatenate(
                [jnp.concatenate([orbs[0], empty], axis=1), jnp.concatenate([empty, orbs[1]], axis=1)], axis=0
            )
            blocks = jnp.concatenate([held[v >> 15] for v in pair], axis=1)
            products = jnp.dot(blocks, diagonal, preferred_element_type=F32)
            for w, v in enumerate(pair):
                product = products[:, w * occupied : (w + 1) * occupied]
                total = jnp.where((v & 1) == 1, product, total + product)
                slab[(v & 1023) >> 1] = total.astype(BF16)
        return needed, total

    bodies = (live_ref[0] + UNROLL - 1) // UNROLL
    arrived, _ = lax.fori_loop(0, bodies, step, (jnp.int32(0), jnp.zeros((size, occupied), F32)))
    lax.fori_loop(arrived, chunks, arrive, 0)

    @pl.loop(jnp.minimum(bodies * TURNS, nblk), nblk)
    def _(b):
        turn(b)

    small[2].wait()
    metric = metric_ref[...]
    high = metric.astype(BF16)
    naux = metric.shape[0]
    split_ref[0:naux, :] = high
    split_ref[naux : 2 * naux, :] = (metric - high.astype(F32)).astype(BF16)

    @pl.loop(0, q_dev // 2, unroll=8)
    def _(t):
        block = jnp.concatenate(
            [slab[pl.ds((2 * t + u) * nblk, nblk)].reshape(nblk * size, occupied) for u in range(2)], axis=1
        )
        total = jnp.dot(orb_t[...], block, preferred_element_type=F32)
        for u in range(2):
            pair = total[:, u * occupied : (u + 1) * occupied].T
            if owners:
                pairs_ref[:, 2 * t + u] = pair.reshape(owners, occupied // owners, occupied).astype(BF16)
            else:
                pairs_ref[2 * t + u] = pair.astype(BF16)


def half_transform(blocks, index, live, orbitals, metric, q_dev, owners):
    slots, size, _ = blocks.shape
    basis, occupied = orbitals.shape
    nblk = basis // size
    split = (occupied // owners) % 8 == 0
    pairs_shape = (owners, q_dev, occupied // owners, occupied) if split else (q_dev, occupied, occupied)
    wide = -(-(slots + UNROLL) // 128) * 128
    slab, pairs, metric_split = pl.pallas_call(
        functools.partial(half_kernel, owners if split else 0, q_dev),
        out_shape=(
            pltpu.VMEM((q_dev * nblk, size, occupied), BF16),
            jax.ShapeDtypeStruct(pairs_shape, BF16),
            pltpu.VMEM((2 * metric.shape[0], metric.shape[1]), BF16),
        ),
        in_specs=[pl.BlockSpec(memory_space=pltpu.SMEM)] + [pl.BlockSpec(memory_space=pl.ANY)] * 4,
        out_specs=(pl.BlockSpec(memory_space=pltpu.VMEM),) * 3,
        scratch_shapes=[
            pltpu.VMEM(index.shape, jnp.int32),
            pltpu.VMEM((slots + 1, size, size), BF16),
            pltpu.VMEM((basis, occupied), BF16),
            pltpu.VMEM(metric.shape, F32),
            pltpu.VMEM((occupied, basis), BF16),
            pltpu.VMEM((8, wide), F32),
            pltpu.VMEM((8, wide), jnp.int32),
            pltpu.SMEM((8, wide), jnp.int32),
            pltpu.SemaphoreType.DMA((slots // CHUNK,)),
            pltpu.SemaphoreType.DMA((4,)),
        ],
        compiler_params=pltpu.CompilerParams(vmem_limit_bytes=36 * 2**20),
        cost_estimate=pl.CostEstimate(
            flops=2 * slots * size * size * occupied + 2 * q_dev * basis * occupied * occupied,
            bytes_accessed=2 * slots * size * size + 2 * q_dev * basis * occupied,
            transcendentals=0,
        ),
        name="half_transform_pairs",
    )(live, *(pltpu.with_memory_space_constraint(x, pltpu.HBM) for x in (index, blocks, orbitals, metric)))
    if not split:
        pairs = pairs.reshape(q_dev, owners, occupied // owners, occupied).transpose(1, 0, 2, 3)
    return slab.reshape(q_dev, basis, occupied), pairs, metric_split


def metric_kernel(split_ref, held_ref, out_ref, spread, mixed):
    naux, each, occupied = held_ref.shape
    spread[...] = held_ref[...].astype(F32).reshape(naux * each, occupied)
    for r in range(0, each, 2):
        both = [spread[pl.ds(r + u, naux, stride=each), :].astype(BF16) for u in range(2)]
        parts = jnp.dot(split_ref[...], jnp.concatenate(both, axis=1), preferred_element_type=F32)
        fitted = parts[:naux] + parts[naux:]
        for u in range(2):
            mixed[pl.ds(r + u, naux, stride=each), :] = fitted[:, u * occupied : (u + 1) * occupied]
    out_ref[...] = mixed[...].reshape(naux, each, occupied).astype(BF16)


def apply_metric(metric, metric_split, held):
    naux, each, occupied = held.shape
    if each % 8:
        fitted = jnp.einsum("qp,pij->qij", metric, held.astype(F32), precision=lax.Precision.HIGHEST)
        return fitted.astype(BF16)
    return pl.pallas_call(
        metric_kernel,
        out_shape=jax.ShapeDtypeStruct(held.shape, BF16),
        in_specs=[pl.BlockSpec(memory_space=pltpu.VMEM)] * 2,
        out_specs=pl.BlockSpec(memory_space=pltpu.VMEM),
        scratch_shapes=[pltpu.VMEM((naux * each, occupied), F32)] * 2,
        compiler_params=pltpu.CompilerParams(vmem_limit_bytes=12 * 2**20),
        cost_estimate=pl.CostEstimate(
            flops=4 * naux * naux * each * occupied, bytes_accessed=4 * naux * each * occupied, transcendentals=0
        ),
        name="apply_metric",
    )(pltpu.with_memory_space_constraint(metric_split, pltpu.VMEM), held)


def gather_fitted(fitted_ref, fitted):
    q_dev = fitted.shape[0] // fitted.shape[1]
    occupied = fitted.shape[1]
    for q in range(q_dev):
        if len(fitted_ref.shape) == 4:
            block = fitted_ref[:, q].astype(F32).reshape(occupied, occupied).astype(BF16)
        else:
            block = fitted_ref[q]
        fitted[q * occupied : (q + 1) * occupied, :] = block


def exchange_kernel(blocks, gather, more, slab, fitted_ref, *refs):
    refs = list(refs)
    more_ref = refs.pop(0) if more else None
    out_refs = [refs.pop(0) for _ in blocks]
    if gather:
        fitted = refs.pop(0)
        gather_fitted(fitted_ref, fitted)
    else:
        fitted = fitted_ref
    q_dev = slab.shape[0]
    each = out_refs[0].shape[1]
    me = lax.axis_index("aux").astype(jnp.int32)
    todo = [(k, c, h) for c, part in enumerate(blocks) for h, k in enumerate(part)]
    together = next(n for n in (4, 3, 2, 1) if len(todo) % n == 0)
    for g in range(0, len(todo), together):
        rows = [pl.ds(pl.multiple_of((me ^ k) * each, each), each) for k, _, _ in todo[g : g + together]]
        every = jnp.concatenate(
            [jnp.concatenate([slab[q, r, :] for r in rows], axis=0) for q in range(q_dev)], axis=1
        )
        sums = jnp.dot(every, fitted[...], preferred_element_type=F32)
        for u, (_, c, h) in enumerate(todo[g : g + together]):
            part = sums[u * each : (u + 1) * each]
            if more:
                part = part + more_ref[g + u].astype(F32)
            out_refs[c][h] = part.astype(out_refs[c].dtype)


def exchange_rows(slab, fitted, owners, blocks, dtype, gather=False, more=None):
    q_dev, basis, occupied = slab.shape
    each = basis // owners
    count = sum(len(part) for part in blocks)
    out = [jax.ShapeDtypeStruct((len(part), each, occupied), dtype) for part in blocks]
    if gather:
        out.append(jax.ShapeDtypeStruct((q_dev * occupied, occupied), BF16))
    operands = [pltpu.with_memory_space_constraint(slab, pltpu.VMEM), fitted] + ([] if more is None else [more])
    return pl.pallas_call(
        functools.partial(exchange_kernel, blocks, gather, more is not None),
        out_shape=out,
        in_specs=[pl.BlockSpec(memory_space=pltpu.VMEM)] * len(operands),
        out_specs=[pl.BlockSpec(memory_space=pltpu.VMEM)] * len(out),
        compiler_params=pltpu.CompilerParams(vmem_limit_bytes=24 * 2**20),
        cost_estimate=pl.CostEstimate(
            flops=2 * q_dev * occupied * count * each * occupied,
            bytes_accessed=2 * q_dev * occupied * count * each,
            transcendentals=0,
        ),
        name="exchange_rows",
    )(*operands)


def body(owners, integrals, block_index, live_count, orbitals, metric):
    basis, occupied = orbitals.shape
    naux = metric.shape[1]
    q_dev = naux // owners

    slab, pairs, metric_split = half_transform(integrals, block_index.T, live_count, orbitals, metric, q_dev, owners)

    trade = functools.partial(lax.all_to_all, axis_name="aux", split_axis=0, concat_axis=0, tiled=True)
    held = trade(pairs).reshape(naux, occupied // owners, occupied)
    fitted = apply_metric(metric, metric_split, held)
    fitted = trade(fitted.reshape(owners, q_dev, occupied // owners, occupied))
    if (occupied // owners) % 8:
        fitted = fitted.transpose(1, 0, 2, 3).reshape(q_dev, occupied, occupied)

    def swap(x, bits):
        return lax.ppermute(x, "aux", [(d, d ^ bits) for d in range(owners)])

    far = range(0, owners, 8)
    leave = [tuple(x + k for k in far) for x in (2, 4, 6)]
    stay = [tuple(far)]
    flip = lambda parts: [tuple(k ^ 1 for k in part) for part in parts]
    *away, fitted = exchange_rows(slab, fitted, owners, flip([sum(leave, ())]), BF16, gather=True)
    from_core = swap(away[0], 1)
    away = exchange_rows(slab, fitted, owners, flip(stay), BF16)
    to_stay = swap(away[0], 1)
    away = exchange_rows(slab, fitted, owners, leave, BF16, more=from_core)
    arrived = [swap(x, bits) for x, bits in zip(away, (2, 4, 6))]
    (near,) = exchange_rows(slab, fitted, owners, stay, F32, more=to_stay)
    for x in arrived:
        near = near + x.astype(F32)
    total = near[0]
    for c, k in enumerate(far):
        if k:
            total = total + swap(near[c].astype(BF16), k).astype(F32)
    return total


def solution(mesh):
    placed = (
        P(("groups", "aux"), None, None),
        P(("groups", "aux"), None),
        P(("groups", "aux")),
        P("groups", None),
        P("groups", None),
    )
    return jax.shard_map(
        functools.partial(body, mesh.shape["aux"]),
        mesh=mesh, in_specs=placed, out_specs=P(("groups", "aux"), None), check_vma=False,
    )
```

```python
import functools

import jax
import jax.numpy as jnp
from jax import lax
from jax.experimental import pallas as pl
from jax.experimental.pallas import tpu as pltpu
from jax.sharding import PartitionSpec as P

UNROLL = 32
CHUNK = 32
TURNS = 3
FLIGHT = 4
F32 = jnp.float32
BF16 = jnp.bfloat16


def rank_slots(live, index_ref, rows, meta, nblk, nkeys, chunks, pump):
    slots = index_ref.shape[1]
    wide = rows.shape[1]
    never = float(chunks * nkeys)
    assert slots < 512 and nblk <= 32 and nkeys <= 512 and CHUNK % 8 == 0
    rows[...] = jnp.full(rows.shape, nkeys, F32)
    key = index_ref[0:1, :] * nblk + index_ref[1:2, :]
    slot = lax.broadcasted_iota(jnp.int32, (1, slots), 1)
    rows[0:1, 0:slots] = jnp.where(slot < live, key, nkeys).astype(F32)
    rows[1:2, 0:slots] = (slot * 32768 + index_ref[2:3, :] * 1024).astype(F32)
    row = rows[0:1, :]
    lives = row < nkeys
    tile = (8, wide)
    zero = jnp.zeros(tile, F32)
    lane = lax.broadcasted_iota(jnp.int32, tile, 1)
    ahead = lane - lax.broadcasted_iota(jnp.int32, tile, 0)

    every = jnp.broadcast_to(row, tile)
    columns = rows[...].T
    late = zero
    for s in range(0, slots, 8):
        late = jnp.where(columns[s : s + 8, 0:1] == every, float(s // CHUNK), late)
    late = jnp.max(late, axis=0, keepdims=True)
    pump()
    order = jnp.where(lives, late * nkeys + row, never)

    every = jnp.broadcast_to(order, tile)
    columns = every.T
    rank, place = zero, zero
    for s in range(0, slots, 8):
        column = columns[s : s + 8, 0:1]
        same = (column == every) & (ahead > s)
        rank = rank + jnp.where(same, 1.0, 0.0)
        place = place + jnp.where(same | (column < every), 1.0, 0.0)
    pump()
    rank = jnp.sum(rank, axis=0, keepdims=True)
    place = jnp.sum(place, axis=0, keepdims=True)
    end = jnp.max(jnp.where(lives, order, 0.0), axis=1, keepdims=True)
    last = jnp.max(jnp.where(lives & (order == end), row, 0.0), axis=1, keepdims=True)
    nothing = 2.0 * last + slots * 32768.0
    rows[1:2, :] = rows[1:2, :] + 2.0 * row + jnp.where(rank == 0.0, 1.0, 0.0) - nothing
    rows[2:3, :] = jnp.where(lives, place, -1.0)
    rows[3:4, :] = late - (chunks - 1)

    columns = rows[...].T
    spot = lane.astype(F32)
    number, need = zero, zero
    for s in range(0, slots, 8):
        found = columns[s : s + 8, 2:3] == spot
        number = number + jnp.where(found, columns[s : s + 8, 1:2], 0.0)
        need = need + jnp.where(found, columns[s : s + 8, 3:4], 0.0)
    meta[0:1, :] = (jnp.sum(number, axis=0, keepdims=True) + nothing).astype(jnp.int32)
    meta[1:2, :] = (jnp.sum(need, axis=0, keepdims=True) + (chunks - 1)).astype(jnp.int32)


def half_kernel(
    owners, q_dev, live_ref, index_hbm, blocks_hbm, orb_hbm, metric_hbm, slab, pairs_ref, split_ref,
    index_ref, held, orb_ref, metric_ref, orb_t, rows, meta, facts, in_sem, small_sem,
):
    slots, size, _ = blocks_hbm.shape
    occupied = orb_ref.shape[1]
    nblk = orb_ref.shape[0] // size
    nkeys = q_dev * nblk
    chunks = slots // CHUNK

    def fetch(c):
        part = pl.ds(c * CHUNK, CHUNK)
        return pltpu.make_async_copy(blocks_hbm.at[part], held.at[part], in_sem.at[c])

    def clear(first, last):
        @pl.loop(first, last, step=8)
        def _(k):
            for u in range(8):
                slab[k + u] = jnp.zeros((size, occupied), BF16)

    small = [
        pltpu.make_async_copy(source, target, small_sem.at[1 + k])
        for k, (source, target) in enumerate(
            [(index_hbm, index_ref), (orb_hbm, orb_ref), (metric_hbm, metric_ref)]
        )
    ]
    small[0].start()
    small[1].start()
    for c in range(min(FLIGHT, chunks)):
        fetch(c).start()
    came = [0]

    def pump():
        if came[0] + FLIGHT < chunks:
            fetch(came[0]).wait()
            fetch(came[0] + FLIGHT).start()
            came[0] += 1


    held[slots] = jnp.zeros((size, size), BF16)
    clear(0, nkeys // 2)

    small[0].wait()
    pump()
    rank_slots(live_ref[0], index_ref, rows, meta, nblk, nkeys, chunks, pump)
    pump()
    copy = pltpu.make_async_copy(meta, facts, small_sem.at[0])
    copy.start()

    clear(nkeys // 2, 3 * nkeys // 4)
    pump()
    clear(3 * nkeys // 4, nkeys)
    while came[0] + FLIGHT < chunks:
        pump()
    small[2].start()
    small[1].wait()
    copy.wait()

    def arrive(c, nothing):
        fetch(c).wait()
        return nothing

    def turn(b):
        part = pl.ds(pl.multiple_of(b * size, size), size)
        orb_t[:, part] = orb_ref[part, :].T

    def step(g, carry):
        arrived, total = carry
        needed = jnp.maximum(arrived, facts[1, g * UNROLL + UNROLL - 1] + 1)
        lax.fori_loop(arrived, needed, arrive, 0)
        for u in range(TURNS):
            turn(jnp.minimum(g * TURNS + u, nblk - 1))
        empty = jnp.zeros((size, occupied), BF16)
        for u in range(0, UNROLL, 2):
            pair = [facts[0, g * UNROLL + u + w] for w in range(2)]
            orbs = [orb_ref[pl.ds(pl.multiple_of(((v >> 10) & 31) * size, size), size), :] for v in pair]
            diagonal = jnp.concatenate(
                [jnp.concatenate([orbs[0], empty], axis=1), jnp.concatenate([empty, orbs[1]], axis=1)], axis=0
            )
            blocks = jnp.concatenate([held[v >> 15] for v in pair], axis=1)
            products = jnp.dot(blocks, diagonal, preferred_element_type=F32)
            for w, v in enumerate(pair):
                product = products[:, w * occupied : (w + 1) * occupied]
                total = jnp.where((v & 1) == 1, product, total + product)
                slab[(v & 1023) >> 1] = total.astype(BF16)
        return needed, total

    bodies = (live_ref[0] + UNROLL - 1) // UNROLL
    arrived, _ = lax.fori_loop(0, bodies, step, (jnp.int32(came[0]), jnp.zeros((size, occupied), F32)))
    lax.fori_loop(arrived, chunks, arrive, 0)

    @pl.loop(jnp.minimum(bodies * TURNS, nblk), nblk)
    def _(b):
        turn(b)

    small[2].wait()
    metric = metric_ref[...]
    high = metric.astype(BF16)
    naux = metric.shape[0]
    split_ref[0:naux, :] = high
    split_ref[naux : 2 * naux, :] = (metric - high.astype(F32)).astype(BF16)

    @pl.loop(0, q_dev // 2, unroll=8)
    def _(t):
        block = jnp.concatenate(
            [slab[pl.ds((2 * t + u) * nblk, nblk)].reshape(nblk * size, occupied) for u in range(2)], axis=1
        )
        total = jnp.dot(orb_t[...], block, preferred_element_type=F32)
        for u in range(2):
            pair = total[:, u * occupied : (u + 1) * occupied].T
            if owners:
                pairs_ref[:, 2 * t + u] = pair.reshape(owners, occupied // owners, occupied).astype(BF16)
            else:
                pairs_ref[2 * t + u] = pair.astype(BF16)


def half_transform(blocks, index, live, orbitals, metric, q_dev, owners):
    slots, size, _ = blocks.shape
    basis, occupied = orbitals.shape
    nblk = basis // size
    split = (occupied // owners) % 8 == 0
    pairs_shape = (owners, q_dev, occupied // owners, occupied) if split else (q_dev, occupied, occupied)
    wide = -(-(slots + UNROLL) // 128) * 128
    slab, pairs, metric_split = pl.pallas_call(
        functools.partial(half_kernel, owners if split else 0, q_dev),
        out_shape=(
            pltpu.VMEM((q_dev * nblk, size, occupied), BF16),
            jax.ShapeDtypeStruct(pairs_shape, BF16),
            pltpu.VMEM((2 * metric.shape[0], metric.shape[1]), BF16),
        ),
        in_specs=[pl.BlockSpec(memory_space=pltpu.SMEM)] + [pl.BlockSpec(memory_space=pl.ANY)] * 4,
        out_specs=(pl.BlockSpec(memory_space=pltpu.VMEM),) * 3,
        scratch_shapes=[
            pltpu.VMEM(index.shape, jnp.int32),
            pltpu.VMEM((slots + 1, size, size), BF16),
            pltpu.VMEM((basis, occupied), BF16),
            pltpu.VMEM(metric.shape, F32),
            pltpu.VMEM((occupied, basis), BF16),
            pltpu.VMEM((8, wide), F32),
            pltpu.VMEM((8, wide), jnp.int32),
            pltpu.SMEM((8, wide), jnp.int32),
            pltpu.SemaphoreType.DMA((slots // CHUNK,)),
            pltpu.SemaphoreType.DMA((4,)),
        ],
        compiler_params=pltpu.CompilerParams(vmem_limit_bytes=36 * 2**20),
        cost_estimate=pl.CostEstimate(
            flops=2 * slots * size * size * occupied + 2 * q_dev * basis * occupied * occupied,
            bytes_accessed=2 * slots * size * size + 2 * q_dev * basis * occupied,
            transcendentals=0,
        ),
        name="half_transform_pairs",
    )(live, *(pltpu.with_memory_space_constraint(x, pltpu.HBM) for x in (index, blocks, orbitals, metric)))
    if not split:
        pairs = pairs.reshape(q_dev, owners, occupied // owners, occupied).transpose(1, 0, 2, 3)
    return slab.reshape(q_dev, basis, occupied), pairs, metric_split


def metric_kernel(split_ref, held_ref, out_ref, spread, mixed):
    naux, each, occupied = held_ref.shape
    spread[...] = held_ref[...].astype(F32).reshape(naux * each, occupied)
    for r in range(0, each, 2):
        both = [spread[pl.ds(r + u, naux, stride=each), :].astype(BF16) for u in range(2)]
        parts = jnp.dot(split_ref[...], jnp.concatenate(both, axis=1), preferred_element_type=F32)
        fitted = parts[:naux] + parts[naux:]
        for u in range(2):
            mixed[pl.ds(r + u, naux, stride=each), :] = fitted[:, u * occupied : (u + 1) * occupied]
    out_ref[...] = mixed[...].reshape(naux, each, occupied).astype(BF16)


def apply_metric(metric, metric_split, held):
    naux, each, occupied = held.shape
    if each % 8:
        fitted = jnp.einsum("qp,pij->qij", metric, held.astype(F32), precision=lax.Precision.HIGHEST)
        return fitted.astype(BF16)
    return pl.pallas_call(
        metric_kernel,
        out_shape=jax.ShapeDtypeStruct(held.shape, BF16),
        in_specs=[pl.BlockSpec(memory_space=pltpu.VMEM)] * 2,
        out_specs=pl.BlockSpec(memory_space=pltpu.VMEM),
        scratch_shapes=[pltpu.VMEM((naux * each, occupied), F32)] * 2,
        compiler_params=pltpu.CompilerParams(vmem_limit_bytes=12 * 2**20),
        cost_estimate=pl.CostEstimate(
            flops=4 * naux * naux * each * occupied, bytes_accessed=4 * naux * each * occupied, transcendentals=0
        ),
        name="apply_metric",
    )(pltpu.with_memory_space_constraint(metric_split, pltpu.VMEM), held)


def gather_fitted(fitted_ref, fitted):
    q_dev = fitted.shape[0] // fitted.shape[1]
    occupied = fitted.shape[1]
    for q in range(q_dev):
        if len(fitted_ref.shape) == 4:
            block = fitted_ref[:, q].astype(F32).reshape(occupied, occupied).astype(BF16)
        else:
            block = fitted_ref[q]
        fitted[q * occupied : (q + 1) * occupied, :] = block


def exchange_kernel(blocks, gather, more, slab, fitted_ref, *refs):
    refs = list(refs)
    more_ref = refs.pop(0) if more else None
    out_refs = [refs.pop(0) for _ in blocks]
    if gather:
        fitted = refs.pop(0)
        gather_fitted(fitted_ref, fitted)
    else:
        fitted = fitted_ref
    q_dev = slab.shape[0]
    each = out_refs[0].shape[1]
    me = lax.axis_index("aux").astype(jnp.int32)
    todo = [(k, c, h) for c, part in enumerate(blocks) for h, k in enumerate(part)]
    together = next(n for n in (4, 3, 2, 1) if len(todo) % n == 0)
    for g in range(0, len(todo), together):
        rows = [pl.ds(pl.multiple_of((me ^ k) * each, each), each) for k, _, _ in todo[g : g + together]]
        every = jnp.concatenate(
            [jnp.concatenate([slab[q, r, :] for r in rows], axis=0) for q in range(q_dev)], axis=1
        )
        sums = jnp.dot(every, fitted[...], preferred_element_type=F32)
        for u, (_, c, h) in enumerate(todo[g : g + together]):
            part = sums[u * each : (u + 1) * each]
            if more:
                part = part + more_ref[g + u].astype(F32)
            out_refs[c][h] = part.astype(out_refs[c].dtype)


def exchange_rows(slab, fitted, owners, blocks, dtype, gather=False, more=None):
    q_dev, basis, occupied = slab.shape
    each = basis // owners
    count = sum(len(part) for part in blocks)
    out = [jax.ShapeDtypeStruct((len(part), each, occupied), dtype) for part in blocks]
    if gather:
        out.append(jax.ShapeDtypeStruct((q_dev * occupied, occupied), BF16))
    operands = [pltpu.with_memory_space_constraint(slab, pltpu.VMEM), fitted] + ([] if more is None else [more])
    return pl.pallas_call(
        functools.partial(exchange_kernel, blocks, gather, more is not None),
        out_shape=out,
        in_specs=[pl.BlockSpec(memory_space=pltpu.VMEM)] * len(operands),
        out_specs=[pl.BlockSpec(memory_space=pltpu.VMEM)] * len(out),
        compiler_params=pltpu.CompilerParams(vmem_limit_bytes=24 * 2**20),
        cost_estimate=pl.CostEstimate(
            flops=2 * q_dev * occupied * count * each * occupied,
            bytes_accessed=2 * q_dev * occupied * count * each,
            transcendentals=0,
        ),
        name="exchange_rows",
    )(*operands)


def body(owners, integrals, block_index, live_count, orbitals, metric):
    basis, occupied = orbitals.shape
    naux = metric.shape[1]
    q_dev = naux // owners

    slab, pairs, metric_split = half_transform(integrals, block_index.T, live_count, orbitals, metric, q_dev, owners)

    trade = functools.partial(lax.all_to_all, axis_name="aux", split_axis=0, concat_axis=0, tiled=True)
    held = trade(pairs).reshape(naux, occupied // owners, occupied)
    fitted = apply_metric(metric, metric_split, held)
    fitted = trade(fitted.reshape(owners, q_dev, occupied // owners, occupied))
    if (occupied // owners) % 8:
        fitted = fitted.transpose(1, 0, 2, 3).reshape(q_dev, occupied, occupied)

    def swap(x, bits):
        return lax.ppermute(x, "aux", [(d, d ^ bits) for d in range(owners)])

    far = range(0, owners, 8)
    leave = [tuple(x + k for k in far) for x in (2, 4, 6)]
    stay = [tuple(far)]
    flip = lambda parts: [tuple(k ^ 1 for k in part) for part in parts]
    *away, fitted = exchange_rows(slab, fitted, owners, flip([sum(leave, ())]), BF16, gather=True)
    from_core = swap(away[0], 1)
    away = exchange_rows(slab, fitted, owners, flip(stay), BF16)
    to_stay = swap(away[0], 1)
    away = exchange_rows(slab, fitted, owners, leave, BF16, more=from_core)
    arrived = [swap(x, bits) for x, bits in zip(away, (2, 4, 6))]
    (near,) = exchange_rows(slab, fitted, owners, stay, F32, more=to_stay)
    for x in arrived:
        near = near + x.astype(F32)
    total = near[0]
    for c, k in enumerate(far):
        if k:
            total = total + swap(near[c].astype(BF16), k).astype(F32)
    return total


def solution(mesh):
    placed = (
        P(("groups", "aux"), None, None),
        P(("groups", "aux"), None),
        P(("groups", "aux")),
        P("groups", None),
        P("groups", None),
    )
    return jax.shard_map(
        functools.partial(body, mesh.shape["aux"]),
        mesh=mesh, in_specs=placed, out_specs=P(("groups", "aux"), None), check_vma=False,
    )
```

```python
import functools

import jax
import jax.numpy as jnp
from jax import lax
from jax.experimental import pallas as pl
from jax.experimental.pallas import tpu as pltpu
from jax.sharding import PartitionSpec as P

UNROLL = 64
CHUNK = 32
TURNS = 5
FLIGHT = 4
F32 = jnp.float32
BF16 = jnp.bfloat16


def rank_slots(live, index_ref, rows, meta, nblk, nkeys, chunks, pump):
    slots = index_ref.shape[1]
    wide = rows.shape[1]
    never = float(chunks * nkeys)
    assert slots < 512 and nblk <= 32 and nkeys <= 512 and CHUNK % 8 == 0
    rows[...] = jnp.full(rows.shape, nkeys, F32)
    key = index_ref[0:1, :] * nblk + index_ref[1:2, :]
    slot = lax.broadcasted_iota(jnp.int32, (1, slots), 1)
    rows[0:1, 0:slots] = jnp.where(slot < live, key, nkeys).astype(F32)
    rows[1:2, 0:slots] = (slot * 32768 + index_ref[2:3, :] * 1024).astype(F32)
    row = rows[0:1, :]
    lives = row < nkeys
    tile = (8, wide)
    zero = jnp.zeros(tile, F32)
    lane = lax.broadcasted_iota(jnp.int32, tile, 1)
    ahead = lane - lax.broadcasted_iota(jnp.int32, tile, 0)

    every = jnp.broadcast_to(row, tile)
    columns = rows[...].T
    late = zero
    for s in range(0, slots, 8):
        late = jnp.where(columns[s : s + 8, 0:1] == every, float(s // CHUNK), late)
    late = jnp.max(late, axis=0, keepdims=True)
    pump()
    order = jnp.where(lives, late * nkeys + row, never)

    every = jnp.broadcast_to(order, tile)
    columns = every.T
    rank, place = zero, zero
    for s in range(0, slots, 8):
        column = columns[s : s + 8, 0:1]
        same = (column == every) & (ahead > s)
        rank = rank + jnp.where(same, 1.0, 0.0)
        place = place + jnp.where(same | (column < every), 1.0, 0.0)
    pump()
    rank = jnp.sum(rank, axis=0, keepdims=True)
    place = jnp.sum(place, axis=0, keepdims=True)
    end = jnp.max(jnp.where(lives, order, 0.0), axis=1, keepdims=True)
    last = jnp.max(jnp.where(lives & (order == end), row, 0.0), axis=1, keepdims=True)
    nothing = 2.0 * last + slots * 32768.0
    rows[1:2, :] = rows[1:2, :] + 2.0 * row + jnp.where(rank == 0.0, 1.0, 0.0) - nothing
    rows[2:3, :] = jnp.where(lives, place, -1.0)
    rows[3:4, :] = late - (chunks - 1)

    columns = rows[...].T
    spot = lane.astype(F32)
    number, need = zero, zero
    for s in range(0, slots, 8):
        found = columns[s : s + 8, 2:3] == spot
        number = number + jnp.where(found, columns[s : s + 8, 1:2], 0.0)
        need = need + jnp.where(found, columns[s : s + 8, 3:4], 0.0)
    meta[0:1, :] = (jnp.sum(number, axis=0, keepdims=True) + nothing).astype(jnp.int32)
    meta[1:2, :] = (jnp.sum(need, axis=0, keepdims=True) + (chunks - 1)).astype(jnp.int32)


def half_kernel(
    owners, q_dev, live_ref, index_hbm, blocks_hbm, orb_hbm, metric_hbm, slab, pairs_ref, split_ref,
    index_ref, held, orb_ref, metric_ref, orb_t, rows, meta, facts, in_sem, small_sem,
):
    slots, size, _ = blocks_hbm.shape
    occupied = orb_ref.shape[1]
    nblk = orb_ref.shape[0] // size
    nkeys = q_dev * nblk
    chunks = slots // CHUNK

    def fetch(c):
        part = pl.ds(c * CHUNK, CHUNK)
        return pltpu.make_async_copy(blocks_hbm.at[part], held.at[part], in_sem.at[c])

    def clear(first, last):
        @pl.loop(first, last, step=8)
        def _(k):
            for u in range(8):
                slab[k + u] = jnp.zeros((size, occupied), BF16)

    small = [
        pltpu.make_async_copy(source, target, small_sem.at[1 + k])
        for k, (source, target) in enumerate(
            [(index_hbm, index_ref), (orb_hbm, orb_ref), (metric_hbm, metric_ref)]
        )
    ]
    small[0].start()
    small[1].start()
    for c in range(min(FLIGHT, chunks)):
        fetch(c).start()
    came = [0]

    def pump():
        if came[0] + FLIGHT < chunks:
            fetch(came[0]).wait()
            fetch(came[0] + FLIGHT).start()
            came[0] += 1


    held[slots] = jnp.zeros((size, size), BF16)
    clear(0, nkeys // 2)

    small[0].wait()
    pump()
    rank_slots(live_ref[0], index_ref, rows, meta, nblk, nkeys, chunks, pump)
    pump()
    copy = pltpu.make_async_copy(meta, facts, small_sem.at[0])
    copy.start()

    clear(nkeys // 2, 3 * nkeys // 4)
    pump()
    clear(3 * nkeys // 4, nkeys)
    while came[0] + FLIGHT < chunks:
        pump()
    small[2].start()
    small[1].wait()
    copy.wait()

    def arrive(c, nothing):
        fetch(c).wait()
        return nothing

    def turn(b):
        part = pl.ds(pl.multiple_of(b * size, size), size)
        orb_t[:, part] = orb_ref[part, :].T

    def step(g, carry):
        arrived, total = carry
        needed = jnp.maximum(arrived, facts[1, g * UNROLL + UNROLL - 1] + 1)
        lax.fori_loop(arrived, needed, arrive, 0)
        for u in range(TURNS):
            turn(jnp.minimum(g * TURNS + u, nblk - 1))
        empty = jnp.zeros((size, occupied), BF16)
        for u in range(0, UNROLL, 2):
            pair = [facts[0, g * UNROLL + u + w] for w in range(2)]
            orbs = [orb_ref[pl.ds(pl.multiple_of(((v >> 10) & 31) * size, size), size), :] for v in pair]
            diagonal = jnp.concatenate(
                [jnp.concatenate([orbs[0], empty], axis=1), jnp.concatenate([empty, orbs[1]], axis=1)], axis=0
            )
            blocks = jnp.concatenate([held[v >> 15] for v in pair], axis=1)
            products = jnp.dot(blocks, diagonal, preferred_element_type=F32)
            for w, v in enumerate(pair):
                product = products[:, w * occupied : (w + 1) * occupied]
                total = jnp.where((v & 1) == 1, product, total + product)
                slab[(v & 1023) >> 1] = total.astype(BF16)
        return needed, total

    bodies = (live_ref[0] + UNROLL - 1) // UNROLL
    arrived, _ = lax.fori_loop(0, bodies, step, (jnp.int32(came[0]), jnp.zeros((size, occupied), F32)))
    lax.fori_loop(arrived, chunks, arrive, 0)

    @pl.loop(jnp.minimum(bodies * TURNS, nblk), nblk)
    def _(b):
        turn(b)

    small[2].wait()
    metric = metric_ref[...]
    high = metric.astype(BF16)
    naux = metric.shape[0]
    split_ref[0:naux, :] = high
    split_ref[naux : 2 * naux, :] = (metric - high.astype(F32)).astype(BF16)

    @pl.loop(0, q_dev // 2, unroll=8)
    def _(t):
        block = jnp.concatenate(
            [slab[pl.ds((2 * t + u) * nblk, nblk)].reshape(nblk * size, occupied) for u in range(2)], axis=1
        )
        total = jnp.dot(orb_t[...], block, preferred_element_type=F32)
        for u in range(2):
            pair = total[:, u * occupied : (u + 1) * occupied].T
            if owners:
                pairs_ref[:, 2 * t + u] = pair.reshape(owners, occupied // owners, occupied).astype(BF16)
            else:
                pairs_ref[2 * t + u] = pair.astype(BF16)


def half_transform(blocks, index, live, orbitals, metric, q_dev, owners):
    slots, size, _ = blocks.shape
    basis, occupied = orbitals.shape
    nblk = basis // size
    split = (occupied // owners) % 8 == 0
    pairs_shape = (owners, q_dev, occupied // owners, occupied) if split else (q_dev, occupied, occupied)
    wide = -(-(slots + UNROLL) // 128) * 128
    slab, pairs, metric_split = pl.pallas_call(
        functools.partial(half_kernel, owners if split else 0, q_dev),
        out_shape=(
            pltpu.VMEM((q_dev * nblk, size, occupied), BF16),
            jax.ShapeDtypeStruct(pairs_shape, BF16),
            pltpu.VMEM((2 * metric.shape[0], metric.shape[1]), BF16),
        ),
        in_specs=[pl.BlockSpec(memory_space=pltpu.SMEM)] + [pl.BlockSpec(memory_space=pl.ANY)] * 4,
        out_specs=(pl.BlockSpec(memory_space=pltpu.VMEM),) * 3,
        scratch_shapes=[
            pltpu.VMEM(index.shape, jnp.int32),
            pltpu.VMEM((slots + 1, size, size), BF16),
            pltpu.VMEM((basis, occupied), BF16),
            pltpu.VMEM(metric.shape, F32),
            pltpu.VMEM((occupied, basis), BF16),
            pltpu.VMEM((8, wide), F32),
            pltpu.VMEM((8, wide), jnp.int32),
            pltpu.SMEM((8, wide), jnp.int32),
            pltpu.SemaphoreType.DMA((slots // CHUNK,)),
            pltpu.SemaphoreType.DMA((4,)),
        ],
        compiler_params=pltpu.CompilerParams(vmem_limit_bytes=36 * 2**20),
        cost_estimate=pl.CostEstimate(
            flops=2 * slots * size * size * occupied + 2 * q_dev * basis * occupied * occupied,
            bytes_accessed=2 * slots * size * size + 2 * q_dev * basis * occupied,
            transcendentals=0,
        ),
        name="half_transform_pairs",
    )(live, *(pltpu.with_memory_space_constraint(x, pltpu.HBM) for x in (index, blocks, orbitals, metric)))
    if not split:
        pairs = pairs.reshape(q_dev, owners, occupied // owners, occupied).transpose(1, 0, 2, 3)
    return slab.reshape(q_dev, basis, occupied), pairs, metric_split


def metric_kernel(split_ref, held_ref, out_ref, spread, mixed):
    naux, each, occupied = held_ref.shape
    spread[...] = held_ref[...].astype(F32).reshape(naux * each, occupied)
    for r in range(0, each, 2):
        both = [spread[pl.ds(r + u, naux, stride=each), :].astype(BF16) for u in range(2)]
        parts = jnp.dot(split_ref[...], jnp.concatenate(both, axis=1), preferred_element_type=F32)
        fitted = parts[:naux] + parts[naux:]
        for u in range(2):
            mixed[pl.ds(r + u, naux, stride=each), :] = fitted[:, u * occupied : (u + 1) * occupied]
    out_ref[...] = mixed[...].reshape(naux, each, occupied).astype(BF16)


def apply_metric(metric, metric_split, held):
    naux, each, occupied = held.shape
    if each % 8:
        fitted = jnp.einsum("qp,pij->qij", metric, held.astype(F32), precision=lax.Precision.HIGHEST)
        return fitted.astype(BF16)
    return pl.pallas_call(
        metric_kernel,
        out_shape=jax.ShapeDtypeStruct(held.shape, BF16),
        in_specs=[pl.BlockSpec(memory_space=pltpu.VMEM)] * 2,
        out_specs=pl.BlockSpec(memory_space=pltpu.VMEM),
        scratch_shapes=[pltpu.VMEM((naux * each, occupied), F32)] * 2,
        compiler_params=pltpu.CompilerParams(vmem_limit_bytes=12 * 2**20),
        cost_estimate=pl.CostEstimate(
            flops=4 * naux * naux * each * occupied, bytes_accessed=4 * naux * each * occupied, transcendentals=0
        ),
        name="apply_metric",
    )(pltpu.with_memory_space_constraint(metric_split, pltpu.VMEM), held)


def gather_fitted(fitted_ref, fitted):
    q_dev = fitted.shape[0] // fitted.shape[1]
    occupied = fitted.shape[1]
    for q in range(q_dev):
        if len(fitted_ref.shape) == 4:
            block = fitted_ref[:, q].astype(F32).reshape(occupied, occupied).astype(BF16)
        else:
            block = fitted_ref[q]
        fitted[q * occupied : (q + 1) * occupied, :] = block


def exchange_kernel(blocks, gather, more, slab, fitted_ref, *refs):
    refs = list(refs)
    more_ref = refs.pop(0) if more else None
    out_refs = [refs.pop(0) for _ in blocks]
    if gather:
        fitted = refs.pop(0)
        gather_fitted(fitted_ref, fitted)
    else:
        fitted = fitted_ref
    q_dev = slab.shape[0]
    each = out_refs[0].shape[1]
    me = lax.axis_index("aux").astype(jnp.int32)
    todo = [(k, c, h) for c, part in enumerate(blocks) for h, k in enumerate(part)]
    together = next(n for n in (4, 3, 2, 1) if len(todo) % n == 0)
    for g in range(0, len(todo), together):
        rows = [pl.ds(pl.multiple_of((me ^ k) * each, each), each) for k, _, _ in todo[g : g + together]]
        every = jnp.concatenate(
            [jnp.concatenate([slab[q, r, :] for r in rows], axis=0) for q in range(q_dev)], axis=1
        )
        sums = jnp.dot(every, fitted[...], preferred_element_type=F32)
        for u, (_, c, h) in enumerate(todo[g : g + together]):
            part = sums[u * each : (u + 1) * each]
            if more:
                part = part + more_ref[g + u].astype(F32)
            out_refs[c][h] = part.astype(out_refs[c].dtype)


def exchange_rows(slab, fitted, owners, blocks, dtype, gather=False, more=None):
    q_dev, basis, occupied = slab.shape
    each = basis // owners
    count = sum(len(part) for part in blocks)
    out = [jax.ShapeDtypeStruct((len(part), each, occupied), dtype) for part in blocks]
    if gather:
        out.append(jax.ShapeDtypeStruct((q_dev * occupied, occupied), BF16))
    operands = [pltpu.with_memory_space_constraint(slab, pltpu.VMEM), fitted] + ([] if more is None else [more])
    return pl.pallas_call(
        functools.partial(exchange_kernel, blocks, gather, more is not None),
        out_shape=out,
        in_specs=[pl.BlockSpec(memory_space=pltpu.VMEM)] * len(operands),
        out_specs=[pl.BlockSpec(memory_space=pltpu.VMEM)] * len(out),
        compiler_params=pltpu.CompilerParams(vmem_limit_bytes=24 * 2**20),
        cost_estimate=pl.CostEstimate(
            flops=2 * q_dev * occupied * count * each * occupied,
            bytes_accessed=2 * q_dev * occupied * count * each,
            transcendentals=0,
        ),
        name="exchange_rows",
    )(*operands)


def body(owners, integrals, block_index, live_count, orbitals, metric):
    basis, occupied = orbitals.shape
    naux = metric.shape[1]
    q_dev = naux // owners

    slab, pairs, metric_split = half_transform(integrals, block_index.T, live_count, orbitals, metric, q_dev, owners)

    trade = functools.partial(lax.all_to_all, axis_name="aux", split_axis=0, concat_axis=0, tiled=True)
    held = trade(pairs).reshape(naux, occupied // owners, occupied)
    fitted = apply_metric(metric, metric_split, held)
    fitted = trade(fitted.reshape(owners, q_dev, occupied // owners, occupied))
    if (occupied // owners) % 8:
        fitted = fitted.transpose(1, 0, 2, 3).reshape(q_dev, occupied, occupied)

    def swap(x, bits):
        return lax.ppermute(x, "aux", [(d, d ^ bits) for d in range(owners)])

    far = range(0, owners, 8)
    leave = [tuple(x + k for k in far) for x in (2, 4, 6)]
    stay = [tuple(far)]
    flip = lambda parts: [tuple(k ^ 1 for k in part) for part in parts]
    *away, fitted = exchange_rows(slab, fitted, owners, flip([sum(leave, ())]), BF16, gather=True)
    from_core = swap(away[0], 1)
    away = exchange_rows(slab, fitted, owners, flip(stay), BF16)
    to_stay = swap(away[0], 1)
    away = exchange_rows(slab, fitted, owners, leave, BF16, more=from_core)
    arrived = [swap(x, bits) for x, bits in zip(away, (2, 4, 6))]
    (near,) = exchange_rows(slab, fitted, owners, stay, F32, more=to_stay)
    for x in arrived:
        near = near + x.astype(F32)
    total = near[0]
    for c, k in enumerate(far):
        if k:
            total = total + swap(near[c].astype(BF16), k).astype(F32)
    return total


def solution(mesh):
    placed = (
        P(("groups", "aux"), None, None),
        P(("groups", "aux"), None),
        P(("groups", "aux")),
        P("groups", None),
        P("groups", None),
    )
    return jax.shard_map(
        functools.partial(body, mesh.shape["aux"]),
        mesh=mesh, in_specs=placed, out_specs=P(("groups", "aux"), None), check_vma=False,
    )
```

```python
import functools

import jax
import jax.numpy as jnp
from jax import lax
from jax.experimental import pallas as pl
from jax.experimental.pallas import tpu as pltpu
from jax.sharding import PartitionSpec as P

UNROLL = 64
CHUNK = 32
TURNS = 5
FLIGHT = 4
F32 = jnp.float32
BF16 = jnp.bfloat16


def rank_slots(live, index_ref, rows, meta, nblk, nkeys, chunks, pump):
    slots = index_ref.shape[1]
    wide = rows.shape[1]
    never = float(chunks * nkeys)
    assert slots < 512 and nblk <= 32 and nkeys <= 512 and CHUNK % 8 == 0
    rows[...] = jnp.full(rows.shape, nkeys, F32)
    key = index_ref[0:1, :] * nblk + index_ref[1:2, :]
    slot = lax.broadcasted_iota(jnp.int32, (1, slots), 1)
    rows[0:1, 0:slots] = jnp.where(slot < live, key, nkeys).astype(F32)
    rows[1:2, 0:slots] = (slot * 32768 + index_ref[2:3, :] * 1024).astype(F32)
    row = rows[0:1, :]
    lives = row < nkeys
    tile = (8, wide)
    zero = jnp.zeros(tile, F32)
    lane = lax.broadcasted_iota(jnp.int32, tile, 1)
    ahead = lane - lax.broadcasted_iota(jnp.int32, tile, 0)

    every = jnp.broadcast_to(row, tile)
    columns = rows[...].T
    late = zero
    for s in range(0, slots, 8):
        late = jnp.where(columns[s : s + 8, 0:1] == every, float(s // CHUNK), late)
    late = jnp.max(late, axis=0, keepdims=True)
    pump()
    order = jnp.where(lives, late * nkeys + row, never)

    every = jnp.broadcast_to(order, tile)
    columns = every.T
    rank, place = zero, zero
    for s in range(0, slots, 8):
        column = columns[s : s + 8, 0:1]
        same = (column == every) & (ahead > s)
        rank = rank + jnp.where(same, 1.0, 0.0)
        place = place + jnp.where(same | (column < every), 1.0, 0.0)
    pump()
    rank = jnp.sum(rank, axis=0, keepdims=True)
    place = jnp.sum(place, axis=0, keepdims=True)
    end = jnp.max(jnp.where(lives, order, 0.0), axis=1, keepdims=True)
    last = jnp.max(jnp.where(lives & (order == end), row, 0.0), axis=1, keepdims=True)
    nothing = 2.0 * last + slots * 32768.0
    rows[1:2, :] = rows[1:2, :] + 2.0 * row + jnp.where(rank == 0.0, 1.0, 0.0) - nothing
    rows[2:3, :] = jnp.where(lives, place, -1.0)
    rows[3:4, :] = late - (chunks - 1)

    columns = rows[...].T
    spot = lane.astype(F32)
    number, need = zero, zero
    for s in range(0, slots, 8):
        found = columns[s : s + 8, 2:3] == spot
        number = number + jnp.where(found, columns[s : s + 8, 1:2], 0.0)
        need = need + jnp.where(found, columns[s : s + 8, 3:4], 0.0)
    meta[0:1, :] = (jnp.sum(number, axis=0, keepdims=True) + nothing).astype(jnp.int32)
    meta[1:2, :] = (jnp.sum(need, axis=0, keepdims=True) + (chunks - 1)).astype(jnp.int32)


def half_kernel(
    owners, q_dev, live_ref, index_hbm, blocks_hbm, orb_hbm, metric_hbm, slab, pairs_ref, split_ref,
    index_ref, held, orb_ref, metric_ref, orb_t, rows, meta, facts, in_sem, small_sem,
):
    slots, size, _ = blocks_hbm.shape
    occupied = orb_ref.shape[1]
    nblk = orb_ref.shape[0] // size
    nkeys = q_dev * nblk
    chunks = slots // CHUNK

    def fetch(c):
        part = pl.ds(c * CHUNK, CHUNK)
        return pltpu.make_async_copy(blocks_hbm.at[part], held.at[part], in_sem.at[c])

    def clear(first, last):
        @pl.loop(first, last, step=8)
        def _(k):
            for u in range(8):
                slab[k + u] = jnp.zeros((size, occupied), BF16)

    small = [
        pltpu.make_async_copy(source, target, small_sem.at[1 + k])
        for k, (source, target) in enumerate(
            [(index_hbm, index_ref), (orb_hbm, orb_ref), (metric_hbm, metric_ref)]
        )
    ]
    small[0].start()
    small[1].start()
    for c in range(min(FLIGHT, chunks)):
        fetch(c).start()
    came = [0]

    def pump():
        if came[0] + FLIGHT < chunks:
            fetch(came[0]).wait()
            fetch(came[0] + FLIGHT).start()
            came[0] += 1


    held[slots] = jnp.zeros((size, size), BF16)
    clear(0, nkeys // 2)

    small[0].wait()
    pump()
    rank_slots(live_ref[0], index_ref, rows, meta, nblk, nkeys, chunks, pump)
    pump()
    copy = pltpu.make_async_copy(meta, facts, small_sem.at[0])
    copy.start()

    clear(nkeys // 2, 3 * nkeys // 4)
    pump()
    clear(3 * nkeys // 4, nkeys)
    while came[0] + FLIGHT < chunks:
        pump()
    small[2].start()
    small[1].wait()
    copy.wait()

    def arrive(c, nothing):
        fetch(c).wait()
        return nothing

    def turn(b):
        part = pl.ds(pl.multiple_of(b * size, size), size)
        orb_t[:, part] = orb_ref[part, :].T

    def step(g, carry):
        arrived, total = carry
        needed = jnp.maximum(arrived, facts[1, g * UNROLL + UNROLL - 1] + 1)
        lax.fori_loop(arrived, needed, arrive, 0)
        for u in range(TURNS):
            turn(jnp.minimum(g * TURNS + u, nblk - 1))
        empty = jnp.zeros((size, occupied), BF16)
        for u in range(0, UNROLL, 2):
            pair = [facts[0, g * UNROLL + u + w] for w in range(2)]
            orbs = [orb_ref[pl.ds(pl.multiple_of(((v >> 10) & 31) * size, size), size), :] for v in pair]
            diagonal = jnp.concatenate(
                [jnp.concatenate([orbs[0], empty], axis=1), jnp.concatenate([empty, orbs[1]], axis=1)], axis=0
            )
            blocks = jnp.concatenate([held[v >> 15] for v in pair], axis=1)
            products = jnp.dot(blocks, diagonal, preferred_element_type=F32)
            for w, v in enumerate(pair):
                product = products[:, w * occupied : (w + 1) * occupied]
                total = jnp.where((v & 1) == 1, product, total + product)
                slab[(v & 1023) >> 1] = total.astype(BF16)
        return needed, total

    bodies = (live_ref[0] + UNROLL - 1) // UNROLL
    arrived, _ = lax.fori_loop(0, bodies, step, (jnp.int32(came[0]), jnp.zeros((size, occupied), F32)))
    lax.fori_loop(arrived, chunks, arrive, 0)

    @pl.loop(jnp.minimum(bodies * TURNS, nblk), nblk)
    def _(b):
        turn(b)

    small[2].wait()
    metric = metric_ref[...]
    high = metric.astype(BF16)
    naux = metric.shape[0]
    split_ref[0:naux, :] = high
    split_ref[naux : 2 * naux, :] = (metric - high.astype(F32)).astype(BF16)

    @pl.loop(0, q_dev // 2, unroll=8)
    def _(t):
        block = jnp.concatenate(
            [slab[pl.ds((2 * t + u) * nblk, nblk)].reshape(nblk * size, occupied) for u in range(2)], axis=1
        )
        total = jnp.dot(orb_t[...], block, preferred_element_type=F32)
        for u in range(2):
            pair = total[:, u * occupied : (u + 1) * occupied].T
            if owners:
                pairs_ref[:, 2 * t + u] = pair.reshape(owners, occupied // owners, occupied).astype(BF16)
            else:
                pairs_ref[2 * t + u] = pair.astype(BF16)


def half_transform(blocks, index, live, orbitals, metric, q_dev, owners):
    slots, size, _ = blocks.shape
    basis, occupied = orbitals.shape
    nblk = basis // size
    split = (occupied // owners) % 8 == 0
    pairs_shape = (owners, q_dev, occupied // owners, occupied) if split else (q_dev, occupied, occupied)
    wide = -(-(slots + UNROLL) // 128) * 128
    slab, pairs, metric_split = pl.pallas_call(
        functools.partial(half_kernel, owners if split else 0, q_dev),
        out_shape=(
            pltpu.VMEM((q_dev * nblk, size, occupied), BF16),
            jax.ShapeDtypeStruct(pairs_shape, BF16),
            pltpu.VMEM((2 * metric.shape[0], metric.shape[1]), BF16),
        ),
        in_specs=[pl.BlockSpec(memory_space=pltpu.SMEM)] + [pl.BlockSpec(memory_space=pl.ANY)] * 4,
        out_specs=(pl.BlockSpec(memory_space=pltpu.VMEM),) * 3,
        scratch_shapes=[
            pltpu.VMEM(index.shape, jnp.int32),
            pltpu.VMEM((slots + 1, size, size), BF16),
            pltpu.VMEM((basis, occupied), BF16),
            pltpu.VMEM(metric.shape, F32),
            pltpu.VMEM((occupied, basis), BF16),
            pltpu.VMEM((8, wide), F32),
            pltpu.VMEM((8, wide), jnp.int32),
            pltpu.SMEM((8, wide), jnp.int32),
            pltpu.SemaphoreType.DMA((slots // CHUNK,)),
            pltpu.SemaphoreType.DMA((4,)),
        ],
        compiler_params=pltpu.CompilerParams(vmem_limit_bytes=36 * 2**20),
        cost_estimate=pl.CostEstimate(
            flops=2 * slots * size * size * occupied + 2 * q_dev * basis * occupied * occupied,
            bytes_accessed=2 * slots * size * size + 2 * q_dev * basis * occupied,
            transcendentals=0,
        ),
        name="half_transform_pairs",
    )(live, *(pltpu.with_memory_space_constraint(x, pltpu.HBM) for x in (index, blocks, orbitals, metric)))
    if not split:
        pairs = pairs.reshape(q_dev, owners, occupied // owners, occupied).transpose(1, 0, 2, 3)
    return slab.reshape(q_dev, basis, occupied), pairs, metric_split


def metric_kernel(split_ref, held_ref, out_ref, spread, mixed):
    naux, each, occupied = held_ref.shape
    spread[...] = held_ref[...].astype(F32).reshape(naux * each, occupied)
    for r in range(0, each, 2):
        both = [spread[pl.ds(r + u, naux, stride=each), :].astype(BF16) for u in range(2)]
        parts = jnp.dot(split_ref[...], jnp.concatenate(both, axis=1), preferred_element_type=F32)
        fitted = parts[:naux] + parts[naux:]
        for u in range(2):
            mixed[pl.ds(r + u, naux, stride=each), :] = fitted[:, u * occupied : (u + 1) * occupied]
    out_ref[...] = mixed[...].reshape(naux, each, occupied).astype(BF16)


def apply_metric(metric, metric_split, held):
    naux, each, occupied = held.shape
    if each % 8:
        fitted = jnp.einsum("qp,pij->qij", metric, held.astype(F32), precision=lax.Precision.HIGHEST)
        return fitted.astype(BF16)
    return pl.pallas_call(
        metric_kernel,
        out_shape=jax.ShapeDtypeStruct(held.shape, BF16),
        in_specs=[pl.BlockSpec(memory_space=pltpu.VMEM)] * 2,
        out_specs=pl.BlockSpec(memory_space=pltpu.VMEM),
        scratch_shapes=[pltpu.VMEM((naux * each, occupied), F32)] * 2,
        compiler_params=pltpu.CompilerParams(vmem_limit_bytes=12 * 2**20),
        cost_estimate=pl.CostEstimate(
            flops=4 * naux * naux * each * occupied, bytes_accessed=4 * naux * each * occupied, transcendentals=0
        ),
        name="apply_metric",
    )(pltpu.with_memory_space_constraint(metric_split, pltpu.VMEM), held)


def gather_fitted(fitted_ref, fitted):
    q_dev = fitted.shape[0] // fitted.shape[1]
    occupied = fitted.shape[1]
    for q in range(q_dev):
        if len(fitted_ref.shape) == 4:
            block = fitted_ref[:, q].astype(F32).reshape(occupied, occupied).astype(BF16)
        else:
            block = fitted_ref[q]
        fitted[q * occupied : (q + 1) * occupied, :] = block


def exchange_kernel(blocks, gather, more, skip, slab, fitted_ref, *refs):
    refs = list(refs)
    more_ref = refs.pop(0) if more else None
    out_refs = [refs.pop(0) for _ in blocks]
    if gather:
        fitted = refs.pop(0)
        gather_fitted(fitted_ref, fitted)
    else:
        fitted = fitted_ref
    q_dev = slab.shape[0]
    each = out_refs[0].shape[1]
    me = lax.axis_index("aux").astype(jnp.int32)
    todo = [(k, c, h) for c, part in enumerate(blocks) for h, k in enumerate(part)]
    together = next(n for n in (4, 3, 2, 1) if len(todo) % n == 0)
    for g in range(0, len(todo), together):
        rows = [pl.ds(pl.multiple_of((me ^ k) * each, each), each) for k, _, _ in todo[g : g + together]]
        every = jnp.concatenate(
            [jnp.concatenate([slab[q, r, :] for r in rows], axis=0) for q in range(q_dev)], axis=1
        )
        sums = jnp.dot(every, fitted[...], preferred_element_type=F32)
        for u, (_, c, h) in enumerate(todo[g : g + together]):
            part = sums[u * each : (u + 1) * each]
            if more:
                part = part + more_ref[skip + g + u].astype(F32)
            out_refs[c][h] = part.astype(out_refs[c].dtype)


def exchange_rows(slab, fitted, owners, blocks, dtype, gather=False, more=None, skip=0):
    q_dev, basis, occupied = slab.shape
    each = basis // owners
    count = sum(len(part) for part in blocks)
    out = [jax.ShapeDtypeStruct((len(part), each, occupied), dtype) for part in blocks]
    if gather:
        out.append(jax.ShapeDtypeStruct((q_dev * occupied, occupied), BF16))
    operands = [pltpu.with_memory_space_constraint(slab, pltpu.VMEM), fitted] + ([] if more is None else [more])
    return pl.pallas_call(
        functools.partial(exchange_kernel, blocks, gather, more is not None, skip),
        out_shape=out,
        in_specs=[pl.BlockSpec(memory_space=pltpu.VMEM)] * len(operands),
        out_specs=[pl.BlockSpec(memory_space=pltpu.VMEM)] * len(out),
        compiler_params=pltpu.CompilerParams(vmem_limit_bytes=24 * 2**20),
        cost_estimate=pl.CostEstimate(
            flops=2 * q_dev * occupied * count * each * occupied,
            bytes_accessed=2 * q_dev * occupied * count * each,
            transcendentals=0,
        ),
        name="exchange_rows",
    )(*operands)


def body(owners, integrals, block_index, live_count, orbitals, metric):
    basis, occupied = orbitals.shape
    naux = metric.shape[1]
    q_dev = naux // owners

    slab, pairs, metric_split = half_transform(integrals, block_index.T, live_count, orbitals, metric, q_dev, owners)

    trade = functools.partial(lax.all_to_all, axis_name="aux", split_axis=0, concat_axis=0, tiled=True)
    held = trade(pairs).reshape(naux, occupied // owners, occupied)
    fitted = apply_metric(metric, metric_split, held)
    fitted = trade(fitted.reshape(owners, q_dev, occupied // owners, occupied))
    if (occupied // owners) % 8:
        fitted = fitted.transpose(1, 0, 2, 3).reshape(q_dev, occupied, occupied)

    def swap(x, bits):
        return lax.ppermute(x, "aux", [(d, d ^ bits) for d in range(owners)])

    far = range(0, owners, 8)
    stay, out2, out4, out6 = (tuple(x + k for k in far) for x in (0, 2, 4, 6))
    flip = lambda blocks: [tuple(k ^ 1 for k in blocks)]
    away, fitted = exchange_rows(slab, fitted, owners, flip(out6 + out4), BF16, gather=True)
    early = swap(away, 1)
    (away,) = exchange_rows(slab, fitted, owners, flip(out2 + stay), BF16)
    late = swap(away, 1)
    away6, away4 = exchange_rows(slab, fitted, owners, [out6, out4], BF16, more=early)
    arrived = [swap(away6, 6), swap(away4, 4)]
    (away2,) = exchange_rows(slab, fitted, owners, [out2], BF16, more=late)
    arrived.append(swap(away2, 2))
    (near,) = exchange_rows(slab, fitted, owners, [stay], F32, more=late, skip=len(far))
    for x in arrived:
        near = near + x.astype(F32)
    total = near[0]
    for c, k in enumerate(far):
        if k:
            total = total + swap(near[c].astype(BF16), k).astype(F32)
    return total


def solution(mesh):
    placed = (
        P(("groups", "aux"), None, None),
        P(("groups", "aux"), None),
        P(("groups", "aux")),
        P("groups", None),
        P("groups", None),
    )
    return jax.shard_map(
        functools.partial(body, mesh.shape["aux"]),
        mesh=mesh, in_specs=placed, out_specs=P(("groups", "aux"), None), check_vma=False,
    )
```

```python
import functools

import jax
import jax.numpy as jnp
from jax import lax
from jax.experimental import pallas as pl
from jax.experimental.pallas import tpu as pltpu
from jax.sharding import PartitionSpec as P

UNROLL = 64
CHUNK = 32
TURNS = 5
FLIGHT = 4
F32 = jnp.float32
BF16 = jnp.bfloat16


def rank_slots(live, index_ref, rows, meta, nblk, nkeys, chunks, pump):
    slots = index_ref.shape[1]
    wide = rows.shape[1]
    never = float(chunks * nkeys)
    assert slots < 512 and nblk <= 32 and nkeys <= 512 and CHUNK % 8 == 0
    rows[...] = jnp.full(rows.shape, nkeys, F32)
    key = index_ref[0:1, :] * nblk + index_ref[1:2, :]
    slot = lax.broadcasted_iota(jnp.int32, (1, slots), 1)
    rows[0:1, 0:slots] = jnp.where(slot < live, key, nkeys).astype(F32)
    rows[1:2, 0:slots] = (slot * 32768 + index_ref[2:3, :] * 1024).astype(F32)
    row = rows[0:1, :]
    lives = row < nkeys
    tile = (8, wide)
    zero = jnp.zeros(tile, F32)
    lane = lax.broadcasted_iota(jnp.int32, tile, 1)
    ahead = lane - lax.broadcasted_iota(jnp.int32, tile, 0)

    every = jnp.broadcast_to(row, tile)
    columns = rows[...].T
    late = zero
    for s in range(0, slots, 8):
        late = jnp.where(columns[s : s + 8, 0:1] == every, float(s // CHUNK), late)
    late = jnp.max(late, axis=0, keepdims=True)
    pump()
    order = jnp.where(lives, late * nkeys + row, never)

    every = jnp.broadcast_to(order, tile)
    columns = every.T
    rank, place = zero, zero
    for s in range(0, slots, 8):
        column = columns[s : s + 8, 0:1]
        same = (column == every) & (ahead > s)
        rank = rank + jnp.where(same, 1.0, 0.0)
        place = place + jnp.where(same | (column < every), 1.0, 0.0)
    pump()
    rank = jnp.sum(rank, axis=0, keepdims=True)
    place = jnp.sum(place, axis=0, keepdims=True)
    end = jnp.max(jnp.where(lives, order, 0.0), axis=1, keepdims=True)
    last = jnp.max(jnp.where(lives & (order == end), row, 0.0), axis=1, keepdims=True)
    nothing = 2.0 * last + slots * 32768.0
    rows[1:2, :] = rows[1:2, :] + 2.0 * row + jnp.where(rank == 0.0, 1.0, 0.0) - nothing
    rows[2:3, :] = jnp.where(lives, place, -1.0)
    rows[3:4, :] = late - (chunks - 1)

    columns = rows[...].T
    spot = lane.astype(F32)
    number, need = zero, zero
    for s in range(0, slots, 8):
        found = columns[s : s + 8, 2:3] == spot
        number = number + jnp.where(found, columns[s : s + 8, 1:2], 0.0)
        need = need + jnp.where(found, columns[s : s + 8, 3:4], 0.0)
    meta[0:1, :] = (jnp.sum(number, axis=0, keepdims=True) + nothing).astype(jnp.int32)
    meta[1:2, :] = (jnp.sum(need, axis=0, keepdims=True) + (chunks - 1)).astype(jnp.int32)


def half_kernel(
    owners, q_dev, live_ref, index_hbm, blocks_hbm, orb_hbm, metric_hbm, slab, pairs_ref, split_ref,
    index_ref, held, orb_ref, metric_ref, orb_t, rows, meta, facts, in_sem, small_sem,
):
    slots, size, _ = blocks_hbm.shape
    occupied = orb_ref.shape[1]
    nblk = orb_ref.shape[0] // size
    nkeys = q_dev * nblk
    chunks = slots // CHUNK

    def fetch(c):
        part = pl.ds(c * CHUNK, CHUNK)
        return pltpu.make_async_copy(blocks_hbm.at[part], held.at[part], in_sem.at[c])

    def clear(first, last):
        @pl.loop(first, last, step=8)
        def _(k):
            for u in range(8):
                slab[k + u] = jnp.zeros((size, occupied), BF16)

    small = [
        pltpu.make_async_copy(source, target, small_sem.at[1 + k])
        for k, (source, target) in enumerate(
            [(index_hbm, index_ref), (orb_hbm, orb_ref), (metric_hbm, metric_ref)]
        )
    ]
    small[0].start()
    small[1].start()
    for c in range(min(FLIGHT, chunks)):
        fetch(c).start()
    came = [0]

    def pump():
        if came[0] + FLIGHT < chunks:
            fetch(came[0]).wait()
            fetch(came[0] + FLIGHT).start()
            came[0] += 1


    held[slots] = jnp.zeros((size, size), BF16)
    clear(0, nkeys // 2)

    small[0].wait()
    pump()
    rank_slots(live_ref[0], index_ref, rows, meta, nblk, nkeys, chunks, pump)
    pump()
    copy = pltpu.make_async_copy(meta, facts, small_sem.at[0])
    copy.start()

    clear(nkeys // 2, 3 * nkeys // 4)
    pump()
    clear(3 * nkeys // 4, nkeys)
    while came[0] + FLIGHT < chunks:
        pump()
    small[2].start()
    small[1].wait()
    copy.wait()

    def arrive(c, nothing):
        fetch(c).wait()
        return nothing

    def turn(b):
        part = pl.ds(pl.multiple_of(b * size, size), size)
        orb_t[:, part] = orb_ref[part, :].T

    def step(g, carry):
        arrived, total = carry
        needed = jnp.maximum(arrived, facts[1, g * UNROLL + UNROLL - 1] + 1)
        lax.fori_loop(arrived, needed, arrive, 0)
        for u in range(TURNS):
            turn(jnp.minimum(g * TURNS + u, nblk - 1))
        empty = jnp.zeros((size, occupied), BF16)
        for u in range(0, UNROLL, 2):
            pair = [facts[0, g * UNROLL + u + w] for w in range(2)]
            orbs = [orb_ref[pl.ds(pl.multiple_of(((v >> 10) & 31) * size, size), size), :] for v in pair]
            diagonal = jnp.concatenate(
                [jnp.concatenate([orbs[0], empty], axis=1), jnp.concatenate([empty, orbs[1]], axis=1)], axis=0
            )
            blocks = jnp.concatenate([held[v >> 15] for v in pair], axis=1)
            products = jnp.dot(blocks, diagonal, preferred_element_type=F32)
            for w, v in enumerate(pair):
                product = products[:, w * occupied : (w + 1) * occupied]
                total = jnp.where((v & 1) == 1, product, total + product)
                slab[(v & 1023) >> 1] = total.astype(BF16)
        return needed, total

    bodies = (live_ref[0] + UNROLL - 1) // UNROLL
    arrived, _ = lax.fori_loop(0, bodies, step, (jnp.int32(came[0]), jnp.zeros((size, occupied), F32)))
    lax.fori_loop(arrived, chunks, arrive, 0)

    @pl.loop(jnp.minimum(bodies * TURNS, nblk), nblk)
    def _(b):
        turn(b)

    small[2].wait()
    metric = metric_ref[...]
    high = metric.astype(BF16)
    naux = metric.shape[0]
    split_ref[0:naux, :] = high
    split_ref[naux : 2 * naux, :] = (metric - high.astype(F32)).astype(BF16)

    @pl.loop(0, q_dev // 2, unroll=8)
    def _(t):
        block = jnp.concatenate(
            [slab[pl.ds((2 * t + u) * nblk, nblk)].reshape(nblk * size, occupied) for u in range(2)], axis=1
        )
        total = jnp.dot(orb_t[...], block, preferred_element_type=F32)
        for u in range(2):
            pair = total[:, u * occupied : (u + 1) * occupied].T
            if owners:
                pairs_ref[:, 2 * t + u] = pair.reshape(owners, occupied // owners, occupied).astype(BF16)
            else:
                pairs_ref[2 * t + u] = pair.astype(BF16)


def half_transform(blocks, index, live, orbitals, metric, q_dev, owners):
    slots, size, _ = blocks.shape
    basis, occupied = orbitals.shape
    nblk = basis // size
    split = (occupied // owners) % 8 == 0
    pairs_shape = (owners, q_dev, occupied // owners, occupied) if split else (q_dev, occupied, occupied)
    wide = -(-(slots + UNROLL) // 128) * 128
    slab, pairs, metric_split = pl.pallas_call(
        functools.partial(half_kernel, owners if split else 0, q_dev),
        out_shape=(
            pltpu.VMEM((q_dev * nblk, size, occupied), BF16),
            jax.ShapeDtypeStruct(pairs_shape, BF16),
            pltpu.VMEM((2 * metric.shape[0], metric.shape[1]), BF16),
        ),
        in_specs=[pl.BlockSpec(memory_space=pltpu.SMEM)] + [pl.BlockSpec(memory_space=pl.ANY)] * 4,
        out_specs=(pl.BlockSpec(memory_space=pltpu.VMEM),) * 3,
        scratch_shapes=[
            pltpu.VMEM(index.shape, jnp.int32),
            pltpu.VMEM((slots + 1, size, size), BF16),
            pltpu.VMEM((basis, occupied), BF16),
            pltpu.VMEM(metric.shape, F32),
            pltpu.VMEM((occupied, basis), BF16),
            pltpu.VMEM((8, wide), F32),
            pltpu.VMEM((8, wide), jnp.int32),
            pltpu.SMEM((8, wide), jnp.int32),
            pltpu.SemaphoreType.DMA((slots // CHUNK,)),
            pltpu.SemaphoreType.DMA((4,)),
        ],
        compiler_params=pltpu.CompilerParams(vmem_limit_bytes=36 * 2**20),
        cost_estimate=pl.CostEstimate(
            flops=2 * slots * size * size * occupied + 2 * q_dev * basis * occupied * occupied,
            bytes_accessed=2 * slots * size * size + 2 * q_dev * basis * occupied,
            transcendentals=0,
        ),
        name="half_transform_pairs",
    )(live, *(pltpu.with_memory_space_constraint(x, pltpu.HBM) for x in (index, blocks, orbitals, metric)))
    if not split:
        pairs = pairs.reshape(q_dev, owners, occupied // owners, occupied).transpose(1, 0, 2, 3)
    return slab.reshape(q_dev, basis, occupied), pairs, metric_split


def metric_kernel(split_ref, held_ref, out_ref, spread, mixed):
    naux, each, occupied = held_ref.shape
    spread[...] = held_ref[...].astype(F32).reshape(naux * each, occupied)
    for r in range(0, each, 2):
        both = [spread[pl.ds(r + u, naux, stride=each), :].astype(BF16) for u in range(2)]
        parts = jnp.dot(split_ref[...], jnp.concatenate(both, axis=1), preferred_element_type=F32)
        fitted = parts[:naux] + parts[naux:]
        for u in range(2):
            mixed[pl.ds(r + u, naux, stride=each), :] = fitted[:, u * occupied : (u + 1) * occupied]
    out_ref[...] = mixed[...].reshape(naux, each, occupied).astype(BF16)


def apply_metric(metric, metric_split, held):
    naux, each, occupied = held.shape
    if each % 8:
        fitted = jnp.einsum("qp,pij->qij", metric, held.astype(F32), precision=lax.Precision.HIGHEST)
        return fitted.astype(BF16)
    return pl.pallas_call(
        metric_kernel,
        out_shape=jax.ShapeDtypeStruct(held.shape, BF16),
        in_specs=[pl.BlockSpec(memory_space=pltpu.VMEM)] * 2,
        out_specs=pl.BlockSpec(memory_space=pltpu.VMEM),
        scratch_shapes=[pltpu.VMEM((naux * each, occupied), F32)] * 2,
        compiler_params=pltpu.CompilerParams(vmem_limit_bytes=12 * 2**20),
        cost_estimate=pl.CostEstimate(
            flops=4 * naux * naux * each * occupied, bytes_accessed=4 * naux * each * occupied, transcendentals=0
        ),
        name="apply_metric",
    )(pltpu.with_memory_space_constraint(metric_split, pltpu.VMEM), held)


def gather_fitted(fitted_ref, fitted):
    q_dev = fitted.shape[0] // fitted.shape[1]
    occupied = fitted.shape[1]
    for q in range(q_dev):
        if len(fitted_ref.shape) == 4:
            block = fitted_ref[:, q].astype(F32).reshape(occupied, occupied).astype(BF16)
        else:
            block = fitted_ref[q]
        fitted[q * occupied : (q + 1) * occupied, :] = block


def exchange_kernel(blocks, gather, more, skip, after, slab, fitted_ref, *refs):
    refs = list(refs)
    more_ref = refs.pop(0) if more else None
    if after:
        refs.pop(0)
    out_refs = [refs.pop(0) for _ in blocks]
    if gather:
        fitted = refs.pop(0)
        gather_fitted(fitted_ref, fitted)
    else:
        fitted = fitted_ref
        refs.pop(0)[...] = jnp.zeros((8, 128), F32)
    q_dev = slab.shape[0]
    each = out_refs[0].shape[1]
    me = lax.axis_index("aux").astype(jnp.int32)
    todo = [(k, c, h) for c, part in enumerate(blocks) for h, k in enumerate(part)]
    together = next(n for n in (4, 3, 2, 1) if len(todo) % n == 0)
    for g in range(0, len(todo), together):
        rows = [pl.ds(pl.multiple_of((me ^ k) * each, each), each) for k, _, _ in todo[g : g + together]]
        every = jnp.concatenate(
            [jnp.concatenate([slab[q, r, :] for r in rows], axis=0) for q in range(q_dev)], axis=1
        )
        sums = jnp.dot(every, fitted[...], preferred_element_type=F32)
        for u, (_, c, h) in enumerate(todo[g : g + together]):
            part = sums[u * each : (u + 1) * each]
            if more:
                part = part + more_ref[skip + g + u].astype(F32)
            out_refs[c][h] = part.astype(out_refs[c].dtype)


def exchange_rows(slab, fitted, owners, blocks, dtype, gather=False, more=None, skip=0, after=None):
    q_dev, basis, occupied = slab.shape
    each = basis // owners
    count = sum(len(part) for part in blocks)
    out = [jax.ShapeDtypeStruct((len(part), each, occupied), dtype) for part in blocks]
    if gather:
        out.append(jax.ShapeDtypeStruct((q_dev * occupied, occupied), BF16))
    else:
        out.append(jax.ShapeDtypeStruct((8, 128), F32))
    operands = [pltpu.with_memory_space_constraint(slab, pltpu.VMEM), fitted] + [x for x in (more, after) if x is not None]
    return pl.pallas_call(
        functools.partial(exchange_kernel, blocks, gather, more is not None, skip, after is not None),
        out_shape=out,
        in_specs=[pl.BlockSpec(memory_space=pltpu.VMEM)] * len(operands),
        out_specs=[pl.BlockSpec(memory_space=pltpu.VMEM)] * len(out),
        compiler_params=pltpu.CompilerParams(vmem_limit_bytes=24 * 2**20),
        cost_estimate=pl.CostEstimate(
            flops=2 * q_dev * occupied * count * each * occupied,
            bytes_accessed=2 * q_dev * occupied * count * each,
            transcendentals=0,
        ),
        name="exchange_rows",
    )(*operands)


def body(owners, integrals, block_index, live_count, orbitals, metric):
    basis, occupied = orbitals.shape
    naux = metric.shape[1]
    q_dev = naux // owners

    slab, pairs, metric_split = half_transform(integrals, block_index.T, live_count, orbitals, metric, q_dev, owners)

    trade = functools.partial(lax.all_to_all, axis_name="aux", split_axis=0, concat_axis=0, tiled=True)
    held = trade(pairs).reshape(naux, occupied // owners, occupied)
    fitted = apply_metric(metric, metric_split, held)
    fitted = trade(fitted.reshape(owners, q_dev, occupied // owners, occupied))
    if (occupied // owners) % 8:
        fitted = fitted.transpose(1, 0, 2, 3).reshape(q_dev, occupied, occupied)

    def swap(x, bits):
        return lax.ppermute(x, "aux", [(d, d ^ bits) for d in range(owners)])

    far = range(0, owners, 8)
    stay, out2, out4, out6 = (tuple(x + k for k in far) for x in (0, 2, 4, 6))
    flip = lambda blocks: [tuple(k ^ 1 for k in blocks)]
    away, fitted = exchange_rows(slab, fitted, owners, flip(out6 + out4 + out2), BF16, gather=True)
    leave = swap(away, 1)
    away, _ = exchange_rows(slab, fitted, owners, flip(stay), BF16)
    keep = swap(away, 1)
    away6, away4, tie = exchange_rows(slab, fitted, owners, [out6, out4], BF16, more=leave)
    arrived = [swap(away6, 6), swap(away4, 4)]
    away2, tie = exchange_rows(slab, fitted, owners, [out2], BF16, more=leave, skip=2 * len(far), after=tie)
    arrived.append(swap(away2, 2))
    near, _ = exchange_rows(slab, fitted, owners, [stay], F32, more=keep, after=tie)
    for x in arrived:
        near = near + x.astype(F32)
    total = near[0]
    for c, k in enumerate(far):
        if k:
            total = total + swap(near[c].astype(BF16), k).astype(F32)
    return total


def solution(mesh):
    placed = (
        P(("groups", "aux"), None, None),
        P(("groups", "aux"), None),
        P(("groups", "aux")),
        P("groups", None),
        P("groups", None),
    )
    return jax.shard_map(
        functools.partial(body, mesh.shape["aux"]),
        mesh=mesh, in_specs=placed, out_specs=P(("groups", "aux"), None), check_vma=False,
    )
```

```python
import functools

import jax
import jax.numpy as jnp
from jax import lax
from jax.experimental import pallas as pl
from jax.experimental.pallas import tpu as pltpu
from jax.sharding import PartitionSpec as P

UNROLL = 64
CHUNK = 32
TURNS = 5
FLIGHT = 4
F32 = jnp.float32
BF16 = jnp.bfloat16


def rank_slots(live, index_ref, rows, meta, nblk, nkeys, chunks, pump):
    slots = index_ref.shape[1]
    wide = rows.shape[1]
    never = float(chunks * nkeys)
    assert slots < 512 and nblk <= 32 and nkeys <= 512 and CHUNK % 8 == 0
    rows[...] = jnp.full(rows.shape, nkeys, F32)
    key = index_ref[0:1, :] * nblk + index_ref[1:2, :]
    slot = lax.broadcasted_iota(jnp.int32, (1, slots), 1)
    rows[0:1, 0:slots] = jnp.where(slot < live, key, nkeys).astype(F32)
    rows[1:2, 0:slots] = (slot * 32768 + index_ref[2:3, :] * 1024).astype(F32)
    row = rows[0:1, :]
    lives = row < nkeys
    tile = (8, wide)
    zero = jnp.zeros(tile, F32)
    lane = lax.broadcasted_iota(jnp.int32, tile, 1)
    ahead = lane - lax.broadcasted_iota(jnp.int32, tile, 0)

    every = jnp.broadcast_to(row, tile)
    columns = rows[...].T
    late = zero
    for s in range(0, slots, 8):
        late = jnp.where(columns[s : s + 8, 0:1] == every, float(s // CHUNK), late)
    late = jnp.max(late, axis=0, keepdims=True)
    pump()
    order = jnp.where(lives, late * nkeys + row, never)

    every = jnp.broadcast_to(order, tile)
    columns = every.T
    rank, place = zero, zero
    for s in range(0, slots, 8):
        column = columns[s : s + 8, 0:1]
        same = (column == every) & (ahead > s)
        rank = rank + jnp.where(same, 1.0, 0.0)
        place = place + jnp.where(same | (column < every), 1.0, 0.0)
    pump()
    rank = jnp.sum(rank, axis=0, keepdims=True)
    place = jnp.sum(place, axis=0, keepdims=True)
    end = jnp.max(jnp.where(lives, order, 0.0), axis=1, keepdims=True)
    last = jnp.max(jnp.where(lives & (order == end), row, 0.0), axis=1, keepdims=True)
    nothing = 2.0 * last + slots * 32768.0
    rows[1:2, :] = rows[1:2, :] + 2.0 * row + jnp.where(rank == 0.0, 1.0, 0.0) - nothing
    rows[2:3, :] = jnp.where(lives, place, -1.0)
    rows[3:4, :] = late - (chunks - 1)

    columns = rows[...].T
    spot = lane.astype(F32)
    number, need = zero, zero
    for s in range(0, slots, 8):
        found = columns[s : s + 8, 2:3] == spot
        number = number + jnp.where(found, columns[s : s + 8, 1:2], 0.0)
        need = need + jnp.where(found, columns[s : s + 8, 3:4], 0.0)
    meta[0:1, :] = (jnp.sum(number, axis=0, keepdims=True) + nothing).astype(jnp.int32)
    meta[1:2, :] = (jnp.sum(need, axis=0, keepdims=True) + (chunks - 1)).astype(jnp.int32)


def half_kernel(
    owners, q_dev, live_ref, index_hbm, blocks_hbm, orb_hbm, metric_hbm, slab, pairs_ref, split_ref,
    index_ref, held, orb_ref, metric_ref, orb_t, rows, meta, facts, in_sem, small_sem,
):
    slots, size, _ = blocks_hbm.shape
    occupied = orb_ref.shape[1]
    nblk = orb_ref.shape[0] // size
    nkeys = q_dev * nblk
    chunks = slots // CHUNK

    def fetch(c):
        part = pl.ds(c * CHUNK, CHUNK)
        return pltpu.make_async_copy(blocks_hbm.at[part], held.at[part], in_sem.at[c])

    def clear(first, last):
        @pl.loop(first, last, step=8)
        def _(k):
            for u in range(8):
                slab[k + u] = jnp.zeros((size, occupied), BF16)

    small = [
        pltpu.make_async_copy(source, target, small_sem.at[1 + k])
        for k, (source, target) in enumerate(
            [(index_hbm, index_ref), (orb_hbm, orb_ref), (metric_hbm, metric_ref)]
        )
    ]
    small[0].start()
    small[1].start()
    for c in range(min(FLIGHT, chunks)):
        fetch(c).start()
    came = [0]

    def pump():
        if came[0] + FLIGHT < chunks:
            fetch(came[0]).wait()
            fetch(came[0] + FLIGHT).start()
            came[0] += 1


    held[slots] = jnp.zeros((size, size), BF16)
    clear(0, nkeys // 2)

    small[0].wait()
    pump()
    rank_slots(live_ref[0], index_ref, rows, meta, nblk, nkeys, chunks, pump)
    pump()
    copy = pltpu.make_async_copy(meta, facts, small_sem.at[0])
    copy.start()

    clear(nkeys // 2, 3 * nkeys // 4)
    pump()
    clear(3 * nkeys // 4, nkeys)
    while came[0] + FLIGHT < chunks:
        pump()
    small[2].start()
    small[1].wait()
    copy.wait()

    def arrive(c, nothing):
        fetch(c).wait()
        return nothing

    def turn(b):
        part = pl.ds(pl.multiple_of(b * size, size), size)
        orb_t[:, part] = orb_ref[part, :].T

    def step(g, carry):
        arrived, total = carry
        needed = jnp.maximum(arrived, facts[1, g * UNROLL + UNROLL - 1] + 1)
        lax.fori_loop(arrived, needed, arrive, 0)
        for u in range(TURNS):
            turn(jnp.minimum(g * TURNS + u, nblk - 1))
        empty = jnp.zeros((size, occupied), BF16)
        for u in range(0, UNROLL, 2):
            pair = [facts[0, g * UNROLL + u + w] for w in range(2)]
            orbs = [orb_ref[pl.ds(pl.multiple_of(((v >> 10) & 31) * size, size), size), :] for v in pair]
            diagonal = jnp.concatenate(
                [jnp.concatenate([orbs[0], empty], axis=1), jnp.concatenate([empty, orbs[1]], axis=1)], axis=0
            )
            blocks = jnp.concatenate([held[v >> 15] for v in pair], axis=1)
            products = jnp.dot(blocks, diagonal, preferred_element_type=F32)
            for w, v in enumerate(pair):
                product = products[:, w * occupied : (w + 1) * occupied]
                total = jnp.where((v & 1) == 1, product, total + product)
                slab[(v & 1023) >> 1] = total.astype(BF16)
        return needed, total

    bodies = (live_ref[0] + UNROLL - 1) // UNROLL
    arrived, _ = lax.fori_loop(0, bodies, step, (jnp.int32(came[0]), jnp.zeros((size, occupied), F32)))
    lax.fori_loop(arrived, chunks, arrive, 0)

    @pl.loop(jnp.minimum(bodies * TURNS, nblk), nblk)
    def _(b):
        turn(b)

    small[2].wait()
    metric = metric_ref[...]
    high = metric.astype(BF16)
    naux = metric.shape[0]
    split_ref[0:naux, :] = high
    split_ref[naux : 2 * naux, :] = (metric - high.astype(F32)).astype(BF16)

    @pl.loop(0, q_dev // 2, unroll=8)
    def _(t):
        block = jnp.concatenate(
            [slab[pl.ds((2 * t + u) * nblk, nblk)].reshape(nblk * size, occupied) for u in range(2)], axis=1
        )
        total = jnp.dot(orb_t[...], block, preferred_element_type=F32)
        for u in range(2):
            pair = total[:, u * occupied : (u + 1) * occupied].T
            if owners:
                pairs_ref[:, 2 * t + u] = pair.reshape(owners, occupied // owners, occupied).astype(BF16)
            else:
                pairs_ref[2 * t + u] = pair.astype(BF16)


def half_transform(blocks, index, live, orbitals, metric, q_dev, owners):
    slots, size, _ = blocks.shape
    basis, occupied = orbitals.shape
    nblk = basis // size
    split = (occupied // owners) % 8 == 0
    pairs_shape = (owners, q_dev, occupied // owners, occupied) if split else (q_dev, occupied, occupied)
    wide = -(-(slots + UNROLL) // 128) * 128
    slab, pairs, metric_split = pl.pallas_call(
        functools.partial(half_kernel, owners if split else 0, q_dev),
        out_shape=(
            pltpu.VMEM((q_dev * nblk, size, occupied), BF16),
            jax.ShapeDtypeStruct(pairs_shape, BF16),
            pltpu.VMEM((2 * metric.shape[0], metric.shape[1]), BF16),
        ),
        in_specs=[pl.BlockSpec(memory_space=pltpu.SMEM)] + [pl.BlockSpec(memory_space=pl.ANY)] * 4,
        out_specs=(pl.BlockSpec(memory_space=pltpu.VMEM),) * 3,
        scratch_shapes=[
            pltpu.VMEM(index.shape, jnp.int32),
            pltpu.VMEM((slots + 1, size, size), BF16),
            pltpu.VMEM((basis, occupied), BF16),
            pltpu.VMEM(metric.shape, F32),
            pltpu.VMEM((occupied, basis), BF16),
            pltpu.VMEM((8, wide), F32),
            pltpu.VMEM((8, wide), jnp.int32),
            pltpu.SMEM((8, wide), jnp.int32),
            pltpu.SemaphoreType.DMA((slots // CHUNK,)),
            pltpu.SemaphoreType.DMA((4,)),
        ],
        compiler_params=pltpu.CompilerParams(vmem_limit_bytes=36 * 2**20),
        cost_estimate=pl.CostEstimate(
            flops=2 * slots * size * size * occupied + 2 * q_dev * basis * occupied * occupied,
            bytes_accessed=2 * slots * size * size + 2 * q_dev * basis * occupied,
            transcendentals=0,
        ),
        name="half_transform_pairs",
    )(live, *(pltpu.with_memory_space_constraint(x, pltpu.HBM) for x in (index, blocks, orbitals, metric)))
    if not split:
        pairs = pairs.reshape(q_dev, owners, occupied // owners, occupied).transpose(1, 0, 2, 3)
    return slab.reshape(q_dev, basis, occupied), pairs, metric_split


def metric_kernel(split_ref, held_ref, out_ref, spread, mixed):
    naux, each, occupied = held_ref.shape
    spread[...] = held_ref[...].astype(F32).reshape(naux * each, occupied)
    for r in range(0, each, 2):
        both = [spread[pl.ds(r + u, naux, stride=each), :].astype(BF16) for u in range(2)]
        parts = jnp.dot(split_ref[...], jnp.concatenate(both, axis=1), preferred_element_type=F32)
        fitted = parts[:naux] + parts[naux:]
        for u in range(2):
            mixed[pl.ds(r + u, naux, stride=each), :] = fitted[:, u * occupied : (u + 1) * occupied]
    out_ref[...] = mixed[...].reshape(naux, each, occupied).astype(BF16)


def apply_metric(metric, metric_split, held):
    naux, each, occupied = held.shape
    if each % 8:
        fitted = jnp.einsum("qp,pij->qij", metric, held.astype(F32), precision=lax.Precision.HIGHEST)
        return fitted.astype(BF16)
    return pl.pallas_call(
        metric_kernel,
        out_shape=jax.ShapeDtypeStruct(held.shape, BF16),
        in_specs=[pl.BlockSpec(memory_space=pltpu.VMEM)] * 2,
        out_specs=pl.BlockSpec(memory_space=pltpu.VMEM),
        scratch_shapes=[pltpu.VMEM((naux * each, occupied), F32)] * 2,
        compiler_params=pltpu.CompilerParams(vmem_limit_bytes=12 * 2**20),
        cost_estimate=pl.CostEstimate(
            flops=4 * naux * naux * each * occupied, bytes_accessed=4 * naux * each * occupied, transcendentals=0
        ),
        name="apply_metric",
    )(pltpu.with_memory_space_constraint(metric_split, pltpu.VMEM), held)


def gather_fitted(fitted_ref, fitted):
    q_dev = fitted.shape[0] // fitted.shape[1]
    occupied = fitted.shape[1]
    for q in range(q_dev):
        if len(fitted_ref.shape) == 4:
            block = fitted_ref[:, q].astype(F32).reshape(occupied, occupied).astype(BF16)
        else:
            block = fitted_ref[q]
        fitted[q * occupied : (q + 1) * occupied, :] = block


def exchange_kernel(blocks, gather, more, skip, after, tie, slab, fitted_ref, *refs):
    refs = list(refs)
    more_ref = refs.pop(0) if more else None
    if after:
        refs.pop(0)
    out_refs = [refs.pop(0) for _ in blocks]
    if gather:
        fitted = refs.pop(0)
        gather_fitted(fitted_ref, fitted)
    else:
        fitted = fitted_ref
    if tie:
        refs.pop(0)[...] = jnp.zeros((8, 128), F32)
    q_dev = slab.shape[0]
    each = out_refs[0].shape[1]
    me = lax.axis_index("aux").astype(jnp.int32)
    todo = [(k, c, h) for c, part in enumerate(blocks) for h, k in enumerate(part)]
    together = next(n for n in (4, 3, 2, 1) if len(todo) % n == 0)
    for g in range(0, len(todo), together):
        rows = [pl.ds(pl.multiple_of((me ^ k) * each, each), each) for k, _, _ in todo[g : g + together]]
        every = jnp.concatenate(
            [jnp.concatenate([slab[q, r, :] for r in rows], axis=0) for q in range(q_dev)], axis=1
        )
        sums = jnp.dot(every, fitted[...], preferred_element_type=F32)
        for u, (_, c, h) in enumerate(todo[g : g + together]):
            part = sums[u * each : (u + 1) * each]
            if more:
                part = part + more_ref[skip + g + u].astype(F32)
            out_refs[c][h] = part.astype(out_refs[c].dtype)


def exchange_rows(slab, fitted, owners, blocks, dtype, gather=False, more=None, skip=0, after=None, tie=False):
    q_dev, basis, occupied = slab.shape
    each = basis // owners
    count = sum(len(part) for part in blocks)
    out = [jax.ShapeDtypeStruct((len(part), each, occupied), dtype) for part in blocks]
    if gather:
        out.append(jax.ShapeDtypeStruct((q_dev * occupied, occupied), BF16))
    if tie:
        out.append(jax.ShapeDtypeStruct((8, 128), F32))
    operands = [pltpu.with_memory_space_constraint(slab, pltpu.VMEM), fitted] + [x for x in (more, after) if x is not None]
    return pl.pallas_call(
        functools.partial(exchange_kernel, blocks, gather, more is not None, skip, after is not None, tie),
        out_shape=out,
        in_specs=[pl.BlockSpec(memory_space=pltpu.VMEM)] * len(operands),
        out_specs=[pl.BlockSpec(memory_space=pltpu.VMEM)] * len(out),
        compiler_params=pltpu.CompilerParams(vmem_limit_bytes=24 * 2**20),
        cost_estimate=pl.CostEstimate(
            flops=2 * q_dev * occupied * count * each * occupied if after is None else 1,
            bytes_accessed=2 * q_dev * occupied * count * each if after is None else 1,
            transcendentals=0,
        ),
        name="exchange_rows",
    )(*operands)


def body(owners, integrals, block_index, live_count, orbitals, metric):
    basis, occupied = orbitals.shape
    naux = metric.shape[1]
    q_dev = naux // owners

    slab, pairs, metric_split = half_transform(integrals, block_index.T, live_count, orbitals, metric, q_dev, owners)

    trade = functools.partial(lax.all_to_all, axis_name="aux", split_axis=0, concat_axis=0, tiled=True)
    held = trade(pairs).reshape(naux, occupied // owners, occupied)
    fitted = apply_metric(metric, metric_split, held)
    fitted = trade(fitted.reshape(owners, q_dev, occupied // owners, occupied))
    if (occupied // owners) % 8:
        fitted = fitted.transpose(1, 0, 2, 3).reshape(q_dev, occupied, occupied)

    def swap(x, bits):
        return lax.ppermute(x, "aux", [(d, d ^ bits) for d in range(owners)])

    far = range(0, owners, 8)
    stay, out2, out4, out6 = (tuple(x + k for k in far) for x in (0, 2, 4, 6))
    flip = lambda blocks: [tuple(k ^ 1 for k in blocks)]
    away, fitted = exchange_rows(slab, fitted, owners, flip(out6 + out4 + out2), BF16, gather=True)
    leave = swap(away, 1)
    (away,) = exchange_rows(slab, fitted, owners, flip(stay), BF16)
    keep = swap(away, 1)
    away6, away4, tie = exchange_rows(slab, fitted, owners, [out6, out4], BF16, more=leave, tie=True)
    arrived = [swap(away6, 6), swap(away4, 4)]
    away2, tie = exchange_rows(slab, fitted, owners, [out2], BF16, more=leave, skip=2 * len(far), after=tie, tie=True)
    arrived.append(swap(away2, 2))
    (near,) = exchange_rows(slab, fitted, owners, [stay], F32, more=keep, after=tie)
    for x in arrived:
        near = near + x.astype(F32)
    total = near[0]
    for c, k in enumerate(far):
        if k:
            total = total + swap(near[c].astype(BF16), k).astype(F32)
    return total


def solution(mesh):
    placed = (
        P(("groups", "aux"), None, None),
        P(("groups", "aux"), None),
        P(("groups", "aux")),
        P("groups", None),
        P("groups", None),
    )
    return jax.shard_map(
        functools.partial(body, mesh.shape["aux"]),
        mesh=mesh, in_specs=placed, out_specs=P(("groups", "aux"), None), check_vma=False,
    )
```

```python
import functools

import jax
import jax.numpy as jnp
from jax import lax
from jax.experimental import pallas as pl
from jax.experimental.pallas import tpu as pltpu
from jax.sharding import PartitionSpec as P

UNROLL = 64
CHUNK = 32
TURNS = 5
FLIGHT = 4
F32 = jnp.float32
BF16 = jnp.bfloat16


def rank_slots(live, index_ref, rows, meta, nblk, nkeys, chunks, pump):
    slots = index_ref.shape[1]
    wide = rows.shape[1]
    never = float(chunks * nkeys)
    assert slots < 512 and nblk <= 32 and nkeys <= 512 and CHUNK % 8 == 0
    rows[...] = jnp.full(rows.shape, nkeys, F32)
    key = index_ref[0:1, :] * nblk + index_ref[1:2, :]
    slot = lax.broadcasted_iota(jnp.int32, (1, slots), 1)
    rows[0:1, 0:slots] = jnp.where(slot < live, key, nkeys).astype(F32)
    rows[1:2, 0:slots] = (slot * 32768 + index_ref[2:3, :] * 1024).astype(F32)
    row = rows[0:1, :]
    lives = row < nkeys
    tile = (8, wide)
    zero = jnp.zeros(tile, F32)
    lane = lax.broadcasted_iota(jnp.int32, tile, 1)
    ahead = lane - lax.broadcasted_iota(jnp.int32, tile, 0)

    every = jnp.broadcast_to(row, tile)
    columns = rows[...].T
    late = zero
    for s in range(0, slots, 8):
        late = jnp.where(columns[s : s + 8, 0:1] == every, float(s // CHUNK), late)
    late = jnp.max(late, axis=0, keepdims=True)
    pump()
    order = jnp.where(lives, late * nkeys + row, never)

    every = jnp.broadcast_to(order, tile)
    columns = every.T
    rank, place = zero, zero
    for s in range(0, slots, 8):
        column = columns[s : s + 8, 0:1]
        same = (column == every) & (ahead > s)
        rank = rank + jnp.where(same, 1.0, 0.0)
        place = place + jnp.where(same | (column < every), 1.0, 0.0)
    pump()
    rank = jnp.sum(rank, axis=0, keepdims=True)
    place = jnp.sum(place, axis=0, keepdims=True)
    end = jnp.max(jnp.where(lives, order, 0.0), axis=1, keepdims=True)
    last = jnp.max(jnp.where(lives & (order == end), row, 0.0), axis=1, keepdims=True)
    nothing = 2.0 * last + slots * 32768.0
    rows[1:2, :] = rows[1:2, :] + 2.0 * row + jnp.where(rank == 0.0, 1.0, 0.0) - nothing
    rows[2:3, :] = jnp.where(lives, place, -1.0)
    rows[3:4, :] = late - (chunks - 1)

    columns = rows[...].T
    spot = lane.astype(F32)
    number, need = zero, zero
    for s in range(0, slots, 8):
        found = columns[s : s + 8, 2:3] == spot
        number = number + jnp.where(found, columns[s : s + 8, 1:2], 0.0)
        need = need + jnp.where(found, columns[s : s + 8, 3:4], 0.0)
    meta[0:1, :] = (jnp.sum(number, axis=0, keepdims=True) + nothing).astype(jnp.int32)
    meta[1:2, :] = (jnp.sum(need, axis=0, keepdims=True) + (chunks - 1)).astype(jnp.int32)


def half_kernel(
    owners, q_dev, live_ref, index_hbm, blocks_hbm, orb_hbm, metric_hbm, slab, pairs_ref, split_ref,
    index_ref, held, orb_ref, metric_ref, orb_t, rows, meta, facts, in_sem, small_sem,
):
    slots, size, _ = blocks_hbm.shape
    occupied = orb_ref.shape[1]
    nblk = orb_ref.shape[0] // size
    nkeys = q_dev * nblk
    chunks = slots // CHUNK

    def fetch(c):
        part = pl.ds(c * CHUNK, CHUNK)
        return pltpu.make_async_copy(blocks_hbm.at[part], held.at[part], in_sem.at[c])

    def clear(first, last):
        @pl.loop(first, last, step=8)
        def _(k):
            for u in range(8):
                slab[k + u] = jnp.zeros((size, occupied), BF16)

    small = [
        pltpu.make_async_copy(source, target, small_sem.at[1 + k])
        for k, (source, target) in enumerate(
            [(index_hbm, index_ref), (orb_hbm, orb_ref), (metric_hbm, metric_ref)]
        )
    ]
    small[0].start()
    small[1].start()
    for c in range(min(FLIGHT, chunks)):
        fetch(c).start()
    came = [0]

    def pump():
        if came[0] + FLIGHT < chunks:
            fetch(came[0]).wait()
            fetch(came[0] + FLIGHT).start()
            came[0] += 1


    held[slots] = jnp.zeros((size, size), BF16)
    clear(0, nkeys // 2)

    small[0].wait()
    pump()
    rank_slots(live_ref[0], index_ref, rows, meta, nblk, nkeys, chunks, pump)
    pump()
    copy = pltpu.make_async_copy(meta, facts, small_sem.at[0])
    copy.start()

    clear(nkeys // 2, 3 * nkeys // 4)
    pump()
    clear(3 * nkeys // 4, nkeys)
    while came[0] + FLIGHT < chunks:
        pump()
    small[2].start()
    small[1].wait()
    copy.wait()

    def arrive(c, nothing):
        fetch(c).wait()
        return nothing

    def turn(b):
        part = pl.ds(pl.multiple_of(b * size, size), size)
        orb_t[:, part] = orb_ref[part, :].T

    def step(g, carry):
        arrived, total = carry
        needed = jnp.maximum(arrived, facts[1, g * UNROLL + UNROLL - 1] + 1)
        lax.fori_loop(arrived, needed, arrive, 0)
        for u in range(TURNS):
            turn(jnp.minimum(g * TURNS + u, nblk - 1))
        for u in range(UNROLL):
            v = facts[0, g * UNROLL + u]
            orbs = orb_ref[pl.ds(pl.multiple_of(((v >> 10) & 31) * size, size), size), :]
            product = jnp.dot(held[v >> 15], orbs, preferred_element_type=F32)
            total = jnp.where((v & 1) == 1, product, total + product)
            slab[(v & 1023) >> 1] = total.astype(BF16)
        return needed, total

    bodies = (live_ref[0] + UNROLL - 1) // UNROLL
    arrived, _ = lax.fori_loop(0, bodies, step, (jnp.int32(came[0]), jnp.zeros((size, occupied), F32)))
    lax.fori_loop(arrived, chunks, arrive, 0)

    @pl.loop(jnp.minimum(bodies * TURNS, nblk), nblk)
    def _(b):
        turn(b)

    small[2].wait()
    metric = metric_ref[...]
    high = metric.astype(BF16)
    naux = metric.shape[0]
    split_ref[0:naux, :] = high
    split_ref[naux : 2 * naux, :] = (metric - high.astype(F32)).astype(BF16)

    @pl.loop(0, q_dev // 2, unroll=8)
    def _(t):
        block = jnp.concatenate(
            [slab[pl.ds((2 * t + u) * nblk, nblk)].reshape(nblk * size, occupied) for u in range(2)], axis=1
        )
        total = jnp.dot(orb_t[...], block, preferred_element_type=F32)
        for u in range(2):
            pair = total[:, u * occupied : (u + 1) * occupied].T
            if owners:
                pairs_ref[:, 2 * t + u] = pair.reshape(owners, occupied // owners, occupied).astype(BF16)
            else:
                pairs_ref[2 * t + u] = pair.astype(BF16)


def half_transform(blocks, index, live, orbitals, metric, q_dev, owners):
    slots, size, _ = blocks.shape
    basis, occupied = orbitals.shape
    nblk = basis // size
    split = (occupied // owners) % 8 == 0
    pairs_shape = (owners, q_dev, occupied // owners, occupied) if split else (q_dev, occupied, occupied)
    wide = -(-(slots + UNROLL) // 128) * 128
    slab, pairs, metric_split = pl.pallas_call(
        functools.partial(half_kernel, owners if split else 0, q_dev),
        out_shape=(
            pltpu.VMEM((q_dev * nblk, size, occupied), BF16),
            jax.ShapeDtypeStruct(pairs_shape, BF16),
            pltpu.VMEM((2 * metric.shape[0], metric.shape[1]), BF16),
        ),
        in_specs=[pl.BlockSpec(memory_space=pltpu.SMEM)] + [pl.BlockSpec(memory_space=pl.ANY)] * 4,
        out_specs=(pl.BlockSpec(memory_space=pltpu.VMEM),) * 3,
        scratch_shapes=[
            pltpu.VMEM(index.shape, jnp.int32),
            pltpu.VMEM((slots + 1, size, size), BF16),
            pltpu.VMEM((basis, occupied), BF16),
            pltpu.VMEM(metric.shape, F32),
            pltpu.VMEM((occupied, basis), BF16),
            pltpu.VMEM((8, wide), F32),
            pltpu.VMEM((8, wide), jnp.int32),
            pltpu.SMEM((8, wide), jnp.int32),
            pltpu.SemaphoreType.DMA((slots // CHUNK,)),
            pltpu.SemaphoreType.DMA((4,)),
        ],
        compiler_params=pltpu.CompilerParams(vmem_limit_bytes=36 * 2**20),
        cost_estimate=pl.CostEstimate(
            flops=2 * slots * size * size * occupied + 2 * q_dev * basis * occupied * occupied,
            bytes_accessed=2 * slots * size * size + 2 * q_dev * basis * occupied,
            transcendentals=0,
        ),
        name="half_transform_pairs",
    )(live, *(pltpu.with_memory_space_constraint(x, pltpu.HBM) for x in (index, blocks, orbitals, metric)))
    if not split:
        pairs = pairs.reshape(q_dev, owners, occupied // owners, occupied).transpose(1, 0, 2, 3)
    return slab.reshape(q_dev, basis, occupied), pairs, metric_split


def metric_kernel(split_ref, held_ref, out_ref, spread, mixed):
    naux, each, occupied = held_ref.shape
    spread[...] = held_ref[...].astype(F32).reshape(naux * each, occupied)
    for r in range(0, each, 2):
        both = [spread[pl.ds(r + u, naux, stride=each), :].astype(BF16) for u in range(2)]
        parts = jnp.dot(split_ref[...], jnp.concatenate(both, axis=1), preferred_element_type=F32)
        fitted = parts[:naux] + parts[naux:]
        for u in range(2):
            mixed[pl.ds(r + u, naux, stride=each), :] = fitted[:, u * occupied : (u + 1) * occupied]
    out_ref[...] = mixed[...].reshape(naux, each, occupied).astype(BF16)


def apply_metric(metric, metric_split, held):
    naux, each, occupied = held.shape
    if each % 8:
        fitted = jnp.einsum("qp,pij->qij", metric, held.astype(F32), precision=lax.Precision.HIGHEST)
        return fitted.astype(BF16)
    return pl.pallas_call(
        metric_kernel,
        out_shape=jax.ShapeDtypeStruct(held.shape, BF16),
        in_specs=[pl.BlockSpec(memory_space=pltpu.VMEM)] * 2,
        out_specs=pl.BlockSpec(memory_space=pltpu.VMEM),
        scratch_shapes=[pltpu.VMEM((naux * each, occupied), F32)] * 2,
        compiler_params=pltpu.CompilerParams(vmem_limit_bytes=12 * 2**20),
        cost_estimate=pl.CostEstimate(
            flops=4 * naux * naux * each * occupied, bytes_accessed=4 * naux * each * occupied, transcendentals=0
        ),
        name="apply_metric",
    )(pltpu.with_memory_space_constraint(metric_split, pltpu.VMEM), held)


def gather_fitted(fitted_ref, fitted):
    q_dev = fitted.shape[0] // fitted.shape[1]
    occupied = fitted.shape[1]
    for q in range(q_dev):
        if len(fitted_ref.shape) == 4:
            block = fitted_ref[:, q].astype(F32).reshape(occupied, occupied).astype(BF16)
        else:
            block = fitted_ref[q]
        fitted[q * occupied : (q + 1) * occupied, :] = block


def exchange_kernel(blocks, gather, more, slab, fitted_ref, *refs):
    refs = list(refs)
    more_ref = refs.pop(0) if more else None
    out_refs = [refs.pop(0) for _ in blocks]
    if gather:
        fitted = refs.pop(0)
        gather_fitted(fitted_ref, fitted)
    else:
        fitted = fitted_ref
    q_dev = slab.shape[0]
    each = out_refs[0].shape[1]
    me = lax.axis_index("aux").astype(jnp.int32)
    todo = [(k, c, h) for c, part in enumerate(blocks) for h, k in enumerate(part)]
    together = next(n for n in (4, 3, 2, 1) if len(todo) % n == 0)
    for g in range(0, len(todo), together):
        rows = [pl.ds(pl.multiple_of((me ^ k) * each, each), each) for k, _, _ in todo[g : g + together]]
        every = jnp.concatenate(
            [jnp.concatenate([slab[q, r, :] for r in rows], axis=0) for q in range(q_dev)], axis=1
        )
        sums = jnp.dot(every, fitted[...], preferred_element_type=F32)
        for u, (_, c, h) in enumerate(todo[g : g + together]):
            part = sums[u * each : (u + 1) * each]
            if more:
                part = part + more_ref[g + u].astype(F32)
            out_refs[c][h] = part.astype(out_refs[c].dtype)


def exchange_rows(slab, fitted, owners, blocks, dtype, gather=False, more=None):
    q_dev, basis, occupied = slab.shape
    each = basis // owners
    count = sum(len(part) for part in blocks)
    out = [jax.ShapeDtypeStruct((len(part), each, occupied), dtype) for part in blocks]
    if gather:
        out.append(jax.ShapeDtypeStruct((q_dev * occupied, occupied), BF16))
    operands = [pltpu.with_memory_space_constraint(slab, pltpu.VMEM), fitted] + ([] if more is None else [more])
    return pl.pallas_call(
        functools.partial(exchange_kernel, blocks, gather, more is not None),
        out_shape=out,
        in_specs=[pl.BlockSpec(memory_space=pltpu.VMEM)] * len(operands),
        out_specs=[pl.BlockSpec(memory_space=pltpu.VMEM)] * len(out),
        compiler_params=pltpu.CompilerParams(vmem_limit_bytes=24 * 2**20),
        cost_estimate=pl.CostEstimate(
            flops=2 * q_dev * occupied * count * each * occupied,
            bytes_accessed=2 * q_dev * occupied * count * each,
            transcendentals=0,
        ),
        name="exchange_rows",
    )(*operands)


def body(owners, integrals, block_index, live_count, orbitals, metric):
    basis, occupied = orbitals.shape
    naux = metric.shape[1]
    q_dev = naux // owners

    slab, pairs, metric_split = half_transform(integrals, block_index.T, live_count, orbitals, metric, q_dev, owners)

    trade = functools.partial(lax.all_to_all, axis_name="aux", split_axis=0, concat_axis=0, tiled=True)
    held = trade(pairs).reshape(naux, occupied // owners, occupied)
    fitted = apply_metric(metric, metric_split, held)
    fitted = trade(fitted.reshape(owners, q_dev, occupied // owners, occupied))
    if (occupied // owners) % 8:
        fitted = fitted.transpose(1, 0, 2, 3).reshape(q_dev, occupied, occupied)

    def swap(x, bits):
        return lax.ppermute(x, "aux", [(d, d ^ bits) for d in range(owners)])

    far = range(0, owners, 8)
    leave = [tuple(x + k for k in far) for x in (2, 4, 6)]
    stay = [tuple(far)]
    flip = lambda parts: [tuple(k ^ 1 for k in part) for part in parts]
    *away, fitted = exchange_rows(slab, fitted, owners, flip([sum(leave, ())]), BF16, gather=True)
    from_core = swap(away[0], 1)
    away = exchange_rows(slab, fitted, owners, flip(stay), BF16)
    to_stay = swap(away[0], 1)
    away = exchange_rows(slab, fitted, owners, leave, BF16, more=from_core)
    arrived = [swap(x, bits) for x, bits in zip(away, (2, 4, 6))]
    (near,) = exchange_rows(slab, fitted, owners, stay, F32, more=to_stay)
    for x in arrived:
        near = near + x.astype(F32)
    total = near[0]
    for c, k in enumerate(far):
        if k:
            total = total + swap(near[c].astype(BF16), k).astype(F32)
    return total


def solution(mesh):
    placed = (
        P(("groups", "aux"), None, None),
        P(("groups", "aux"), None),
        P(("groups", "aux")),
        P("groups", None),
        P("groups", None),
    )
    return jax.shard_map(
        functools.partial(body, mesh.shape["aux"]),
        mesh=mesh, in_specs=placed, out_specs=P(("groups", "aux"), None), check_vma=False,
    )
```

```python
import functools

import jax
import jax.numpy as jnp
from jax import lax
from jax.experimental import pallas as pl
from jax.experimental.pallas import tpu as pltpu
from jax.sharding import PartitionSpec as P

UNROLL = 64
CHUNK = 32
TURNS = 5
FLIGHT = 3
F32 = jnp.float32
BF16 = jnp.bfloat16


def rank_slots(live, index_ref, rows, meta, nblk, nkeys, chunks, pump):
    slots = index_ref.shape[1]
    wide = rows.shape[1]
    never = float(chunks * nkeys)
    assert slots < 512 and nblk <= 32 and nkeys <= 512 and CHUNK % 8 == 0
    rows[...] = jnp.full(rows.shape, nkeys, F32)
    key = index_ref[0:1, :] * nblk + index_ref[1:2, :]
    slot = lax.broadcasted_iota(jnp.int32, (1, slots), 1)
    rows[0:1, 0:slots] = jnp.where(slot < live, key, nkeys).astype(F32)
    rows[1:2, 0:slots] = (slot * 32768 + index_ref[2:3, :] * 1024).astype(F32)
    row = rows[0:1, :]
    lives = row < nkeys
    tile = (8, wide)
    zero = jnp.zeros(tile, F32)
    lane = lax.broadcasted_iota(jnp.int32, tile, 1)
    ahead = lane - lax.broadcasted_iota(jnp.int32, tile, 0)

    every = jnp.broadcast_to(row, tile)
    columns = rows[...].T
    late = zero
    for s in range(0, slots, 8):
        late = jnp.where(columns[s : s + 8, 0:1] == every, float(s // CHUNK), late)
    late = jnp.max(late, axis=0, keepdims=True)
    pump()
    order = jnp.where(lives, late * nkeys + row, never)

    every = jnp.broadcast_to(order, tile)
    columns = every.T
    rank, place = zero, zero
    for s in range(0, slots, 8):
        column = columns[s : s + 8, 0:1]
        same = (column == every) & (ahead > s)
        rank = rank + jnp.where(same, 1.0, 0.0)
        place = place + jnp.where(same | (column < every), 1.0, 0.0)
    pump()
    rank = jnp.sum(rank, axis=0, keepdims=True)
    place = jnp.sum(place, axis=0, keepdims=True)
    end = jnp.max(jnp.where(lives, order, 0.0), axis=1, keepdims=True)
    last = jnp.max(jnp.where(lives & (order == end), row, 0.0), axis=1, keepdims=True)
    nothing = 2.0 * last + slots * 32768.0
    rows[1:2, :] = rows[1:2, :] + 2.0 * row + jnp.where(rank == 0.0, 1.0, 0.0) - nothing
    rows[2:3, :] = jnp.where(lives, place, -1.0)
    rows[3:4, :] = late - (chunks - 1)

    columns = rows[...].T
    spot = lane.astype(F32)
    number, need = zero, zero
    for s in range(0, slots, 8):
        found = columns[s : s + 8, 2:3] == spot
        number = number + jnp.where(found, columns[s : s + 8, 1:2], 0.0)
        need = need + jnp.where(found, columns[s : s + 8, 3:4], 0.0)
    meta[0:1, :] = (jnp.sum(number, axis=0, keepdims=True) + nothing).astype(jnp.int32)
    meta[1:2, :] = (jnp.sum(need, axis=0, keepdims=True) + (chunks - 1)).astype(jnp.int32)


def half_kernel(
    owners, q_dev, live_ref, index_hbm, blocks_hbm, orb_hbm, metric_hbm, slab, pairs_ref, split_ref,
    index_ref, held, orb_ref, metric_ref, orb_t, rows, meta, facts, in_sem, small_sem,
):
    slots, size, _ = blocks_hbm.shape
    occupied = orb_ref.shape[1]
    nblk = orb_ref.shape[0] // size
    nkeys = q_dev * nblk
    chunks = slots // CHUNK

    def fetch(c):
        part = pl.ds(c * CHUNK, CHUNK)
        return pltpu.make_async_copy(blocks_hbm.at[part], held.at[part], in_sem.at[c])

    def clear(first, last):
        @pl.loop(first, last, step=8)
        def _(k):
            for u in range(8):
                slab[k + u] = jnp.zeros((size, occupied), BF16)

    small = [
        pltpu.make_async_copy(source, target, small_sem.at[1 + k])
        for k, (source, target) in enumerate(
            [(index_hbm, index_ref), (orb_hbm, orb_ref), (metric_hbm, metric_ref)]
        )
    ]
    small[0].start()
    small[1].start()
    for c in range(min(FLIGHT, chunks)):
        fetch(c).start()
    came = [0]

    def pump():
        if came[0] + FLIGHT < chunks:
            fetch(came[0]).wait()
            fetch(came[0] + FLIGHT).start()
            came[0] += 1


    held[slots] = jnp.zeros((size, size), BF16)
    clear(0, nkeys // 2)

    small[0].wait()
    pump()
    rank_slots(live_ref[0], index_ref, rows, meta, nblk, nkeys, chunks, pump)
    pump()
    copy = pltpu.make_async_copy(meta, facts, small_sem.at[0])
    copy.start()

    clear(nkeys // 2, 3 * nkeys // 4)
    pump()
    clear(3 * nkeys // 4, nkeys)
    while came[0] + FLIGHT < chunks:
        pump()
    small[2].start()
    small[1].wait()
    copy.wait()

    def arrive(c, nothing):
        fetch(c).wait()
        return nothing

    def turn(b):
        part = pl.ds(pl.multiple_of(b * size, size), size)
        orb_t[:, part] = orb_ref[part, :].T

    def step(g, carry):
        arrived, total = carry
        needed = jnp.maximum(arrived, facts[1, g * UNROLL + UNROLL - 1] + 1)
        lax.fori_loop(arrived, needed, arrive, 0)
        for u in range(TURNS):
            turn(jnp.minimum(g * TURNS + u, nblk - 1))
        empty = jnp.zeros((size, occupied), BF16)
        for u in range(0, UNROLL, 2):
            pair = [facts[0, g * UNROLL + u + w] for w in range(2)]
            orbs = [orb_ref[pl.ds(pl.multiple_of(((v >> 10) & 31) * size, size), size), :] for v in pair]
            diagonal = jnp.concatenate(
                [jnp.concatenate([orbs[0], empty], axis=1), jnp.concatenate([empty, orbs[1]], axis=1)], axis=0
            )
            blocks = jnp.concatenate([held[v >> 15] for v in pair], axis=1)
            products = jnp.dot(blocks, diagonal, preferred_element_type=F32)
            for w, v in enumerate(pair):
                product = products[:, w * occupied : (w + 1) * occupied]
                total = jnp.where((v & 1) == 1, product, total + product)
                slab[(v & 1023) >> 1] = total.astype(BF16)
        return needed, total

    bodies = (live_ref[0] + UNROLL - 1) // UNROLL
    arrived, _ = lax.fori_loop(0, bodies, step, (jnp.int32(came[0]), jnp.zeros((size, occupied), F32)))
    lax.fori_loop(arrived, chunks, arrive, 0)

    @pl.loop(jnp.minimum(bodies * TURNS, nblk), nblk)
    def _(b):
        turn(b)

    small[2].wait()
    metric = metric_ref[...]
    high = metric.astype(BF16)
    naux = metric.shape[0]
    split_ref[0:naux, :] = high
    split_ref[naux : 2 * naux, :] = (metric - high.astype(F32)).astype(BF16)

    @pl.loop(0, q_dev // 2, unroll=8)
    def _(t):
        block = jnp.concatenate(
            [slab[pl.ds((2 * t + u) * nblk, nblk)].reshape(nblk * size, occupied) for u in range(2)], axis=1
        )
        total = jnp.dot(orb_t[...], block, preferred_element_type=F32)
        for u in range(2):
            pair = total[:, u * occupied : (u + 1) * occupied].T
            if owners:
                pairs_ref[:, 2 * t + u] = pair.reshape(owners, occupied // owners, occupied).astype(BF16)
            else:
                pairs_ref[2 * t + u] = pair.astype(BF16)


def half_transform(blocks, index, live, orbitals, metric, q_dev, owners):
    slots, size, _ = blocks.shape
    basis, occupied = orbitals.shape
    nblk = basis // size
    split = (occupied // owners) % 8 == 0
    pairs_shape = (owners, q_dev, occupied // owners, occupied) if split else (q_dev, occupied, occupied)
    wide = -(-(slots + UNROLL) // 128) * 128
    slab, pairs, metric_split = pl.pallas_call(
        functools.partial(half_kernel, owners if split else 0, q_dev),
        out_shape=(
            pltpu.VMEM((q_dev * nblk, size, occupied), BF16),
            jax.ShapeDtypeStruct(pairs_shape, BF16),
            pltpu.VMEM((2 * metric.shape[0], metric.shape[1]), BF16),
        ),
        in_specs=[pl.BlockSpec(memory_space=pltpu.SMEM)] + [pl.BlockSpec(memory_space=pl.ANY)] * 4,
        out_specs=(pl.BlockSpec(memory_space=pltpu.VMEM),) * 3,
        scratch_shapes=[
            pltpu.VMEM(index.shape, jnp.int32),
            pltpu.VMEM((slots + 1, size, size), BF16),
            pltpu.VMEM((basis, occupied), BF16),
            pltpu.VMEM(metric.shape, F32),
            pltpu.VMEM((occupied, basis), BF16),
            pltpu.VMEM((8, wide), F32),
            pltpu.VMEM((8, wide), jnp.int32),
            pltpu.SMEM((8, wide), jnp.int32),
            pltpu.SemaphoreType.DMA((slots // CHUNK,)),
            pltpu.SemaphoreType.DMA((4,)),
        ],
        compiler_params=pltpu.CompilerParams(vmem_limit_bytes=36 * 2**20),
        cost_estimate=pl.CostEstimate(
            flops=2 * slots * size * size * occupied + 2 * q_dev * basis * occupied * occupied,
            bytes_accessed=2 * slots * size * size + 2 * q_dev * basis * occupied,
            transcendentals=0,
        ),
        name="half_transform_pairs",
    )(live, *(pltpu.with_memory_space_constraint(x, pltpu.HBM) for x in (index, blocks, orbitals, metric)))
    if not split:
        pairs = pairs.reshape(q_dev, owners, occupied // owners, occupied).transpose(1, 0, 2, 3)
    return slab.reshape(q_dev, basis, occupied), pairs, metric_split


def metric_kernel(split_ref, held_ref, out_ref, spread, mixed):
    naux, each, occupied = held_ref.shape
    spread[...] = held_ref[...].astype(F32).reshape(naux * each, occupied)
    for r in range(0, each, 2):
        both = [spread[pl.ds(r + u, naux, stride=each), :].astype(BF16) for u in range(2)]
        parts = jnp.dot(split_ref[...], jnp.concatenate(both, axis=1), preferred_element_type=F32)
        fitted = parts[:naux] + parts[naux:]
        for u in range(2):
            mixed[pl.ds(r + u, naux, stride=each), :] = fitted[:, u * occupied : (u + 1) * occupied]
    out_ref[...] = mixed[...].reshape(naux, each, occupied).astype(BF16)


def apply_metric(metric, metric_split, held):
    naux, each, occupied = held.shape
    if each % 8:
        fitted = jnp.einsum("qp,pij->qij", metric, held.astype(F32), precision=lax.Precision.HIGHEST)
        return fitted.astype(BF16)
    return pl.pallas_call(
        metric_kernel,
        out_shape=jax.ShapeDtypeStruct(held.shape, BF16),
        in_specs=[pl.BlockSpec(memory_space=pltpu.VMEM)] * 2,
        out_specs=pl.BlockSpec(memory_space=pltpu.VMEM),
        scratch_shapes=[pltpu.VMEM((naux * each, occupied), F32)] * 2,
        compiler_params=pltpu.CompilerParams(vmem_limit_bytes=12 * 2**20),
        cost_estimate=pl.CostEstimate(
            flops=4 * naux * naux * each * occupied, bytes_accessed=4 * naux * each * occupied, transcendentals=0
        ),
        name="apply_metric",
    )(pltpu.with_memory_space_constraint(metric_split, pltpu.VMEM), held)


def gather_fitted(fitted_ref, fitted):
    q_dev = fitted.shape[0] // fitted.shape[1]
    occupied = fitted.shape[1]
    for q in range(q_dev):
        if len(fitted_ref.shape) == 4:
            block = fitted_ref[:, q].astype(F32).reshape(occupied, occupied).astype(BF16)
        else:
            block = fitted_ref[q]
        fitted[q * occupied : (q + 1) * occupied, :] = block


def exchange_kernel(blocks, gather, more, slab, fitted_ref, *refs):
    refs = list(refs)
    more_ref = refs.pop(0) if more else None
    out_refs = [refs.pop(0) for _ in blocks]
    if gather:
        fitted = refs.pop(0)
        gather_fitted(fitted_ref, fitted)
    else:
        fitted = fitted_ref
    q_dev = slab.shape[0]
    each = out_refs[0].shape[1]
    me = lax.axis_index("aux").astype(jnp.int32)
    todo = [(k, c, h) for c, part in enumerate(blocks) for h, k in enumerate(part)]
    together = next(n for n in (4, 3, 2, 1) if len(todo) % n == 0)
    for g in range(0, len(todo), together):
        rows = [pl.ds(pl.multiple_of((me ^ k) * each, each), each) for k, _, _ in todo[g : g + together]]
        every = jnp.concatenate(
            [jnp.concatenate([slab[q, r, :] for r in rows], axis=0) for q in range(q_dev)], axis=1
        )
        sums = jnp.dot(every, fitted[...], preferred_element_type=F32)
        for u, (_, c, h) in enumerate(todo[g : g + together]):
            part = sums[u * each : (u + 1) * each]
            if more:
                part = part + more_ref[g + u].astype(F32)
            out_refs[c][h] = part.astype(out_refs[c].dtype)


def exchange_rows(slab, fitted, owners, blocks, dtype, gather=False, more=None):
    q_dev, basis, occupied = slab.shape
    each = basis // owners
    count = sum(len(part) for part in blocks)
    out = [jax.ShapeDtypeStruct((len(part), each, occupied), dtype) for part in blocks]
    if gather:
        out.append(jax.ShapeDtypeStruct((q_dev * occupied, occupied), BF16))
    operands = [pltpu.with_memory_space_constraint(slab, pltpu.VMEM), fitted] + ([] if more is None else [more])
    return pl.pallas_call(
        functools.partial(exchange_kernel, blocks, gather, more is not None),
        out_shape=out,
        in_specs=[pl.BlockSpec(memory_space=pltpu.VMEM)] * len(operands),
        out_specs=[pl.BlockSpec(memory_space=pltpu.VMEM)] * len(out),
        compiler_params=pltpu.CompilerParams(vmem_limit_bytes=24 * 2**20),
        cost_estimate=pl.CostEstimate(
            flops=2 * q_dev * occupied * count * each * occupied,
            bytes_accessed=2 * q_dev * occupied * count * each,
            transcendentals=0,
        ),
        name="exchange_rows",
    )(*operands)


def body(owners, integrals, block_index, live_count, orbitals, metric):
    basis, occupied = orbitals.shape
    naux = metric.shape[1]
    q_dev = naux // owners

    slab, pairs, metric_split = half_transform(integrals, block_index.T, live_count, orbitals, metric, q_dev, owners)

    trade = functools.partial(lax.all_to_all, axis_name="aux", split_axis=0, concat_axis=0, tiled=True)
    held = trade(pairs).reshape(naux, occupied // owners, occupied)
    fitted = apply_metric(metric, metric_split, held)
    fitted = trade(fitted.reshape(owners, q_dev, occupied // owners, occupied))
    if (occupied // owners) % 8:
        fitted = fitted.transpose(1, 0, 2, 3).reshape(q_dev, occupied, occupied)

    def swap(x, bits):
        return lax.ppermute(x, "aux", [(d, d ^ bits) for d in range(owners)])

    far = range(0, owners, 8)
    leave = [tuple(x + k for k in far) for x in (2, 4, 6)]
    stay = [tuple(far)]
    flip = lambda parts: [tuple(k ^ 1 for k in part) for part in parts]
    *away, fitted = exchange_rows(slab, fitted, owners, flip([sum(leave, ())]), BF16, gather=True)
    from_core = swap(away[0], 1)
    away = exchange_rows(slab, fitted, owners, flip(stay), BF16)
    to_stay = swap(away[0], 1)
    away = exchange_rows(slab, fitted, owners, leave, BF16, more=from_core)
    arrived = [swap(x, bits) for x, bits in zip(away, (2, 4, 6))]
    (near,) = exchange_rows(slab, fitted, owners, stay, F32, more=to_stay)
    for x in arrived:
        near = near + x.astype(F32)
    total = near[0]
    for c, k in enumerate(far):
        if k:
            total = total + swap(near[c].astype(BF16), k).astype(F32)
    return total


def solution(mesh):
    placed = (
        P(("groups", "aux"), None, None),
        P(("groups", "aux"), None),
        P(("groups", "aux")),
        P("groups", None),
        P("groups", None),
    )
    return jax.shard_map(
        functools.partial(body, mesh.shape["aux"]),
        mesh=mesh, in_specs=placed, out_specs=P(("groups", "aux"), None), check_vma=False,
    )
```
